32 devices in a mesh: section: 4 (over y, x), dp: 8 (over z, core).
Axes of the slice: x: 2, y: 2, z: 4, core: 2. Of those that a mesh axis runs over, the one named last changes fastest.
Arguments:
- tokens: bfloat16 [8064, 512], P('dp'), may hold values from -6 to 6
- lengths: int32 [16, 4], P('dp'), may hold values from 1 to 158, as said below
- cotangent: bfloat16 [8064, 512], P('dp'), may hold values from -6 to 6
- full_first_gain: bfloat16 [512], P('section'), may hold values from 0.5 to 1.5
- full_project: bfloat16 [512, 1536], P(None, 'section'), may hold values from -0.25 to 0.25
- full_merge: bfloat16 [512, 512], P(None, 'section'), may hold values from -0.75 to 0.75
- full_second_gain: bfloat16 [512], P('section'), may hold values from 0.5 to 1.5
- full_widen: bfloat16 [512, 2048], P(None, 'section'), may hold values from -0.25 to 0.25
- full_narrow: bfloat16 [2048, 512], P(None, 'section'), may hold values from -0.125 to 0.125
- pool_weight: bfloat16 [1536, 512], P(None, 'section'), may hold values from -0.15625 to 0.15625
- short_first_gain: bfloat16 [512], P('section'), may hold values from 0.5 to 1.5
- short_project: bfloat16 [512, 1536], P(None, 'section'), may hold values from -0.25 to 0.25
- short_merge: bfloat16 [512, 512], P(None, 'section'), may hold values from -0.75 to 0.75
- short_second_gain: bfloat16 [512], P('section'), may hold values from 0.5 to 1.5
- short_widen: bfloat16 [512, 2048], P(None, 'section'), may hold values from -0.25 to 0.25
- short_narrow: bfloat16 [2048, 512], P(None, 'section'), may hold values from -0.125 to 0.125
- expand_weight: bfloat16 [512, 1536], P(None, 'section'), may hold values from -0.25 to 0.25
Outputs:
- mixed_out: bfloat16 [8064, 512], P('dp', 'section')
- token_gradient: bfloat16 [8064, 512], P('dp', 'section')
- full_first_gain_gradient: float32 [512], P('section')
- full_project_gradient: float32 [512, 1536], P(None, 'section')
- full_merge_gradient: float32 [512, 512], P(None, 'section')
- full_second_gain_gradient: float32 [512], P('section')
- full_widen_gradient: float32 [512, 2048], P(None, 'section')
- full_narrow_gradient: float32 [2048, 512], P(None, 'section')
- pool_weight_gradient: float32 [1536, 512], P(None, 'section')
- short_first_gain_gradient: float32 [512], P('section')
- short_project_gradient: float32 [512, 1536], P(None, 'section')
- short_merge_gradient: float32 [512, 512], P(None, 'section')
- short_second_gain_gradient: float32 [512], P('section')
- short_widen_gradient: float32 [512, 2048], P(None, 'section')
- short_narrow_gradient: float32 [2048, 512], P(None, 'section')
- expand_weight_gradient: float32 [512, 1536], P(None, 'section')
The draws below stay inside these ranges and needn't reach their ends.
Inputs may be any that keep to these rules, and one draw needn't show every extreme that they name: `lengths`: per row, in groups of three tokens: three sequences in a drawn order, one of exactly 158 groups and two of 1 to 4 groups, then the row's padding of the remaining groups (2 or more); each row adds up to 168.
All inputs are finite; a program needn't handle non-finite values.
Results may differ from the reference program's by a relative error of at most 0.025.
Values may be sent and summed in bfloat16 or wider, within the bound.
No kernel may reach another device: no remote copies, remote signals or barrier semaphores. Data moves between devices by JAX's collectives and lax.ppermute only.
A program may use at most 384 MiB of HBM per device.

```python
import jax
import jax.numpy as jnp
from jax import lax

D = 512
HEADS = 8
FF = 2048
ROW_GROUPS = 168
SPARE = 10
SEGS = 4
ROW = 504
ROWS = 16
TOKENS = 8064


def draw_lengths(key, part):
    key = jax.random.fold_in(key, 7)
    first_key, second_key, third_key = jax.random.split(key, 3)
    widest = (SPARE - 2) // 2
    first = jax.random.randint(first_key, (ROWS,), 1, widest + 1)
    second = jax.random.randint(second_key, (ROWS,), 1, widest + 1)
    where_long = jax.random.randint(third_key, (ROWS,), 0, 3)
    longest = ROW_GROUPS - SPARE
    slot_zero = jnp.where(where_long == 0, longest, first)
    slot_one = jnp.where(where_long == 1, longest, jnp.where(where_long == 0, first, second))
    slot_two = jnp.where(where_long == 2, longest, second)
    padding = SPARE - first - second
    return jnp.stack([slot_zero, slot_one, slot_two, padding], 1).astype(jnp.int32)


def level_of(own_key, shape, cuts, smallest, top_value):
    factor_of, own = 1.0, jax.random.fold_in(own_key, 6)
    for dim, shards_of in cuts:
        steps = jnp.exp(jax.random.uniform(jax.random.fold_in(own, dim), (shards_of,), jnp.float32, smallest / len(cuts), top_value / len(cuts)))
        factor_of = factor_of * jnp.repeat(steps, shape[dim] // shards_of).reshape([-1 if axis == dim else 1 for axis in range(len(shape))])
    return factor_of


def gaussian(own_key, dims, spread, bound, pieces=(), held_as=jnp.bfloat16):
    entries = spread * jax.random.normal(own_key, dims, jnp.float32)
    if pieces:
        entries = entries * level_of(own_key, dims, pieces, -0.22, 0.18)
    return jnp.clip(entries, -bound, bound).astype(held_as)


def setup_inputs(seed: int = 0) -> dict:
    streams_of = jax.random.split(jax.random.key(seed), 18)
    tokens = gaussian(streams_of[0], (TOKENS, D), 1.0, 6.0, ((0, 8),))
    lengths = draw_lengths(jax.random.fold_in(streams_of[17], 71), 0)
    cotangent = gaussian(streams_of[2], (TOKENS, D), 1.0, 6.0, ((0, 8),))
    full_first_gain = jnp.clip(1.0 + 0.1 * jax.random.normal(streams_of[3], (D,), jnp.float32), 0.5, 1.5).astype(jnp.bfloat16)
    full_project = gaussian(streams_of[4], (D, 3 * D), D ** -0.5, 0.25, ((1, 4),))
    full_merge = gaussian(streams_of[5], (D, D), (D // 8) ** -0.5, 0.75, ((1, 4),))
    full_second_gain = jnp.clip(1.0 + 0.1 * jax.random.normal(streams_of[6], (D,), jnp.float32), 0.5, 1.5).astype(jnp.bfloat16)
    full_widen = gaussian(streams_of[7], (D, FF), D ** -0.5, 0.25, ((1, 4),))
    full_narrow = gaussian(streams_of[8], (FF, D), FF ** -0.5, 0.125, ((1, 4),))
    pool_weight = gaussian(streams_of[9], (3 * D, D), (3 * D) ** -0.5, 0.15625, ((1, 4),))
    short_first_gain = jnp.clip(1.0 + 0.1 * jax.random.normal(streams_of[10], (D,), jnp.float32), 0.5, 1.5).astype(jnp.bfloat16)
    short_project = gaussian(streams_of[11], (D, 3 * D), D ** -0.5, 0.25, ((1, 4),))
    short_merge = gaussian(streams_of[12], (D, D), (D // 8) ** -0.5, 0.75, ((1, 4),))
    short_second_gain = jnp.clip(1.0 + 0.1 * jax.random.normal(streams_of[13], (D,), jnp.float32), 0.5, 1.5).astype(jnp.bfloat16)
    short_widen = gaussian(streams_of[14], (D, FF), D ** -0.5, 0.25, ((1, 4),))
    short_narrow = gaussian(streams_of[15], (FF, D), FF ** -0.5, 0.125, ((1, 4),))
    expand_weight = gaussian(streams_of[16], (D, 3 * D), D ** -0.5, 0.25, ((1, 4),))
    return {"tokens": tokens, "lengths": lengths, "cotangent": cotangent, "full_first_gain": full_first_gain, "full_project": full_project, "full_merge": full_merge, "full_second_gain": full_second_gain, "full_widen": full_widen, "full_narrow": full_narrow, "pool_weight": pool_weight, "short_first_gain": short_first_gain, "short_project": short_project, "short_merge": short_merge, "short_second_gain": short_second_gain, "short_widen": short_widen, "short_narrow": short_narrow, "expand_weight": expand_weight}


EPS = 1e-05
NEG = -1e+30
HIGHEST_PRECISION = lax.Precision.HIGHEST

@jax.custom_vjp
def low(v):
    return lax.optimization_barrier(v.astype(jnp.bfloat16)).astype(jnp.float32)

@jax.custom_vjp
def low_back(v):
    return v

def low_keep(v):
    return (low(v), None)

def low_pass(kept, grad):
    return (grad,)

def back_keep(v):
    return (v, None)

def back_low(kept, grad):
    return (low(grad),)
low.defvjp(low_keep, low_pass)
low_back.defvjp(back_keep, back_low)

def layout(counts, groups):
    ends = jnp.cumsum(counts).astype(jnp.int32)
    starts = (ends - counts).astype(jnp.int32)
    index = jnp.arange(groups, dtype=jnp.int32)
    segment_group = lax.optimization_barrier(jnp.sum((index[:, None] >= ends[None, :]).astype(jnp.int32), axis=1)).astype(jnp.int32)
    member = segment_group[:, None] == jnp.arange(counts.shape[0], dtype=jnp.int32)[None, :]
    begin = lax.optimization_barrier(jnp.sum(jnp.where(member, starts[None, :], 0), axis=1)).astype(jnp.int32)
    place_group = (index - begin).astype(jnp.int32)
    segment_token = jnp.repeat(segment_group, 3)
    place_token = (3 * jnp.repeat(place_group, 3) + jnp.tile(jnp.arange(3, dtype=jnp.int32), groups)).astype(jnp.int32)
    return (segment_token, place_token, segment_group, place_group)

def turn(values):
    half = values.shape[-1] // 2
    return jnp.concatenate([-values[..., half:], values[..., :half]], -1)

def angles(places, size):
    half = size // 2
    freq = 10000.0 ** (-2.0 * jnp.arange(half, dtype=jnp.float32) / size)
    phase = places.astype(jnp.float32)[:, None] * freq[None, :]
    cosine = jnp.concatenate([jnp.cos(phase), jnp.cos(phase)], -1)[:, None, :]
    sine = jnp.concatenate([jnp.sin(phase), jnp.sin(phase)], -1)[:, None, :]
    return (cosine, sine)

def rotary(values, cosine, sine):
    return values * cosine + turn(values) * sine

def layer_norm(states, gain):
    center = states - lax.optimization_barrier(jnp.mean(states, -1, keepdims=True))
    return center * lax.rsqrt(lax.optimization_barrier(jnp.mean(center * center, -1, keepdims=True)) + EPS) * gain

def matmul(left, right):
    return jnp.dot(left, right, precision=HIGHEST_PRECISION, preferred_element_type=jnp.float32)

def block(states, params, segment, places):
    first_gain, project, merge, second_gain, widen, narrow = params
    count, width = states.shape
    size = width // HEADS
    first = low(layer_norm(states, first_gain))
    packed = low_back(matmul(first, project))
    cosine, sine = angles(places, size)
    queries = low(rotary(packed[:, :width].reshape(count, HEADS, size), cosine, sine))
    keys = low(rotary(packed[:, width:2 * width].reshape(count, HEADS, size), cosine, sine))
    values = low(packed[:, 2 * width:].reshape(count, HEADS, size))
    raw = jnp.einsum('qhd,khd->hqk', queries, keys, precision=HIGHEST_PRECISION)
    scores = low_back(raw) * size ** (-0.5)
    order = jnp.arange(count)
    allowed = (segment[:, None] == segment[None, :]) & (order[:, None] >= order[None, :])
    scores = jnp.where(allowed[None], scores, NEG)
    top = lax.optimization_barrier(jnp.max(scores, -1, keepdims=True))
    powered = jnp.exp(scores - top)
    attend = low(powered / lax.optimization_barrier(jnp.sum(powered, -1, keepdims=True)))
    context = jnp.einsum('hqk,khd->qhd', attend, values, precision=HIGHEST_PRECISION).reshape(count, width)
    context = low(low_back(context))
    middle = states + low_back(matmul(context, merge))
    second = low(layer_norm(middle, second_gain))
    inner = low_back(matmul(second, widen))
    hidden = low(jax.nn.gelu(inner, approximate=False))
    return middle + low_back(matmul(hidden, narrow))

def forward_row(row_tokens, weights, layout_data):
    segment_token, place_token, segment_group, place_group = layout_data
    count, width = row_tokens.shape
    groups = count // 3
    full = low(block(row_tokens, weights[0:6], segment_token, place_token))
    grouped = low_back(full).reshape(groups, 3 * width)
    keep = (place_group > 0)[:, None]
    before = jnp.concatenate([jnp.zeros((1, 2 * width), jnp.float32), grouped[:-1, width:]], 0)
    before = jnp.where(keep, before, 0.0)
    joined = jnp.concatenate([before, grouped[:, :width]], 1)
    short_in = low(low_back(matmul(joined, weights[6])))
    short_out = low(low_back(block(short_in, weights[7:13], segment_group, place_group)))
    return full + matmul(short_out, weights[13]).reshape(count, width)

def reference(tokens, lengths, cotangent, full_first_gain, full_project, full_merge, full_second_gain, full_widen, full_narrow, pool_weight, short_first_gain, short_project, short_merge, short_second_gain, short_widen, short_narrow, expand_weight):
    weights = tuple((item.astype(jnp.float32) for item in (full_first_gain, full_project, full_merge, full_second_gain, full_widen, full_narrow, pool_weight, short_first_gain, short_project, short_merge, short_second_gain, short_widen, short_narrow, expand_weight)))
    rows_in = tokens.astype(jnp.float32).reshape(ROWS, ROW, D)
    targets = cotangent.astype(jnp.float32).reshape(ROWS, ROW, D)

    def one_row(totals, item):
        row_tokens, row_target, counts = item
        layout_data = layout(counts, ROW // 3)
        live = (layout_data[0] < SEGS - 1)[:, None]
        result, pull = jax.vjp(lambda row_in, params: forward_row(row_in, params, layout_data), row_tokens, weights)
        row_gradient, weight_terms = pull(jnp.where(live, row_target, 0.0))
        totals = tuple((first + second for first, second in zip(totals, weight_terms)))
        return (totals, (result.astype(jnp.bfloat16), row_gradient.astype(jnp.bfloat16)))
    start = tuple((jnp.zeros_like(item) for item in weights))
    totals, (results, gradients) = lax.scan(one_row, start, (rows_in, targets, lengths))
    return (results.reshape(TOKENS, D), gradients.reshape(TOKENS, D), totals[0], totals[1], totals[2], totals[3], totals[4], totals[5], totals[6], totals[7], totals[8], totals[9], totals[10], totals[11], totals[12], totals[13])
```

```python
import functools

import jax
import jax.numpy as jnp
from jax import lax
from jax.experimental import pallas as pl
from jax.experimental.pallas import tpu as pltpu
from jax.sharding import PartitionSpec as P


WIDTH = 512
QUARTER = 128
HALF = 256
HIDDEN = 1024
LOCAL = 4
SIZE = 64
EPS = 1e-05
NEG = -1e30

BF = jnp.bfloat16
F32 = jnp.float32

ATTN = 512
FFN = 1024
THIRD = 384
PAD = 16


def nn(left, right):
    return lax.dot_general(left, right, (((1,), (0,)), ((), ())), preferred_element_type=F32)


def nt(left, right):
    return lax.dot_general(left, right, (((1,), (1,)), ((), ())), preferred_element_type=F32)


def tn(left, right):
    return lax.dot_general(left, right, (((0,), (0,)), ((), ())), preferred_element_type=F32)


def lanes(start, count=QUARTER):
    return pl.ds(pl.multiple_of(start, QUARTER), count)


def rows_at(start, count, unit):
    return pl.ds(pl.multiple_of(start, unit), count)


def iota(shape, dim):
    return lax.broadcasted_iota(jnp.int32, shape, dim)


def standard(states):
    center = states - jnp.mean(states, -1, keepdims=True)
    inverse = lax.rsqrt(jnp.mean(center * center, -1, keepdims=True) + EPS)
    return center * inverse, inverse


def norm_back(delta, normed, inverse):
    return inverse * (
        delta
        - jnp.mean(delta, -1, keepdims=True)
        - normed * jnp.mean(delta * normed, -1, keepdims=True)
    )


def gelu_parts(x):
    z = x * 0.7071067811865476
    t = 1.0 / (1.0 + 0.3275911 * jnp.abs(z))
    e = jnp.exp(-z * z)
    poly = t * (
        0.127414796
        + t * (-0.142248368 + t * (0.7107068705 + t * (-0.7265760135 + t * 0.5307027145)))
    )
    tail = poly * e
    phi = jnp.where(z >= 0, 1.0 - tail, tail)
    return x * phi, phi + x * e * 0.3989422804014327


def reader(refs, split):
    own, xs, ys, da, db = refs

    def read(r, part, at, rows):
        if r == 3:
            return (da, db)[part][at : at + rows, :]
        start = at + split * part
        return (own, xs, ys)[r][start : start + rows, :]

    return read


def writer(refs):
    ao, ax, bo, by = refs

    def write(r, part, at, value):
        ref, slot = (((ao, 0), (ax, 0), (ao, 1), (ax, 1)), ((bo, 0), (bo, 1), (by, 0), (by, 1)))[part][r]
        ref[slot, at : at + value.shape[0], :] = value

    return write


def pair_rows(pair):
    is_value = pair >= 8
    first = jnp.where(is_value, 512 + 64 * (pair - 8), 256 * (pair >> 2) + 32 * (pair & 3))
    second = jnp.where(is_value, first + 32, first + 128)
    return first, second


def pack_attn(k, project, merge, turned, put, base):
    turned[...] = jnp.swapaxes(project[...], 0, 1)
    for p in range(3):
        chunk = turned[rows_at(128 * p + 64 * k, 64, 64), :]
        for j in range(4):
            put(j // 2, base[j // 2] + (j % 2) * 192 + p * 64, chunk[:, 128 * j : 128 * j + 128])
    for pair in range(4):
        block = merge[rows_at(128 * pair + 64 * k, 64, 64), :]
        put(pair // 2, base[pair // 2] + 384 + (pair % 2) * 64, block)


def unpack_attn(c, read, base, project, merge):
    for r in range(4):
        q = c ^ r
        for p in range(3):
            first, second = pair_rows(3 * q + p)
            for j in range(4):
                block = read(r, j // 2, base[j // 2] + (j % 2) * 192 + p * 64, 64)
                project[rows_at(first, 32, 32), 128 * j : 128 * j + 128] = block[:32]
                project[rows_at(second, 32, 32), 128 * j : 128 * j + 128] = block[32:]
        for pair in range(4):
            block = read(r, pair // 2, base[pair // 2] + 384 + (pair % 2) * 64, 64)
            merge[64 * pair : 64 * pair + 64, lanes(128 * q)] = block


def regroup_attn(c, write, base, project, merge):
    for r in range(4):
        q = c ^ r
        for p in range(3):
            first, second = pair_rows(3 * q + p)
            for j in range(4):
                at = base[j // 2] + (j % 2) * 192 + p * 64
                write(r, j // 2, at, project[rows_at(first, 32, 32), 128 * j : 128 * j + 128])
                write(r, j // 2, at + 32, project[rows_at(second, 32, 32), 128 * j : 128 * j + 128])
        for pair in range(4):
            block = merge[64 * pair : 64 * pair + 64, lanes(128 * q)]
            write(r, pair // 2, base[pair // 2] + 384 + (pair % 2) * 64, block)


def pack_ffn(k, widen, narrow, put):
    for lc in range(2):
        put(0, 512 * lc, widen[:, lanes(256 * k + 128 * lc)])
    for qq in range(4):
        put(1, 256 * qq, narrow[rows_at(512 * qq + 256 * k, 256, 256), :])


def unpack_ffn(c, read, widen, narrow):
    for r in range(4):
        q = c ^ r
        for lc in range(2):
            widen[:, lanes(256 * q + 128 * lc)] = read(r, 0, 512 * lc, 512)
        narrow[:, lanes(128 * q)] = read(r, 1, 0, FFN)


def regroup_ffn(c, write, base, widen, narrow):
    for r in range(4):
        q = c ^ r
        for lc in range(2):
            write(r, 0, base[0] + 512 * lc, widen[:, lanes(256 * q + 128 * lc)])
        write(r, 1, base[1], narrow[:, lanes(128 * q)])


def pack_pool(k, pool, put, base):
    for i in range(6):
        put(i // 3, base + (i % 3) * 128, pool[rows_at(512 * (i // 2) + 256 * k + 128 * (i % 2), 128, 128), :])


def unpack_pool(c, read, base, pool):
    for r in range(4):
        for i in range(6):
            pool[128 * i : 128 * i + 128, lanes(128 * (c ^ r))] = read(r, i // 3, base + (i % 3) * 128, 128)


def regroup_pool(c, write, base, pool):
    for r in range(4):
        for i in range(6):
            block = pool[128 * i : 128 * i + 128, lanes(128 * (c ^ r))]
            write(r, i // 3, base[i // 3] + (i % 3) * 128, block)


def pack_expand(k, expand, put, base):
    for i in range(6):
        block = expand[rows_at(256 * k + 128 * (i % 2), 128, 128), 128 * (i // 2) : 128 * (i // 2) + 128]
        put(i // 3, base + (i % 3) * 128, block)


def unpack_expand(c, read, base, expand):
    for r in range(4):
        for i in range(6):
            block = read(r, i // 3, base + (i % 3) * 128, 128)
            expand[128 * (i % 2) : 128 * (i % 2) + 128, lanes(384 * (c ^ r) + 128 * (i // 2))] = block


def regroup_expand(c, write, base, expand):
    for r in range(4):
        for i in range(6):
            block = expand[128 * (i % 2) : 128 * (i % 2) + 128, lanes(384 * (c ^ r) + 128 * (i // 2))]
            write(r, i // 3, base[i // 3] + (i % 3) * 128, block)


def regroup_gain(c, write, gain):
    for r in range(4):
        write(r, 0, 0, gain[:, lanes(128 * (c ^ r))].astype(BF))


def putter(ref, split):
    def put(part, at, value):
        start = at + split * part
        ref[start : start + value.shape[0], :] = value

    return put


def pack_first_kernel(who, project, merge, g0, g1, g2, g3, out, turned):
    k = who[1]
    row = iota((PAD, QUARTER), 0)
    gains = jnp.zeros((PAD, QUARTER), F32)
    for i, gain in enumerate((g0, g1, g2, g3)):
        gains = jnp.where(row == i, gain[...].astype(F32), gains)
    out[0:PAD, :] = gains.astype(BF)
    pack_attn(k, project, merge, turned, putter(out, PAD + ATTN), (PAD, 0))


def pack_rest_kernel(who, widen, narrow, pool, project, merge, s_widen, s_narrow, expand, out2, out3, out4, turned):
    k = who[1]
    pack_ffn(k, widen, narrow, putter(out2, FFN))
    put = putter(out3, THIRD + ATTN)
    pack_pool(k, pool, put, 0)
    pack_attn(k, project, merge, turned, put, (THIRD, THIRD))
    put = putter(out4, FFN + THIRD)
    pack_ffn(k, s_widen, s_narrow, put)
    pack_expand(k, expand, put, FFN)


def ends_of(who):
    e0 = who[2]
    e1 = e0 + who[3]
    e2 = e1 + who[4]
    return e0, e1, e2, e2 + who[5]


def segment_of(who, index, unit):
    return sum((index >= unit * end).astype(jnp.int32) for end in ends_of(who))


def head_masks():
    lane = iota((1, HALF), 1)
    turned = [((lane & 127) >> 5 == h).astype(F32).astype(BF) for h in range(LOCAL)]
    plain = [((lane >> 6) == h).astype(F32).astype(BF) for h in range(LOCAL)]
    return turned, plain


def attention_forward(who, states, gain, cos, sin, project, merge, first, q, k, v, att, ctx, mix, unit, block):
    count = states.shape[0]
    normed, _ = standard(states)
    start = (normed * gain).astype(BF)
    first[...] = start
    packed = nt(start, project[...])
    cosine, sine = cos[...], sin[...]
    for ref, at in ((q, 0), (k, 256)):
        a, b = packed[:, at : at + 128], packed[:, at + 128 : at + 256]
        ref[:, 0:128] = (a * cosine - b * sine).astype(BF)
        ref[:, 128:256] = (b * cosine + a * sine).astype(BF)
    v[...] = packed[:, 512:768].astype(BF)
    turned, plain = head_masks()
    scale = jnp.asarray(SIZE**-0.5, BF)
    for b in range(count // block):
        low, stop = b * block, (b + 1) * block
        at_row = low + iota((block, 1), 0)
        at_col = iota((1, stop), 1)
        allowed = (segment_of(who, at_row, unit) == segment_of(who, at_col, unit)) & (at_row >= at_col)
        queries = q[low:stop, :] * scale
        keys, values = k[0:stop, :], v[0:stop, :]
        total_context = jnp.zeros((block, HALF), F32)
        for h in range(LOCAL):
            scores = jnp.where(allowed, nt(queries * turned[h], keys), NEG)
            powered = jnp.exp(scores - jnp.max(scores, -1, keepdims=True))
            attend = (powered * (1.0 / jnp.sum(powered, -1, keepdims=True))).astype(BF)
            att[b, h * block : (h + 1) * block, 0:stop] = attend
            total_context = total_context + nn(attend, values * plain[h])
        ctx[low:stop, :] = total_context.astype(BF)
    mix[...] = nn(ctx[...], merge[...]).astype(BF)


def full_attention_kernel(
    who, tokens, cos, sin, s, x, y, da, db, gains, project, merge, first, q, k, v, att, ctx, mix
):
    c = who[0]
    read = reader((s, x, y, da, db), PAD + ATTN)
    for r in range(4):
        gains[:, lanes(128 * (c ^ r))] = read(r, 0, 0, PAD).astype(F32)
    unpack_attn(c, read, (PAD, 0), project, merge)
    states = tokens[...].astype(F32)
    attention_forward(
        who, states, gains[0:1, :], cos, sin, project, merge, first, q, k, v, att, ctx, mix, 3, QUARTER
    )


def short_attention_kernel(
    who, own, came, cos, sin, gains, s, x, y, da, db, states, project, merge, first, q, k, v, att, ctx, mix
):
    unpack_attn(who[0], reader((s, x, y, da, db), THIRD + ATTN), (THIRD, THIRD), project, merge)
    states[...] = (own[...].astype(F32) + came[...].astype(F32)).astype(BF)
    attention_forward(
        who, states[...].astype(F32), gains[2:3, :], cos, sin, project, merge, first, q, k, v, att, ctx, mix,
        1, own.shape[0],
    )


def ffn_kernel(
    gain_row, split, who, states, own, came, gains, s, x, y, da, db, middle, second, widen, narrow, hidden, slope, out
):
    unpack_ffn(who[0], reader((s, x, y, da, db), split), widen, narrow)
    mid = states[...].astype(F32) + (own[...].astype(F32) + came[...].astype(F32))
    middle[...] = mid
    normed, _ = standard(mid)
    start = (normed * gains[gain_row : gain_row + 1, :]).astype(BF)
    second[...] = start
    total = jnp.zeros(mid.shape, F32)
    for i in range(4):
        cols = slice(HALF * i, HALF * i + HALF)
        value, back = gelu_parts(nn(start, widen[:, cols]))
        value = value.astype(BF)
        hidden[:, cols] = value
        slope[:, cols] = back.astype(BF)
        total = total + nn(value, narrow[cols, :])
    out[...] = total.astype(BF)


def join_masks(who, groups, count, real):
    g = iota((groups, 1), 0)
    t = iota((1, count), 1)
    ends = ends_of(who)
    keep = (g != ends[0]) & (g != ends[1]) & (g != ends[2]) & (g < real)
    return [
        jnp.where((t == 3 * g - 2) & keep, 1.0, 0.0).astype(BF),
        jnp.where((t == 3 * g - 1) & keep, 1.0, 0.0).astype(BF),
        jnp.where((t == 3 * g) & (g < real), 1.0, 0.0).astype(BF),
    ]


def group_masks(groups, count, real):
    g = iota((groups, 1), 0)
    t = iota((1, count), 1)
    return [jnp.where((t == 3 * g + i) & (g < real), 1.0, 0.0).astype(BF) for i in range(3)]


def pool_kernel(real, who, middle, own, came, s, x, y, da, db, full, pool, joined, out):
    k = who[1]
    unpack_pool(who[0], reader((s, x, y, da, db), THIRD + ATTN), 0, pool)
    full[...] = (middle[...] + (own[...].astype(F32) + came[...].astype(F32))).astype(BF)
    part = full[:, lanes(HALF * k, HALF)]
    for j, mask in enumerate(join_masks(who, joined.shape[0], full.shape[0], real)):
        joined[:, HALF * j : HALF * j + HALF] = nn(mask, part).astype(BF)
    out[...] = nn(joined[...], pool[...]).astype(BF)


def expand_back_kernel(real, who, target, s, x, y, da, db, expand, grouped, out):
    unpack_expand(who[0], reader((s, x, y, da, db), FFN + THIRD), FFN, expand)
    for i, mask in enumerate(group_masks(grouped.shape[0], target.shape[0], real)):
        grouped[:, WIDTH * i : WIDTH * i + WIDTH] = nn(mask, target[...]).astype(BF)
    out[...] = nt(grouped[...], expand[...]).astype(BF)


def expand_kernel(real, who, middle, own, came, expand, part, out, short):
    k = who[1]
    short[...] = (middle[...] + (own[...].astype(F32) + came[...].astype(F32))).astype(BF)
    part[...] = short[:, lanes(HALF * k, HALF)]
    grown = nn(part[...], expand[...]).astype(BF)
    total = jnp.zeros(out.shape, F32)
    for i, mask in enumerate(group_masks(part.shape[0], out.shape[0], real)):
        total = total + tn(mask, grown[:, WIDTH * i : WIDTH * i + WIDTH])
    out[...] = total.astype(BF)


def mixed_kernel(who, full, own, came, out, whole):
    whole[...] = (full[...].astype(F32) + (own[...].astype(F32) + came[...].astype(F32))).astype(BF)
    for r in range(4):
        out[r] = whole[:, lanes(128 * (who[0] ^ r))]


def ffn_back(gain_row, delta, middle, gains, slope, widen, narrow, inner, out, gain):
    total = jnp.zeros(middle.shape, F32)
    for i in range(4):
        cols = slice(HALF * i, HALF * i + HALF)
        value = (nt(delta, narrow[cols, :]) * slope[:, cols].astype(F32)).astype(BF)
        inner[:, cols] = value
        total = total + nt(value, widen[:, cols])
    normed, _ = standard(middle[...])
    out[...] = total.astype(BF)
    gain[...] = jnp.broadcast_to(jnp.sum(total * normed, 0, keepdims=True), gain.shape)


def short_ffn_back_kernel(who, own, came, middle, gains, slope, widen, narrow, delta, inner, out, gain):
    k = who[1]
    delta[:, lanes(HALF * k, HALF)] = own[...]
    delta[:, lanes(HALF * (1 - k), HALF)] = came[...]
    ffn_back(3, delta[...], middle, gains, slope, widen, narrow, inner, out, gain)


def full_ffn_back_kernel(
    who, target, own, came, middle, gains, slope, widen, narrow, delta, low, inner, out, gain
):
    k = who[1]
    delta[:, lanes(HALF * k, HALF)] = own[...].astype(F32)
    delta[:, lanes(HALF * (1 - k), HALF)] = came[...].astype(F32)
    delta[...] = delta[...] + target[...].astype(F32)
    low[...] = delta[...].astype(BF)
    ffn_back(1, low[...], middle, gains, slope, widen, narrow, inner, out, gain)


def attention_back_kernel(
    first_row, second_row, block, who, delta, own, came, middle, gains, states, merge, project, q, k, v, att, cos, sin,
    mid, mix, packed, out, gain, dk, dv,
):
    count = middle.shape[0]
    normed, inverse = standard(middle[...])
    dsecond = own[...].astype(F32) + came[...].astype(F32)
    dmid = delta[...].astype(F32) + norm_back(dsecond * gains[second_row : second_row + 1, :], normed, inverse)
    mid[...] = dmid
    low = dmid.astype(BF)
    mix[...] = low
    dctx = nt(low, merge[...]).astype(BF)
    turned, plain = head_masks()
    scale = SIZE**-0.5
    cosine, sine = cos[...], sin[...]
    dk[...] = jnp.zeros(dk.shape, F32)
    dv[...] = jnp.zeros(dv.shape, F32)
    for b in range(count // block):
        start, stop = b * block, (b + 1) * block
        keys, values = k[0:stop, :], v[0:stop, :]
        queries = q[start:stop, :]
        dcontext = dctx[start:stop, :]
        dq = jnp.zeros((block, HALF), F32)
        for h in range(LOCAL):
            dhead = dcontext * plain[h]
            low_attend = att[b, h * block : (h + 1) * block, 0:stop]
            attend = low_attend.astype(F32)
            dattend = nt(dhead, values)
            dscores = attend * (dattend - jnp.sum(attend * dattend, -1, keepdims=True))
            dscores = (dscores * scale).astype(BF)
            dq = dq + nn(dscores, keys * turned[h])
            dk[0:stop, :] += tn(dscores, queries * turned[h])
            dv[0:stop, :] += tn(low_attend, dhead)
        a, c = dq[:, 0:128], dq[:, 128:256]
        packed[start:stop, 0:128] = (a * cosine[start:stop] + c * sine[start:stop]).astype(BF)
        packed[start:stop, 128:256] = (c * cosine[start:stop] - a * sine[start:stop]).astype(BF)
    a, c = dk[:, 0:128], dk[:, 128:256]
    packed[:, 256:384] = (a * cosine + c * sine).astype(BF)
    packed[:, 384:512] = (c * cosine - a * sine).astype(BF)
    packed[:, 512:768] = dv[...].astype(BF)
    dfirst = nn(packed[...], project[...])
    out[...] = dfirst.astype(BF)
    normed_one, _ = standard(states[...].astype(F32))
    gain[...] = jnp.broadcast_to(jnp.sum(dfirst * normed_one, 0, keepdims=True), gain.shape)


def input_gradient(gain_row, mid, own, came, gains, states):
    normed, inverse = standard(states[...].astype(F32))
    dfirst = own[...].astype(F32) + came[...].astype(F32)
    return mid[...] + norm_back(dfirst * gains[gain_row : gain_row + 1, :], normed, inverse)


def pool_back_kernel(real, who, mid, own, came, gains, states, pool, delta, out):
    delta[...] = input_gradient(2, mid, own, came, gains, states).astype(BF)
    djoined = nt(delta[...], pool[...]).astype(BF)
    total = jnp.zeros(out.shape, F32)
    for j, mask in enumerate(join_masks(who, delta.shape[0], out.shape[0], real)):
        total = total + tn(mask, djoined[:, HALF * j : HALF * j + HALF])
    out[...] = total.astype(BF)


def token_kernel(who, mid, own, came, gains, states, out, whole):
    whole[...] = input_gradient(0, mid, own, came, gains, states).astype(BF)
    for r in range(4):
        out[r] = whole[:, lanes(128 * (who[0] ^ r))]


def ffn_weights(c, write, hidden, delta, second, inner, gain, dwiden, dnarrow):
    dnarrow[...] = tn(hidden[...], delta[...]).astype(BF)
    dwiden[...] = tn(second[...], inner[...]).astype(BF)
    regroup_gain(c, write, gain)
    regroup_ffn(c, write, (PAD, 0), dwiden, dnarrow)


def attn_weights(c, write, ctx, mix, packed, first, gain, dproject, dmerge):
    dproject[...] = tn(packed[...], first[...]).astype(BF)
    dmerge[...] = tn(ctx[...], mix[...]).astype(BF)
    regroup_gain(c, write, gain)
    regroup_attn(c, write, (PAD, 0), dproject, dmerge)


def group_a_kernel(
    who, hidden, delta, second, inner, gain, part, grouped, ao, ax, bo, by, dwiden, dnarrow, dexpand
):
    c, write = who[0], writer((ao, ax, bo, by))
    ffn_weights(c, write, hidden, delta, second, inner, gain, dwiden, dnarrow)
    dexpand[...] = tn(part[...], grouped[...]).astype(BF)
    regroup_expand(c, write, (PAD + FFN, FFN), dexpand)


def group_b_kernel(
    who, ctx, mix, packed, first, gain, joined, delta, ao, ax, bo, by, dproject, dmerge, dpool
):
    c, write = who[0], writer((ao, ax, bo, by))
    attn_weights(c, write, ctx, mix, packed, first, gain, dproject, dmerge)
    dpool[...] = tn(joined[...], delta[...]).astype(BF)
    regroup_pool(c, write, (PAD + ATTN, ATTN), dpool)


def group_c_kernel(who, hidden, delta, second, inner, gain, ao, ax, bo, by, dwiden, dnarrow):
    ffn_weights(who[0], writer((ao, ax, bo, by)), hidden, delta, second, inner, gain, dwiden, dnarrow)


def group_d_kernel(who, ctx, mix, packed, first, gain, ao, ax, bo, by, dproject, dmerge):
    attn_weights(who[0], writer((ao, ax, bo, by)), ctx, mix, packed, first, gain, dproject, dmerge)


def both(who, own, came):
    return ((who[1], own), (1 - who[1], came))


def spread_gain(own, came, gain):
    gain[...] = own[0:8, :].astype(F32) + came[0:8, :].astype(F32)


def spread_ffn(who, own, came, base_a, base_b, widen, narrow):
    for k, ref in both(who, own, came):
        for lc in range(2):
            widen[:, lanes(256 * k + 128 * lc)] = ref[base_a + 512 * lc : base_a + 512 * lc + 512, :].astype(F32)
        for qq in range(4):
            block = ref[base_b + 256 * qq : base_b + 256 * qq + 256, :]
            narrow[rows_at(512 * qq + 256 * k, 256, 256), :] = block.astype(F32)


def spread_attn(who, own, came, base_a, base_b, project, merge, turned):
    for k, ref in both(who, own, came):
        for j in range(4):
            for p in range(3):
                at = (base_b if j >= 2 else base_a) + (j % 2) * 192 + p * 64
                block = ref[at : at + 64, :].astype(F32)
                turned[rows_at(128 * p + 64 * k, 64, 64), 128 * j : 128 * j + 128] = block
        for pair in range(4):
            at = (base_b if pair >= 2 else base_a) + 384 + (pair % 2) * 64
            merge[rows_at(128 * pair + 64 * k, 64, 64), :] = ref[at : at + 64, :].astype(F32)
    project[...] = jnp.swapaxes(turned[...], 0, 1)


def spread_a_kernel(who, own, came, gain, widen, narrow, expand):
    split = PAD + FFN + THIRD
    spread_gain(own, came, gain)
    spread_ffn(who, own, came, PAD, split, widen, narrow)
    for k, ref in both(who, own, came):
        for i in range(6):
            at = (split + FFN if i >= 3 else PAD + FFN) + (i % 3) * 128
            block = ref[at : at + 128, :].astype(F32)
            expand[rows_at(256 * k + 128 * (i % 2), 128, 128), 128 * (i // 2) : 128 * (i // 2) + 128] = block


def spread_b_kernel(who, own, came, gain, project, merge, pool, turned):
    split = PAD + ATTN + THIRD
    spread_gain(own, came, gain)
    spread_attn(who, own, came, PAD, split, project, merge, turned)
    for k, ref in both(who, own, came):
        for i in range(6):
            at = (split + ATTN if i >= 3 else PAD + ATTN) + (i % 3) * 128
            block = ref[at : at + 128, :].astype(F32)
            pool[rows_at(512 * (i // 2) + 256 * k + 128 * (i % 2), 128, 128), :] = block


def spread_c_kernel(who, own, came, gain, widen, narrow):
    spread_gain(own, came, gain)
    spread_ffn(who, own, came, PAD, PAD + FFN, widen, narrow)


def spread_d_kernel(who, own, came, gain, project, merge, turned):
    spread_gain(own, came, gain)
    spread_attn(who, own, came, PAD, PAD + ATTN, project, merge, turned)


def call(kernel, name, outs, who, *args, scratch=(), flops=0):
    whole = pl.BlockSpec(memory_space=pltpu.VMEM)
    moved = sum(a.size * a.dtype.itemsize for a in args)
    return pl.pallas_call(
        kernel,
        name=name,
        out_shape=[jax.ShapeDtypeStruct(shape, dtype) for shape, dtype in outs],
        in_specs=[pl.BlockSpec(memory_space=pltpu.SMEM)] + [whole] * len(args),
        out_specs=[whole] * len(outs),
        scratch_shapes=[pltpu.VMEM(shape, dtype) for shape, dtype in scratch],
        compiler_params=pltpu.CompilerParams(vmem_limit_bytes=56 * 2**20),
        cost_estimate=pl.CostEstimate(flops=flops, bytes_accessed=moved, transcendentals=0),
    )(who, *args)


def swap(value, distance):
    return lax.ppermute(value, "section", [(i, i ^ distance) for i in range(lax.axis_size("section"))])


def across(value):
    return lax.ppermute(value, "dp", [(i, i ^ 1) for i in range(lax.axis_size("dp"))])


def gather(pieces, split):
    xs, ys = swap(pieces, 1), swap(pieces, 2)
    return pieces, xs, ys, swap(xs[:split], 2), swap(ys[split:], 1)


def reduce_section(ao, ax, bo, by):
    from_x = swap(ax, 1)
    from_y = swap(by, 2)
    send_y = ao[1] + from_x[1]
    send_x = bo[1] + from_y[1]
    last_y = swap(send_y, 2)
    last_x = swap(send_x, 1)
    return jnp.concatenate([ao[0] + from_x[0] + last_y, bo[0] + from_y[0] + last_x], 0)


def reduce_rows(value):
    count = lax.axis_size("dp")
    if count != 8:
        groups = [[i for i in range(count) if i % 2 == core] for core in range(2)]
        return lax.psum(value, "dp", axis_index_groups=groups)

    def line(value, pairs):
        return lax.ppermute(value, "dp", [(2 * a + core, 2 * b + core) for a, b in pairs for core in range(2)])

    place = lax.axis_index("dp") // 2
    value = value + line(value, [(0, 1), (3, 2)])
    value = value + line(value, [(1, 2), (2, 1)])
    ended = line(value, [(1, 0), (2, 3)])
    return jnp.where((place == 0) | (place == 3), ended, value)


def deliver(pieces, c, k):
    chips, count = lax.axis_size("section"), lax.axis_size("dp")
    came = [pieces[0]]
    for r in range(1, 4):
        route = [
            (chip * count + d, (chip ^ r) * count + d)
            for chip in range(chips)
            for d in range(count)
            if d % 2 == chip // 2
        ]
        came.append(lax.ppermute(pieces[r], ("section", "dp"), route))
    rows = []
    for j in range(2):
        r = c ^ (2 * k + j)
        rows.append(jnp.where(r < 2, jnp.where(r == 0, came[0], came[1]), jnp.where(r == 2, came[2], came[3])))
    return rows


def angles(places):
    freq = 10000.0 ** (-2.0 * jnp.arange(SIZE // 2, dtype=F32) / SIZE)
    phase = places.astype(F32)[:, None] * jnp.tile(freq, LOCAL)[None, :]
    return jnp.cos(phase), jnp.sin(phase)


def places_of(counts, count, unit):
    at = jnp.arange(count, dtype=jnp.int32)
    begin = jnp.zeros((count,), jnp.int32)
    end = jnp.int32(0)
    for i in range(3):
        end = end + counts[i]
        begin = jnp.where(at >= unit * end, unit * end, begin)
    return at - begin


def body(
    tokens,
    lengths,
    cotangent,
    full_first_gain,
    full_project,
    full_merge,
    full_second_gain,
    full_widen,
    full_narrow,
    pool_weight,
    short_first_gain,
    short_project,
    short_merge,
    short_second_gain,
    short_widen,
    short_narrow,
    expand_weight,
):
    c = lax.axis_index("section")
    d = lax.axis_index("dp")
    k = d % 2
    rows = lengths.shape[0]
    length = tokens.shape[0] // rows
    groups = length // 3
    count = -(-length // QUARTER) * QUARTER
    short = -(-groups // 16) * 16

    here = k == c // 2
    who_k = jnp.stack([c, k]).astype(jnp.int32)
    pieces1, = call(
        pack_first_kernel, "pack_first", [((PAD + 2 * ATTN, QUARTER), BF)], who_k, full_project, full_merge,
        *[g.reshape(1, QUARTER) for g in (full_first_gain, full_second_gain, short_first_gain, short_second_gain)],
        scratch=[((3 * QUARTER, WIDTH), BF)],
    )
    pieces2, pieces3, pieces4 = call(
        pack_rest_kernel, "pack_rest",
        [((2 * FFN, QUARTER), BF), ((2 * (THIRD + ATTN), QUARTER), BF), ((2 * (FFN + THIRD), QUARTER), BF)],
        who_k, full_widen, full_narrow, pool_weight, short_project, short_merge, short_widen, short_narrow,
        expand_weight, scratch=[((3 * QUARTER, WIDTH), BF)],
    )
    stage1 = gather(pieces1, PAD + ATTN)
    pieces2, stage1 = lax.optimization_barrier((pieces2, stage1))
    stage2 = gather(pieces2, FFN)
    pieces3, stage2 = lax.optimization_barrier((pieces3, stage2))
    stage3 = gather(pieces3, THIRD + ATTN)
    pieces4, stage3 = lax.optimization_barrier((pieces4, stage3))
    stage4 = gather(pieces4, FFN + THIRD)

    def mine(array):
        own = lax.dynamic_index_in_dim(array, c % 2, 0, keepdims=False)
        return jnp.where(here, own, across(own))

    counts = mine(lengths)
    row = jnp.pad(mine(tokens.reshape(rows, length, WIDTH)), ((0, count - length), (0, 0)))
    target = jnp.pad(mine(cotangent.reshape(rows, length, WIDTH)), ((0, count - length), (0, 0)))
    live = 3 * (counts[0] + counts[1] + counts[2])
    target = jnp.where(jnp.arange(count)[:, None] < live, target, jnp.zeros_like(target))
    who = jnp.concatenate([who_k, counts, jnp.zeros((2,), jnp.int32)])
    cos, sin = angles(places_of(counts, count, 3))
    short_cos, short_sin = angles(places_of(counts, short, 1))

    def block_outs(n):
        return [
            ((3 * HALF, WIDTH), BF),
            ((HALF, WIDTH), BF),
            ((n, WIDTH), BF),
            ((n, HALF), BF),
            ((n, HALF), BF),
            ((n, HALF), BF),
        ]

    def ffn_outs(n):
        return [
            ((n, WIDTH), F32),
            ((n, WIDTH), BF),
            ((WIDTH, HIDDEN), BF),
            ((HIDDEN, WIDTH), BF),
            ((n, HIDDEN), BF),
            ((n, HIDDEN), BF),
            ((n, WIDTH), BF),
        ]

    gains, project, merge, first, q, key, v, att, ctx, mix = call(
        full_attention_kernel, "full_attention",
        [((PAD, WIDTH), F32)] + block_outs(count)
        + [((count // QUARTER, LOCAL * QUARTER, count), BF), ((count, HALF), BF), ((count, WIDTH), BF)],
        who, row, cos, sin, *stage1, flops=2 * 10**9,
    )
    middle, second, widen, narrow, hidden, slope, part = call(
        functools.partial(ffn_kernel, 1, FFN), "full_ffn", ffn_outs(count),
        who, row, mix, across(mix), gains, *stage2, flops=2 * 10**9,
    )
    full, pool, joined, pooled = call(
        functools.partial(pool_kernel, groups), "pool",
        [((count, WIDTH), BF), ((3 * HALF, WIDTH), BF), ((short, 3 * HALF), BF), ((short, WIDTH), BF)],
        who, middle, part, across(part), *stage3, flops=3 * 10**8,
    )
    s_in, s_project, s_merge, s_first, s_q, s_key, s_v, s_att, s_ctx, s_mix = call(
        short_attention_kernel, "short_attention",
        [((short, WIDTH), BF)] + block_outs(short)
        + [((1, LOCAL * short, short), BF), ((short, HALF), BF), ((short, WIDTH), BF)],
        who, pooled, across(pooled), short_cos, short_sin, gains, *stage3, flops=5 * 10**8,
    )
    s_middle, s_second, s_widen, s_narrow, s_hidden, s_slope, s_part = call(
        functools.partial(ffn_kernel, 3, FFN + THIRD), "short_ffn", ffn_outs(short),
        who, s_in, s_mix, across(s_mix), gains, *stage4, flops=7 * 10**8,
    )
    expand, grouped, d_half = call(
        functools.partial(expand_back_kernel, groups), "expand_back",
        [((HALF, 3 * WIDTH), BF), ((short, 3 * WIDTH), BF), ((short, HALF), BF)],
        who, target, *stage4, flops=4 * 10**8,
    )
    s_half, grown = call(
        functools.partial(expand_kernel, groups), "expand", [((short, HALF), BF), ((count, WIDTH), BF)],
        who, s_middle, s_part, across(s_part), expand, scratch=[((short, WIDTH), BF)], flops=4 * 10**8,
    )
    mixed, = call(
        mixed_kernel, "mixed", [((4, count, QUARTER), BF)], who, full, grown, across(grown),
        scratch=[((count, WIDTH), BF)],
    )

    def back_outs(n):
        return [
            ((n, WIDTH), F32),
            ((n, WIDTH), BF),
            ((n, 3 * HALF), BF),
            ((n, WIDTH), BF),
            ((PAD, WIDTH), F32),
        ]

    def sent(part_a, part_b):
        return [((2, part_a, QUARTER), BF)] * 2 + [((2, part_b, QUARTER), BF)] * 2

    s_delta, s_inner, s_dsecond, s_gain2 = call(
        short_ffn_back_kernel, "short_ffn_back",
        [((short, WIDTH), BF), ((short, HIDDEN), BF), ((short, WIDTH), BF), ((PAD, WIDTH), F32)],
        who, d_half, across(d_half), s_middle, gains, s_slope, s_widen, s_narrow, flops=7 * 10**8,
    )
    group_a = call(
        group_a_kernel, "group_a", sent(PAD + FFN + THIRD, FFN + THIRD),
        who, s_hidden, s_delta, s_second, s_inner, s_gain2, s_half, grouped,
        scratch=[((WIDTH, HIDDEN), BF), ((HIDDEN, WIDTH), BF), ((HALF, 3 * WIDTH), BF)], flops=10**9,
    )
    s_mid, s_dmix, s_dpacked, s_dfirst, s_gain1 = call(
        functools.partial(attention_back_kernel, 2, 3, short), "short_attention_back", back_outs(short),
        who, s_delta, s_dsecond, across(s_dsecond), s_middle, gains, s_in, s_merge, s_project, s_q, s_key, s_v, s_att,
        short_cos, short_sin, scratch=[((short, HALF), F32)] * 2, flops=5 * 10**8,
    )
    d_in, d_low = call(
        functools.partial(pool_back_kernel, groups), "pool_back", [((short, WIDTH), BF), ((count, HALF), BF)],
        who, s_mid, s_dfirst, across(s_dfirst), gains, s_in, pool, flops=3 * 10**8,
    )
    group_b = call(
        group_b_kernel, "group_b", sent(PAD + ATTN + THIRD, ATTN + THIRD),
        who, s_ctx, s_dmix, s_dpacked, s_first, s_gain1, joined, d_in,
        scratch=[((3 * HALF, WIDTH), BF), ((HALF, WIDTH), BF), ((3 * HALF, WIDTH), BF)], flops=5 * 10**8,
    )
    delta, low, inner, dsecond, gain2 = call(
        full_ffn_back_kernel, "full_ffn_back",
        [((count, WIDTH), F32), ((count, WIDTH), BF), ((count, HIDDEN), BF), ((count, WIDTH), BF), ((PAD, WIDTH), F32)],
        who, target, d_low, across(d_low), middle, gains, slope, widen, narrow, flops=2 * 10**9,
    )
    group_c = call(
        group_c_kernel, "group_c", sent(PAD + FFN, FFN), who, hidden, low, second, inner, gain2,
        scratch=[((WIDTH, HIDDEN), BF), ((HIDDEN, WIDTH), BF)], flops=2 * 10**9,
    )
    mid, dmix, dpacked, dfirst, gain1 = call(
        functools.partial(attention_back_kernel, 0, 1, QUARTER), "full_attention_back", back_outs(count),
        who, delta, dsecond, across(dsecond), middle, gains, row, merge, project, q, key, v, att, cos, sin,
        scratch=[((count, HALF), F32)] * 2, flops=2 * 10**9,
    )
    group_d = call(
        group_d_kernel, "group_d", sent(PAD + ATTN, ATTN), who, ctx, dmix, dpacked, first, gain1,
        scratch=[((3 * HALF, WIDTH), BF), ((HALF, WIDTH), BF)], flops=10**9,
    )
    token, = call(
        token_kernel, "token", [((4, count, QUARTER), BF)], who, mid, dfirst, across(dfirst), gains, row,
        scratch=[((count, WIDTH), BF)],
    )

    def finish(group):
        value = reduce_rows(reduce_section(*group))
        return value, across(value)

    gain_out = ((8, QUARTER), F32)
    ffn_out = [((WIDTH, WIDTH), F32), ((4 * WIDTH, QUARTER), F32)]
    attn_out = [((WIDTH, 3 * QUARTER), F32), ((WIDTH, QUARTER), F32)]
    turned = [((3 * QUARTER, WIDTH), F32)]
    g_s2, g_s_widen, g_s_narrow, g_expand = call(
        spread_a_kernel, "spread_a", [gain_out] + ffn_out + [((WIDTH, 3 * QUARTER), F32)], who, *finish(group_a)
    )
    g_s1, g_s_project, g_s_merge, g_pool = call(
        spread_b_kernel, "spread_b", [gain_out] + attn_out + [((3 * WIDTH, QUARTER), F32)], who, *finish(group_b),
        scratch=turned,
    )
    g_f2, g_widen, g_narrow = call(spread_c_kernel, "spread_c", [gain_out] + ffn_out, who, *finish(group_c))
    g_f1, g_project, g_merge = call(
        spread_d_kernel, "spread_d", [gain_out] + attn_out, who, *finish(group_d), scratch=turned
    )

    def laid(pieces):
        return jnp.concatenate([piece[:length] for piece in deliver(pieces, c, k)], 0)

    return (
        laid(mixed),
        laid(token),
        g_f1[0],
        g_project,
        g_merge,
        g_f2[0],
        g_widen,
        g_narrow,
        g_pool,
        g_s1[0],
        g_s_project,
        g_s_merge,
        g_s2[0],
        g_s_widen,
        g_s_narrow,
        g_expand,
    )


def solution(mesh):
    in_specs = (
        P("dp", None),
        P("dp", None),
        P("dp", None),
        P("section"),
        P(None, "section"),
        P(None, "section"),
        P("section"),
        P(None, "section"),
        P(None, "section"),
        P(None, "section"),
        P("section"),
        P(None, "section"),
        P(None, "section"),
        P("section"),
        P(None, "section"),
        P(None, "section"),
        P(None, "section"),
    )
    out_specs = (
        P("dp", "section"),
        P("dp", "section"),
        P("section"),
        P(None, "section"),
        P(None, "section"),
        P("section"),
        P(None, "section"),
        P(None, "section"),
        P(None, "section"),
        P("section"),
        P(None, "section"),
        P(None, "section"),
        P("section"),
        P(None, "section"),
        P(None, "section"),
        P(None, "section"),
    )
    return jax.shard_map(body, mesh=mesh, in_specs=in_specs, out_specs=out_specs, check_vma=False)
```

```python
import functools

import jax
import jax.numpy as jnp
from jax import lax
from jax.experimental import pallas as pl
from jax.experimental.pallas import tpu as pltpu
from jax.sharding import PartitionSpec as P


WIDTH = 512
QUARTER = 128
HALF = 256
HIDDEN = 1024
SEGS = 4
LOCAL = 4
SIZE = 64
EPS = 1e-05
NEG = -1e30

BF = jnp.bfloat16
F32 = jnp.float32

ATTN = 1024
FFN = 2048
THIRD = 768
PAD = 32
VMEM_LIMIT = 16 * 2**20
PACK_LIMIT = 60 * 2**20


def nn(left, right):
    return lax.dot_general(left, right, (((1,), (0,)), ((), ())), preferred_element_type=F32)


def nt(left, right):
    return lax.dot_general(left, right, (((1,), (1,)), ((), ())), preferred_element_type=F32)


def tn(left, right):
    return lax.dot_general(left, right, (((0,), (0,)), ((), ())), preferred_element_type=F32)


def lanes(start, count=QUARTER):
    return pl.ds(pl.multiple_of(start, QUARTER), count)


def rows_at(start, count, unit):
    return pl.ds(pl.multiple_of(start, unit), count)


def iota(shape, dim):
    return lax.broadcasted_iota(jnp.int32, shape, dim)


def standard(states):
    center = states - jnp.mean(states, -1, keepdims=True)
    inverse = lax.rsqrt(jnp.mean(center * center, -1, keepdims=True) + EPS)
    return center * inverse, inverse


def norm_back(delta, normed, inverse):
    return inverse * (
        delta
        - jnp.mean(delta, -1, keepdims=True)
        - normed * jnp.mean(delta * normed, -1, keepdims=True)
    )


def gelu_parts(x):
    z = x * 0.7071067811865476
    t = 1.0 / (1.0 + 0.3275911 * jnp.abs(z))
    e = jnp.exp(-z * z)
    poly = t * (
        0.127414796
        + t * (-0.142248368 + t * (0.7107068705 + t * (-0.7265760135 + t * 0.5307027145)))
    )
    tail = poly * e
    phi = jnp.where(z >= 0, 1.0 - tail, tail)
    return x * phi, phi + x * e * 0.3989422804014327


def chips(who):
    c, k = who[0], who[1]
    return c, c ^ (1 + k), c ^ (2 - k), c ^ 3


def reader(refs, places):
    def read(r, at, rows):
        return refs[r][places[r] + at : places[r] + at + rows, :]

    return read


def writer(keep, send):
    def write(r, at, value):
        ref, slot = ((keep, 0), (send, 0), (keep, 1), (send, 1))[r]
        ref[slot, at : at + value.shape[0], :] = value

    return write


def pair_rows(pair):
    is_value = pair >= 8
    first = jnp.where(is_value, 512 + 64 * (pair - 8), 256 * (pair >> 2) + 32 * (pair & 3))
    second = jnp.where(is_value, first + 32, first + 128)
    return first, second


def pack_attn(k, turned, merge, put, base):
    for p in range(3):
        chunk = turned[rows_at(128 * p + 64 * k, 64, 64), :]
        for j in range(4):
            put(base + j * 192 + p * 64, chunk[:, 128 * j : 128 * j + 128])
    for pair in range(4):
        put(base + 768 + pair * 64, merge[rows_at(128 * pair + 64 * k, 64, 64), :])


def unpack_attn(who, read, base, project, merge):
    for r, q in enumerate(chips(who)):
        for p in range(3):
            first, second = pair_rows(3 * q + p)
            for j in range(4):
                block = read(r, base + j * 192 + p * 64, 64)
                project[rows_at(first, 32, 32), 128 * j : 128 * j + 128] = block[:32]
                project[rows_at(second, 32, 32), 128 * j : 128 * j + 128] = block[32:]
        for pair in range(4):
            merge[64 * pair : 64 * pair + 64, lanes(128 * q)] = read(r, base + 768 + pair * 64, 64)


def regroup_attn(who, write, base, project, merge):
    for r, q in enumerate(chips(who)):
        for p in range(3):
            first, second = pair_rows(3 * q + p)
            for j in range(4):
                at = base + j * 192 + p * 64
                write(r, at, project[rows_at(first, 32, 32), 128 * j : 128 * j + 128])
                write(r, at + 32, project[rows_at(second, 32, 32), 128 * j : 128 * j + 128])
        for pair in range(4):
            write(r, base + 768 + pair * 64, merge[64 * pair : 64 * pair + 64, lanes(128 * q)])


def pack_ffn(k, widen, narrow, put):
    for lc in range(2):
        put(512 * lc, widen.at[:, lanes(256 * k + 128 * lc)])
    for qq in range(4):
        put(1024 + 256 * qq, narrow.at[rows_at(512 * qq + 256 * k, 256, 256), :])


def unpack_ffn(who, read, widen, narrow):
    for r, q in enumerate(chips(who)):
        for lc in range(2):
            widen[:, lanes(256 * q + 128 * lc)] = read(r, 512 * lc, 512)
        narrow[:, lanes(128 * q)] = read(r, 1024, 1024)


def regroup_ffn(who, write, base, widen, narrow):
    for r, q in enumerate(chips(who)):
        for lc in range(2):
            write(r, base + 512 * lc, widen[:, lanes(256 * q + 128 * lc)])
        write(r, base + 1024, narrow[:, lanes(128 * q)])


def pack_pool(k, pool, put, base):
    for i in range(6):
        put(base + i * 128, pool.at[rows_at(512 * (i // 2) + 256 * k + 128 * (i % 2), 128, 128), :])


def unpack_pool(who, read, base, pool):
    for r, q in enumerate(chips(who)):
        for i in range(6):
            pool[128 * i : 128 * i + 128, lanes(128 * q)] = read(r, base + i * 128, 128)


def regroup_pool(who, write, base, pool):
    for r, q in enumerate(chips(who)):
        for i in range(6):
            write(r, base + i * 128, pool[128 * i : 128 * i + 128, lanes(128 * q)])


def pack_expand(k, expand, put, base):
    for i in range(6):
        put(base + i * 128, expand.at[rows_at(256 * k + 128 * (i % 2), 128, 128), pl.ds(128 * (i // 2), 128)])


def unpack_expand(who, read, base, expand):
    for r, q in enumerate(chips(who)):
        for i in range(6):
            block = read(r, base + i * 128, 128)
            expand[128 * (i % 2) : 128 * (i % 2) + 128, lanes(384 * q + 128 * (i // 2))] = block


def regroup_expand(who, write, base, expand):
    for r, q in enumerate(chips(who)):
        for i in range(6):
            block = expand[128 * (i % 2) : 128 * (i % 2) + 128, lanes(384 * q + 128 * (i // 2))]
            write(r, base + i * 128, block)


def regroup_gain(who, write, gain):
    for r, q in enumerate(chips(who)):
        write(r, 0, gain[:, lanes(128 * q)].astype(BF))


class Copies:
    def __init__(self, sems):
        self.sems, self.all = sems, []

    def start(self, source, target):
        copy = pltpu.make_async_copy(source, target, self.sems.at[len(self.all)])
        copy.start()
        self.all.append(copy)

    def putter(self, ref):
        def put(at, source):
            self.start(source, ref.at[pl.ds(at, source.shape[0]), :])

        return put

    def wait(self):
        for copy in self.all:
            copy.wait()


def putter(ref):
    def put(at, value):
        ref[at : at + value.shape[0], :] = value

    return put


def pack_first_kernel(who, project, merge, gains, out, project_in, merge_in, turned, sems):
    copies = Copies(sems)
    copies.start(project, project_in)
    copies.start(merge, merge_in)
    copies.start(gains, out.at[pl.ds(0, PAD), :])
    copies.wait()
    turned[...] = jnp.swapaxes(project_in[...], 0, 1)
    pack_attn(who[1], turned, merge_in, putter(out), PAD)


def pack_rest_kernel(
    who, widen, narrow, pool, project, merge, expand, s_widen, s_narrow, out2, out3, out4,
    project_in, merge_in, turned, sems,
):
    k = who[1]
    copies, last = Copies(sems), Copies(sems.at[pl.ds(2, 24)])
    copies.start(project, project_in)
    copies.start(merge, merge_in)
    pack_ffn(k, widen, narrow, last.putter(out2))
    pack_pool(k, pool, last.putter(out3), 0)
    pack_expand(k, expand, last.putter(out3), THIRD + ATTN)
    pack_ffn(k, s_widen, s_narrow, last.putter(out4))
    copies.wait()
    turned[...] = jnp.swapaxes(project_in[...], 0, 1)
    pack_attn(k, turned, merge_in, putter(out3), THIRD)
    last.wait()


def ends_of(who):
    e0 = who[2]
    e1 = e0 + who[3]
    e2 = e1 + who[4]
    return e0, e1, e2, e2 + who[5]


def segment_of(who, index, unit):
    return sum((index >= unit * end).astype(jnp.int32) for end in ends_of(who))


def head_masks():
    lane = iota((1, HALF), 1)
    turned = [((lane & 127) >> 5 == h).astype(F32).astype(BF) for h in range(LOCAL)]
    plain = [((lane >> 6) == h).astype(F32).astype(BF) for h in range(LOCAL)]
    return turned, plain


def attention_forward(who, states, gain, cos, sin, project, merge, first, q, k, v, att, ctx, mix, unit, block):
    count = states.shape[0]
    normed, _ = standard(states)
    start = (normed * gain).astype(BF)
    first[...] = start
    packed = nt(start, project[...])
    cosine, sine = cos[...], sin[...]
    for ref, at in ((q, 0), (k, 256)):
        a, b = packed[:, at : at + 128], packed[:, at + 128 : at + 256]
        ref[:, 0:128] = (a * cosine - b * sine).astype(BF)
        ref[:, 128:256] = (b * cosine + a * sine).astype(BF)
    v[...] = packed[:, 512:768].astype(BF)
    turned, plain = head_masks()
    scale = jnp.asarray(SIZE**-0.5, BF)
    for b in range(count // block):
        low, stop = b * block, (b + 1) * block
        at_row = low + iota((block, 1), 0)
        at_col = iota((1, stop), 1)
        allowed = (segment_of(who, at_row, unit) == segment_of(who, at_col, unit)) & (at_row >= at_col)
        queries = q[low:stop, :] * scale
        keys, values = k[0:stop, :], v[0:stop, :]
        total_context = jnp.zeros((block, HALF), F32)
        for h in range(LOCAL):
            scores = jnp.where(allowed, nt(queries * turned[h], keys), NEG)
            powered = jnp.exp(scores - jnp.max(scores, -1, keepdims=True))
            attend = (powered * (1.0 / jnp.sum(powered, -1, keepdims=True))).astype(BF)
            att[b, h * block : (h + 1) * block, 0:stop] = attend
            total_context = total_context + nn(attend, values * plain[h])
        ctx[low:stop, :] = total_context.astype(BF)
    mix[...] = nn(ctx[...], merge[...]).astype(BF)


def full_attention_kernel(
    who, own, came, cos, sin, s, x, y, d, row, gains, project, merge, first, q, k, v, att, ctx, mix, sems
):
    c = who[0]
    here = who[1] == c >> 1
    for i, (source, taken) in enumerate(((own, here), (came, jnp.logical_not(here)))):

        @pl.when(taken)
        def _():
            copy = pltpu.make_async_copy(source.at[0], row, sems.at[i])
            copy.start()
            copy.wait()

    read = reader((s, x, y, d), (0,) * 4)
    for r, chip in enumerate(chips(who)):
        gains[:, lanes(128 * chip)] = read(r, 0, PAD).astype(F32)
    unpack_attn(who, read, PAD, project, merge)
    states = row[...].astype(F32)
    attention_forward(
        who, states, gains[0:1, :], cos, sin, project, merge, first, q, k, v, att, ctx, mix, 3, QUARTER
    )


def short_attention_kernel(
    places, who, own, came, cos, sin, gains, s, x, y, d, states, project, merge, first, q, k, v, att, ctx, mix
):
    unpack_attn(who, reader((s, x, y, d), places), THIRD, project, merge)
    states[...] = (own[...].astype(F32) + came[...].astype(F32)).astype(BF)
    attention_forward(
        who, states[...].astype(F32), gains[2:3, :], cos, sin, project, merge, first, q, k, v, att, ctx, mix,
        1, own.shape[0],
    )


def ffn_kernel(
    gain_row, places, who, states, own, came, gains, s, x, y, d, middle, second, widen, narrow, hidden, slope, out
):
    unpack_ffn(who, reader((s, x, y, d), places), widen, narrow)
    mid = states[...].astype(F32) + (own[...].astype(F32) + came[...].astype(F32))
    middle[...] = mid
    normed, _ = standard(mid)
    start = (normed * gains[gain_row : gain_row + 1, :]).astype(BF)
    second[...] = start
    total = jnp.zeros(mid.shape, F32)
    for i in range(4):
        cols = slice(HALF * i, HALF * i + HALF)
        value, back = gelu_parts(nn(start, widen[:, cols]))
        value = value.astype(BF)
        hidden[:, cols] = value
        slope[:, cols] = back.astype(BF)
        total = total + nn(value, narrow[cols, :])
    out[...] = total.astype(BF)


def join_masks(who, groups, count, real):
    g = iota((groups, 1), 0)
    t = iota((1, count), 1)
    ends = ends_of(who)
    keep = (g != ends[0]) & (g != ends[1]) & (g != ends[2]) & (g < real)
    return [
        jnp.where((t == 3 * g - 2) & keep, 1.0, 0.0).astype(BF),
        jnp.where((t == 3 * g - 1) & keep, 1.0, 0.0).astype(BF),
        jnp.where((t == 3 * g) & (g < real), 1.0, 0.0).astype(BF),
    ]


def group_masks(groups, count, real):
    g = iota((groups, 1), 0)
    t = iota((1, count), 1)
    return [jnp.where((t == 3 * g + i) & (g < real), 1.0, 0.0).astype(BF) for i in range(3)]


def pool_kernel(real, places, who, middle, own, came, s, x, y, d, full, pool, joined, out):
    k = who[1]
    unpack_pool(who, reader((s, x, y, d), places), 0, pool)
    full[...] = (middle[...] + (own[...].astype(F32) + came[...].astype(F32))).astype(BF)
    part = full[:, lanes(HALF * k, HALF)]
    for j, mask in enumerate(join_masks(who, joined.shape[0], full.shape[0], real)):
        joined[:, HALF * j : HALF * j + HALF] = nn(mask, part).astype(BF)
    out[...] = nn(joined[...], pool[...]).astype(BF)


def expand_back_kernel(real, places, who, own, came, s, x, y, d, target, expand, grouped, out, sems):
    here = who[1] == who[0] >> 1
    for i, (source, taken) in enumerate(((own, here), (came, jnp.logical_not(here)))):

        @pl.when(taken)
        def _():
            copy = pltpu.make_async_copy(source.at[1], target, sems.at[i])
            copy.start()
            copy.wait()

    live = segment_of(who, iota((target.shape[0], 1), 0), 3) < 3
    target[...] = jnp.where(live, target[...].astype(F32), 0.0).astype(BF)
    unpack_expand(who, reader((s, x, y, d), places), THIRD + ATTN, expand)
    for i, mask in enumerate(group_masks(grouped.shape[0], target.shape[0], real)):
        grouped[:, WIDTH * i : WIDTH * i + WIDTH] = nn(mask, target[...]).astype(BF)
    out[...] = nt(grouped[...], expand[...]).astype(BF)


def expand_kernel(real, who, middle, own, came, expand, part, out, short):
    k = who[1]
    short[...] = (middle[...] + (own[...].astype(F32) + came[...].astype(F32))).astype(BF)
    part[...] = short[:, lanes(HALF * k, HALF)]
    grown = nn(part[...], expand[...]).astype(BF)
    total = jnp.zeros(out.shape, F32)
    for i, mask in enumerate(group_masks(part.shape[0], out.shape[0], real)):
        total = total + tn(mask, grown[:, WIDTH * i : WIDTH * i + WIDTH])
    out[...] = total.astype(BF)


def ffn_back(gain_row, delta, middle, gains, slope, widen, narrow, inner, out, gain):
    total = jnp.zeros(middle.shape, F32)
    for i in range(4):
        cols = slice(HALF * i, HALF * i + HALF)
        value = (nt(delta, narrow[cols, :]) * slope[:, cols].astype(F32)).astype(BF)
        inner[:, cols] = value
        total = total + nt(value, widen[:, cols])
    normed, _ = standard(middle[...])
    out[...] = total.astype(BF)
    gain[...] = jnp.broadcast_to(jnp.sum(total * normed, 0, keepdims=True), gain.shape)


def short_ffn_back_kernel(who, own, came, middle, gains, slope, widen, narrow, delta, inner, out, gain):
    k = who[1]
    delta[:, lanes(HALF * k, HALF)] = own[...]
    delta[:, lanes(HALF * (1 - k), HALF)] = came[...]
    ffn_back(3, delta[...], middle, gains, slope, widen, narrow, inner, out, gain)


def full_ffn_back_kernel(
    who, target, own, came, middle, gains, slope, widen, narrow, delta, low, inner, out, gain
):
    k = who[1]
    delta[:, lanes(HALF * k, HALF)] = own[...].astype(F32)
    delta[:, lanes(HALF * (1 - k), HALF)] = came[...].astype(F32)
    delta[...] = delta[...] + target[...].astype(F32)
    low[...] = delta[...].astype(BF)
    ffn_back(1, low[...], middle, gains, slope, widen, narrow, inner, out, gain)


def attention_back_kernel(
    first_row, second_row, block, who, delta, own, came, middle, gains, states, merge, project, q, k, v, att, cos, sin,
    mid, mix, packed, out, gain, dk, dv,
):
    count = middle.shape[0]
    normed, inverse = standard(middle[...])
    dsecond = own[...].astype(F32) + came[...].astype(F32)
    dmid = delta[...].astype(F32) + norm_back(dsecond * gains[second_row : second_row + 1, :], normed, inverse)
    mid[...] = dmid
    low = dmid.astype(BF)
    mix[...] = low
    dctx = nt(low, merge[...]).astype(BF)
    turned, plain = head_masks()
    scale = SIZE**-0.5
    cosine, sine = cos[...], sin[...]
    dk[...] = jnp.zeros(dk.shape, F32)
    dv[...] = jnp.zeros(dv.shape, F32)
    for b in range(count // block):
        start, stop = b * block, (b + 1) * block
        keys, values = k[0:stop, :], v[0:stop, :]
        queries = q[start:stop, :]
        dcontext = dctx[start:stop, :]
        dq = jnp.zeros((block, HALF), F32)
        for h in range(LOCAL):
            dhead = dcontext * plain[h]
            low_attend = att[b, h * block : (h + 1) * block, 0:stop]
            attend = low_attend.astype(F32)
            dattend = nt(dhead, values)
            dscores = attend * (dattend - jnp.sum(attend * dattend, -1, keepdims=True))
            dscores = (dscores * scale).astype(BF)
            dq = dq + nn(dscores, keys * turned[h])
            dk[0:stop, :] += tn(dscores, queries * turned[h])
            dv[0:stop, :] += tn(low_attend, dhead)
        a, c = dq[:, 0:128], dq[:, 128:256]
        packed[start:stop, 0:128] = (a * cosine[start:stop] + c * sine[start:stop]).astype(BF)
        packed[start:stop, 128:256] = (c * cosine[start:stop] - a * sine[start:stop]).astype(BF)
    a, c = dk[:, 0:128], dk[:, 128:256]
    packed[:, 256:384] = (a * cosine + c * sine).astype(BF)
    packed[:, 384:512] = (c * cosine - a * sine).astype(BF)
    packed[:, 512:768] = dv[...].astype(BF)
    dfirst = nn(packed[...], project[...])
    out[...] = dfirst.astype(BF)
    normed_one, _ = standard(states[...].astype(F32))
    gain[...] = jnp.broadcast_to(jnp.sum(dfirst * normed_one, 0, keepdims=True), gain.shape)


def input_gradient(gain_row, mid, own, came, gains, states):
    normed, inverse = standard(states[...].astype(F32))
    dfirst = own[...].astype(F32) + came[...].astype(F32)
    return mid[...] + norm_back(dfirst * gains[gain_row : gain_row + 1, :], normed, inverse)


def pool_back_kernel(real, who, mid, own, came, gains, states, pool, delta, out):
    delta[...] = input_gradient(2, mid, own, came, gains, states).astype(BF)
    djoined = nt(delta[...], pool[...]).astype(BF)
    total = jnp.zeros(out.shape, F32)
    for j, mask in enumerate(join_masks(who, delta.shape[0], out.shape[0], real)):
        total = total + tn(mask, djoined[:, HALF * j : HALF * j + HALF])
    out[...] = total.astype(BF)


def outputs_kernel(who, full, grown, grown_came, mid, own, came, gains, states, o0, o1, o2, o3, whole):
    @pl.when(who[1] == 0)
    def _():
        whole[...] = (full[...].astype(F32) + (grown[...].astype(F32) + grown_came[...].astype(F32))).astype(BF)

    @pl.when(who[1] != 0)
    def _():
        whole[...] = input_gradient(0, mid, own, came, gains, states).astype(BF)

    for q, out in zip(chips(who), (o0, o1, o2, o3)):
        out[...] = whole[0 : out.shape[0], lanes(128 * q)]


def ffn_weights(who, write, hidden, delta, second, inner, gain, dwiden, dnarrow):
    dnarrow[...] = tn(hidden[...], delta[...]).astype(BF)
    dwiden[...] = tn(second[...], inner[...]).astype(BF)
    regroup_gain(who, write, gain)
    regroup_ffn(who, write, PAD, dwiden, dnarrow)


def attn_weights(who, write, ctx, mix, packed, first, gain, dproject, dmerge):
    dproject[...] = tn(packed[...], first[...]).astype(BF)
    dmerge[...] = tn(ctx[...], mix[...]).astype(BF)
    regroup_gain(who, write, gain)
    regroup_attn(who, write, PAD, dproject, dmerge)


def group_a_kernel(who, hidden, delta, second, inner, gain, part, grouped, keep, send, dwiden, dnarrow, dexpand):
    write = writer(keep, send)
    ffn_weights(who, write, hidden, delta, second, inner, gain, dwiden, dnarrow)
    dexpand[...] = tn(part[...], grouped[...]).astype(BF)
    regroup_expand(who, write, PAD + FFN, dexpand)


def group_b_kernel(who, ctx, mix, packed, first, gain, joined, delta, keep, send, dproject, dmerge, dpool):
    write = writer(keep, send)
    attn_weights(who, write, ctx, mix, packed, first, gain, dproject, dmerge)
    dpool[...] = tn(joined[...], delta[...]).astype(BF)
    regroup_pool(who, write, PAD + ATTN, dpool)


def group_c_kernel(who, hidden, delta, second, inner, gain, keep, send, dwiden, dnarrow):
    ffn_weights(who, writer(keep, send), hidden, delta, second, inner, gain, dwiden, dnarrow)


def group_d_kernel(who, ctx, mix, packed, first, gain, keep, send, dproject, dmerge):
    attn_weights(who, writer(keep, send), ctx, mix, packed, first, gain, dproject, dmerge)


class Halves:
    def __init__(self, first, second):
        self.first, self.second, self.half = first, second, first.shape[0]

    def read(self, at, rows):
        stop = at + rows
        if stop <= self.half:
            return self.first[at:stop, :].astype(F32)
        if at >= self.half:
            return self.second[at - self.half : stop - self.half, :].astype(F32)
        parts = (self.first[at : self.half, :], self.second[0 : stop - self.half, :])
        return jnp.concatenate([part.astype(F32) for part in parts], 0)


def both(who, own, came):
    return ((who[1], own.read), (1 - who[1], came.read))


def spread_gain(own, came, gain):
    gain[...] = own.read(0, 8)[0:1] + came.read(0, 8)[0:1]


def spread_ffn(who, own, came, widen, narrow):
    for k, read in both(who, own, came):
        for lc in range(2):
            widen[:, lanes(256 * k + 128 * lc)] = read(PAD + 512 * lc, 512)
        for qq in range(4):
            narrow[rows_at(512 * qq + 256 * k, 256, 256), :] = read(PAD + 1024 + 256 * qq, 256)


def spread_attn(who, own, came, project, merge, turned):
    for k, read in both(who, own, came):
        for j in range(4):
            for p in range(3):
                block = read(PAD + j * 192 + p * 64, 64)
                turned[rows_at(128 * p + 64 * k, 64, 64), 128 * j : 128 * j + 128] = block
        for pair in range(4):
            merge[rows_at(128 * pair + 64 * k, 64, 64), :] = read(PAD + 768 + pair * 64, 64)
    project[...] = jnp.swapaxes(turned[...], 0, 1)


def spread_whole(kernel, who, own, came, *outs):
    half = own.shape[0] // 2
    kernel(who, *[Halves(*[ref.at[pl.ds(half * i, half), :] for i in range(2)]) for ref in (own, came)], *outs)


def spread_either(kernel, who, keep, rest, keep_came, rest_came, *outs):
    @pl.when(who[6] == 0)
    def _():
        kernel(who, Halves(keep, rest), Halves(keep_came, rest_came), *outs)

    @pl.when(who[6] != 0)
    def _():
        kernel(who, Halves(rest, keep), Halves(rest_came, keep_came), *outs)


def spread_a_kernel(who, own, came, gain, widen, narrow, expand):
    spread_gain(own, came, gain)
    spread_ffn(who, own, came, widen, narrow)
    for k, read in both(who, own, came):
        for i in range(6):
            block = read(PAD + FFN + i * 128, 128)
            expand[rows_at(256 * k + 128 * (i % 2), 128, 128), 128 * (i // 2) : 128 * (i // 2) + 128] = block


def spread_b_kernel(who, own, came, gain, project, merge, pool, turned):
    spread_gain(own, came, gain)
    spread_attn(who, own, came, project, merge, turned)
    for k, read in both(who, own, came):
        for i in range(6):
            pool[rows_at(512 * (i // 2) + 256 * k + 128 * (i % 2), 128, 128), :] = read(PAD + ATTN + i * 128, 128)


def spread_c_kernel(who, own, came, gain, widen, narrow):
    spread_gain(own, came, gain)
    spread_ffn(who, own, came, widen, narrow)


def spread_d_kernel(who, own, came, gain, project, merge, turned):
    spread_gain(own, came, gain)
    spread_attn(who, own, came, project, merge, turned)


class Far:
    def __init__(self, array):
        self.array = array


class Raw(Far):
    pass


def call(kernel, name, outs, who, *args, scratch=(), sems=0, space=pltpu.VMEM, limit=VMEM_LIMIT):
    whole = pl.BlockSpec(memory_space=pltpu.VMEM)
    spaces = [pltpu.HBM if isinstance(a, Far) else space for a in args]
    kinds = [pltpu.HBM if isinstance(a, Raw) else space for a in args]
    args = [a.array if isinstance(a, Far) else a for a in args]
    return pl.pallas_call(
        kernel,
        name=name,
        out_shape=[(pltpu.HBM if far else pltpu.VMEM)(shape, dtype) for shape, dtype, *far in outs],
        in_specs=[pl.BlockSpec(memory_space=pltpu.SMEM)] + [pl.BlockSpec(memory_space=kind) for kind in kinds],
        out_specs=[whole] * len(outs),
        scratch_shapes=[pltpu.VMEM(shape, dtype) for shape, dtype in scratch]
        + ([pltpu.SemaphoreType.DMA((sems,))] if sems else []),
        compiler_params=pltpu.CompilerParams(vmem_limit_bytes=limit),
        cost_estimate=pl.CostEstimate(flops=1024, bytes_accessed=1024, transcendentals=0),
    )(who, *[pltpu.with_memory_space_constraint(a, place) for a, place in zip(args, spaces)])


def swap(value, role):
    count = lax.axis_size("dp")
    route = []
    for chip in range(lax.axis_size("section")):
        for d in range(count):
            distance = (0, 1 + d % 2, 2 - d % 2, 3)[role]
            route.append((chip * count + d, (chip ^ distance) * count + d))
    return lax.ppermute(value, ("section", "dp"), route)


def across(value):
    return lax.ppermute(value, "dp", [(i, i ^ 1) for i in range(lax.axis_size("dp"))])


class Order:
    def __init__(self):
        self.last = None

    def tie(self, value, *others):
        others = [o for o in (self.last, *others) if o is not None]
        return lax.optimization_barrier((value, others))[0] if others else value

    def wait(self, *values):
        self.last = lax.optimization_barrier((self.last, values))[0]

    def call(self, kernel, name, outs, who, *args, **options):
        results = call(kernel, name, outs, self.tie(who), *args, **options)
        self.last = results[-1]
        return results

    def add(self, first, *others):
        total = self.tie(first)
        for other in others:
            total = total + other
        self.last = total
        return total


class Stage:
    def __init__(self, pieces):
        self.pieces = [pieces]

    def start(self, order):
        own = order.tie(self.pieces[0])
        self.pieces += [swap(own, 1), swap(own, 2)]

    def relay(self, order):
        self.pieces.append(swap(order.tie(self.pieces[1]), 2))

    def all(self):
        return [Far(array) for array in self.pieces]

    def places(self):
        return (0,) * 4


class Sum:
    def __init__(self, order, group):
        self.order = order
        self.keep, self.send = group

    def first(self):
        self.came = swap(self.order.tie(self.send), 1)

    def second(self):
        self.last = swap(self.order.add(self.came[1], self.keep[1]), 2)

    def across_rows(self, value, distance):
        route = [(i, i ^ (2 * distance)) for i in range(lax.axis_size("dp"))]
        return lax.ppermute(value, "dp", route)

    def third(self):
        total = self.order.add(self.last, self.came[0], self.keep[0])
        count = lax.axis_size("dp")
        self.short = count == 8
        if self.short:
            half = total.shape[0] // 2
            odd = (lax.axis_index("dp") // 2) % 2 == 1
            self.keep = jnp.where(odd, total[half:], total[:half])
            self.came = self.across_rows(jnp.where(odd, total[:half], total[half:]), 1)
        else:
            groups = [[i for i in range(count) if i % 2 == core] for core in range(2)]
            self.keep = lax.psum(total, "dp", axis_index_groups=groups)

    def fourth(self):
        if self.short:
            self.keep = self.order.add(self.came, self.keep)
            self.came = self.across_rows(self.keep, 2)

    def fifth(self):
        if self.short:
            self.keep = self.order.add(self.came, self.keep)
            self.rest = self.across_rows(self.keep, 1)
            self.keep_came = across(self.keep)

    def sixth(self):
        if self.short:
            self.rest = self.order.tie(self.rest)
            self.rest_came = across(self.rest)
        else:
            self.keep = self.order.tie(self.keep)
            self.keep_came = across(self.keep)

    def all(self):
        if self.short:
            return self.keep, self.rest, self.keep_came, self.rest_came
        return self.keep, self.keep_came


class Delivery:
    def __init__(self, order, pieces, c, k):
        self.order, self.c, self.k = order, c, k
        pieces = order.tie(pieces)
        self.came = [pieces[0]] + [swap(pieces[r], r) for r in range(1, 4)]

    def row(self, chip):
        far, came = self.c ^ chip, self.came
        first = far == 1 + self.k
        return jnp.where(far == 0, came[0], jnp.where(first, came[1], jnp.where(far == 3, came[3], came[2])))

    def turn(self):
        k = self.k
        self.came = self.order.tie(self.came)
        self.own = jnp.concatenate([self.row(2 * k), self.row(2 * k + 1)], 0)
        other = jnp.concatenate([self.row(2 - 2 * k), self.row(3 - 2 * k)], 0)
        self.order.last = other
        self.other = across(other)

    def finish(self):
        own, other = self.own, self.order.tie(self.other)
        results = jnp.where(self.k == 0, own, other), jnp.where(self.k == 0, other, own)
        self.order.last = results[0]
        return results


def angles(places):
    freq = 10000.0 ** (-2.0 * jnp.arange(SIZE // 2, dtype=F32) / SIZE)
    phase = places.astype(F32)[:, None] * jnp.tile(freq, LOCAL)[None, :]
    return jnp.cos(phase), jnp.sin(phase)


def places_of(counts, count, unit):
    at = jnp.arange(count, dtype=jnp.int32)
    starts = unit * jnp.sum(jnp.where(jnp.arange(3)[:, None] >= jnp.arange(3)[None, :], counts[None, :3], 0), 1)
    begin = jnp.max(jnp.where(at[:, None] >= starts[None, :], starts[None, :], 0), 1)
    return at - begin


def body(
    tokens,
    lengths,
    cotangent,
    full_first_gain,
    full_project,
    full_merge,
    full_second_gain,
    full_widen,
    full_narrow,
    pool_weight,
    short_first_gain,
    short_project,
    short_merge,
    short_second_gain,
    short_widen,
    short_narrow,
    expand_weight,
):
    c = lax.axis_index("section")
    d = lax.axis_index("dp")
    k = d % 2
    rows = lengths.shape[0]
    length = tokens.shape[0] // rows
    groups = length // 3
    count = -(-length // QUARTER) * QUARTER
    short = -(-groups // 16) * 16

    here = k == c // 2
    who_k = jnp.stack([c, k]).astype(jnp.int32)
    order = Order()
    gain_rows = jnp.stack([full_first_gain, full_second_gain, short_first_gain, short_second_gain])
    gain_rows = jnp.pad(gain_rows, ((0, PAD - 4), (0, 0)))
    attn_in = [((WIDTH, 3 * QUARTER), BF), ((WIDTH, QUARTER), BF), ((3 * QUARTER, WIDTH), BF)]
    pieces1, = order.call(
        pack_first_kernel, "pack_first", [((PAD + ATTN, QUARTER), BF)], who_k, full_project, full_merge, gain_rows,
        scratch=attn_in, sems=3, space=pltpu.HBM, limit=PACK_LIMIT,
    )
    stage1 = [Far(pieces1)] + [Far(swap(pieces1, r)) for r in (1, 2, 3)]

    j = order.tie(c % 2)
    pairs = jnp.stack([lax.dynamic_index_in_dim(a.reshape(rows, length, WIDTH), j, 0, False) for a in (tokens, cotangent)])
    ends = lax.dynamic_index_in_dim(lengths, j, 0, False).astype(BF)
    ends = jnp.pad(ends, (0, WIDTH - ends.shape[0]))
    own_row = jnp.concatenate([pairs, jnp.broadcast_to(ends, (2, count - length, WIDTH))], 1)
    came_row = across(own_row)

    pieces2, pieces3, pieces4 = order.call(
        pack_rest_kernel, "pack_rest", [((n, QUARTER), BF) for n in (FFN, THIRD + ATTN + THIRD, FFN)],
        who_k, full_widen, full_narrow, pool_weight, short_project, short_merge, expand_weight, short_widen,
        short_narrow, scratch=attn_in, sems=26, space=pltpu.HBM, limit=PACK_LIMIT,
    )
    stage2, stage3, stage4 = (Stage(p) for p in (pieces2, pieces3, pieces4))
    stage2.start(order)
    stage3.start(order)

    counts = jnp.where(here, own_row[0, length, :SEGS], came_row[0, length, :SEGS]).astype(jnp.int32)
    odd = (d // 2) % 2 if lax.axis_size("dp") == 8 else jnp.zeros_like(d)
    who = jnp.concatenate([who_k, counts, jnp.stack([odd, odd]).astype(jnp.int32)])
    cos, sin = angles(places_of(counts, count, 3))
    short_cos, short_sin = angles(places_of(counts, short, 1))

    def block_outs(n):
        outs = [
            ((3 * HALF, WIDTH), BF, Far),
            ((HALF, WIDTH), BF, Far),
            ((n, WIDTH), BF, Far),
            ((n, HALF), BF, Far),
            ((n, HALF), BF, Far),
            ((n, HALF), BF, Far),
        ]
        return outs if n == count else [out[:2] for out in outs]

    def ffn_outs(n):
        outs = [
            ((n, WIDTH), F32, Far),
            ((n, WIDTH), BF, Far),
            ((WIDTH, HIDDEN), BF, Far),
            ((HIDDEN, WIDTH), BF, Far),
            ((n, HIDDEN), BF, Far),
            ((n, HIDDEN), BF, Far),
            ((n, WIDTH), BF),
        ]
        return outs if n == count else [out[:2] for out in outs]

    def back_outs(n):
        return [
            ((n, WIDTH), F32),
            ((n, WIDTH), BF),
            ((n, 3 * HALF), BF),
            ((n, WIDTH), BF),
            ((PAD, WIDTH), F32),
        ]

    def sent(part):
        return [((2, part, QUARTER), BF, Far)] * 2

    row, gains, project, merge, first, q, key, v, att, ctx, mix = order.call(
        full_attention_kernel, "full_attention",
        [((count, WIDTH), BF), ((PAD, WIDTH), F32)] + block_outs(count)
        + [((count // QUARTER, LOCAL * QUARTER, count), BF, Far), ((count, HALF), BF, Far), ((count, WIDTH), BF)],
        who, Raw(own_row), Raw(came_row), cos, sin, *stage1, sems=2,
    )
    mix_came = across(mix)
    stage2.relay(order)
    stage3.relay(order)
    stage4.start(order)
    middle, second, widen, narrow, hidden, slope, part = order.call(
        functools.partial(ffn_kernel, 1, stage2.places()), "full_ffn", ffn_outs(count),
        who, row, mix, mix_came, gains, *stage2.all(),
    )
    part_came = across(part)
    full, pool, joined, pooled = order.call(
        functools.partial(pool_kernel, groups, stage3.places()), "pool",
        [((count, WIDTH), BF, Far), ((3 * HALF, WIDTH), BF, Far), ((short, 3 * HALF), BF, Far), ((short, WIDTH), BF)],
        who, Far(middle), part, part_came, *stage3.all(),
    )
    s_in, s_project, s_merge, s_first, s_q, s_key, s_v, s_att, s_ctx, s_mix = order.call(
        functools.partial(short_attention_kernel, stage3.places()), "short_attention",
        [((short, WIDTH), BF)] + block_outs(short)
        + [((1, LOCAL * short, short), BF), ((short, HALF), BF), ((short, WIDTH), BF)],
        who, pooled, across(pooled), short_cos, short_sin, gains, *stage3.all(),
    )
    s_mix_came = across(s_mix)
    stage4.relay(order)
    target, expand, grouped, d_half = order.call(
        functools.partial(expand_back_kernel, groups, stage3.places()), "expand_back",
        [((count, WIDTH), BF, Far), ((HALF, 3 * WIDTH), BF), ((short, 3 * WIDTH), BF), ((short, HALF), BF)],
        who, Raw(own_row), Raw(came_row), *stage3.all(), sems=2,
    )
    d_came = across(d_half)
    s_middle, s_second, s_widen, s_narrow, s_hidden, s_slope, s_part = order.call(
        functools.partial(ffn_kernel, 3, stage4.places()), "short_ffn", ffn_outs(short),
        who, s_in, s_mix, s_mix_came, gains, *stage4.all(),
    )
    s_part_came = across(s_part)

    s_delta, s_inner, s_dsecond, s_gain2 = order.call(
        short_ffn_back_kernel, "short_ffn_back",
        [((short, WIDTH), BF), ((short, HIDDEN), BF), ((short, WIDTH), BF), ((PAD, WIDTH), F32)],
        who, d_half, d_came, s_middle, gains, s_slope, s_widen, s_narrow,
    )
    s_dsecond_came = across(s_dsecond)
    s_half, grown = order.call(
        functools.partial(expand_kernel, groups), "expand", [((short, HALF), BF), ((count, WIDTH), BF, Far)],
        who, s_middle, s_part, s_part_came, expand, scratch=[((short, WIDTH), BF)],
    )
    grown_came = across(grown)
    sum_a = Sum(order, order.call(
        group_a_kernel, "group_a", sent(PAD + FFN + THIRD),
        who, s_hidden, s_delta, s_second, s_inner, s_gain2, s_half, grouped,
        scratch=[((WIDTH, HIDDEN), BF), ((HIDDEN, WIDTH), BF), ((HALF, 3 * WIDTH), BF)],
    ))
    sum_a.first()
    s_mid, s_dmix, s_dpacked, s_dfirst, s_gain1 = order.call(
        functools.partial(attention_back_kernel, 2, 3, short), "short_attention_back", back_outs(short),
        who, s_delta, s_dsecond, s_dsecond_came, s_middle, gains, s_in, s_merge, s_project, s_q, s_key, s_v, s_att,
        short_cos, short_sin, scratch=[((short, HALF), F32)] * 2,
    )
    d_in, d_low = order.call(
        functools.partial(pool_back_kernel, groups), "pool_back", [((short, WIDTH), BF), ((count, HALF), BF)],
        who, s_mid, s_dfirst, across(s_dfirst), gains, s_in, Far(pool),
    )
    d_low_came = across(d_low)
    order.wait(grown_came)
    sum_b = Sum(order, order.call(
        group_b_kernel, "group_b", sent(PAD + ATTN + THIRD),
        who, s_ctx, s_dmix, s_dpacked, s_first, s_gain1, Far(joined), d_in,
        scratch=[((3 * HALF, WIDTH), BF), ((HALF, WIDTH), BF), ((3 * HALF, WIDTH), BF)],
    ))
    sum_b.first()
    delta, low, inner, dsecond, gain2 = order.call(
        full_ffn_back_kernel, "full_ffn_back",
        [((count, WIDTH), F32), ((count, WIDTH), BF), ((count, HIDDEN), BF), ((count, WIDTH), BF), ((PAD, WIDTH), F32)],
        who, Far(target), d_low, d_low_came, Far(middle), gains, Far(slope), Far(widen), Far(narrow),
    )
    dsecond_came = across(dsecond)
    sum_a.second()
    sum_c = Sum(order, order.call(
        group_c_kernel, "group_c", sent(PAD + FFN), who, Far(hidden), low, Far(second), inner, gain2,
        scratch=[((WIDTH, HIDDEN), BF), ((HIDDEN, WIDTH), BF)],
    ))
    mid, dmix, dpacked, dfirst, gain1 = order.call(
        functools.partial(attention_back_kernel, 0, 1, QUARTER), "full_attention_back", back_outs(count),
        who, delta, dsecond, dsecond_came, Far(middle), gains, row, Far(merge), Far(project), Far(q), Far(key), Far(v),
        Far(att), cos, sin, scratch=[((count, HALF), F32)] * 2,
    )
    dfirst_came = across(dfirst)
    sum_b.second()
    sum_c.first()
    sum_d = Sum(order, order.call(
        group_d_kernel, "group_d", sent(PAD + ATTN), who, Far(ctx), dmix, dpacked, Far(first), gain1,
        scratch=[((3 * HALF, WIDTH), BF), ((HALF, WIDTH), BF)],
    ))
    sent_rows = order.call(
        outputs_kernel, "outputs", [((length, QUARTER), BF)] * 4,
        who, Far(full), Far(grown), grown_came, mid, dfirst, dfirst_came, gains, row, scratch=[((count, WIDTH), BF)],
    )

    gain_out = ((1, QUARTER), F32)
    ffn_out = [((WIDTH, WIDTH), F32), ((4 * WIDTH, QUARTER), F32)]
    attn_out = [((WIDTH, 3 * QUARTER), F32), ((WIDTH, QUARTER), F32)]
    turned = [((3 * QUARTER, WIDTH), F32)]

    def spread(kernel, name, outs, total, **options):
        outs = [(*out, Far) for out in outs]
        how = spread_either if total.short else spread_whole
        return order.call(functools.partial(how, kernel), name, outs, who, *total.all(), **options)

    sum_a.third()
    sum_b.third()
    sum_d.first()
    sum_a.fourth()
    sum_c.second()
    sum_b.fourth()
    sum_d.second()
    sum_c.third()
    sum_d.third()
    sum_a.fifth()
    delivery = Delivery(order, sent_rows, c, k)
    sum_c.fourth()
    sum_d.fourth()
    sum_b.fifth()
    delivery.turn()
    sum_a.sixth()
    sum_b.sixth()
    sum_c.fifth()
    g_s2, g_s_widen, g_s_narrow, g_expand = spread(
        spread_a_kernel, "spread_a", [gain_out] + ffn_out + [((WIDTH, 3 * QUARTER), F32)], sum_a
    )
    sum_d.fifth()
    g_s1, g_s_project, g_s_merge, g_pool = spread(
        spread_b_kernel, "spread_b", [gain_out] + attn_out + [((3 * WIDTH, QUARTER), F32)], sum_b, scratch=turned
    )
    mixed_out, token_gradient = delivery.finish()
    sum_c.sixth()
    sum_d.sixth()
    g_f2, g_widen, g_narrow = spread(spread_c_kernel, "spread_c", [gain_out] + ffn_out, sum_c)
    g_f1, g_project, g_merge = spread(spread_d_kernel, "spread_d", [gain_out] + attn_out, sum_d, scratch=turned)

    return (
        mixed_out,
        token_gradient,
        g_f1.reshape(-1),
        g_project,
        g_merge,
        g_f2.reshape(-1),
        g_widen,
        g_narrow,
        g_pool,
        g_s1.reshape(-1),
        g_s_project,
        g_s_merge,
        g_s2.reshape(-1),
        g_s_widen,
        g_s_narrow,
        g_expand,
    )


def solution(mesh):
    in_specs = (
        P("dp", None),
        P("dp", None),
        P("dp", None),
        P("section"),
        P(None, "section"),
        P(None, "section"),
        P("section"),
        P(None, "section"),
        P(None, "section"),
        P(None, "section"),
        P("section"),
        P(None, "section"),
        P(None, "section"),
        P("section"),
        P(None, "section"),
        P(None, "section"),
        P(None, "section"),
    )
    out_specs = (
        P("dp", "section"),
        P("dp", "section"),
        P("section"),
        P(None, "section"),
        P(None, "section"),
        P("section"),
        P(None, "section"),
        P(None, "section"),
        P(None, "section"),
        P("section"),
        P(None, "section"),
        P(None, "section"),
        P("section"),
        P(None, "section"),
        P(None, "section"),
        P(None, "section"),
    )
    return jax.shard_map(body, mesh=mesh, in_specs=in_specs, out_specs=out_specs, check_vma=False)
```

```python
import functools

import jax
import jax.numpy as jnp
from jax import lax
from jax.experimental import pallas as pl
from jax.experimental.pallas import tpu as pltpu
from jax.sharding import PartitionSpec as P


WIDTH = 512
QUARTER = 128
HALF = 256
HIDDEN = 1024
SEGS = 4
LOCAL = 4
SIZE = 64
EPS = 1e-05
NEG = -1e30

BF = jnp.bfloat16
F32 = jnp.float32

ATTN = 1024
FFN = 2048
THIRD = 768
PAD = 32
VMEM_LIMIT = 16 * 2**20
PACK_LIMIT = 60 * 2**20


def nn(left, right):
    return lax.dot_general(left, right, (((1,), (0,)), ((), ())), preferred_element_type=F32)


def nt(left, right):
    return lax.dot_general(left, right, (((1,), (1,)), ((), ())), preferred_element_type=F32)


def tn(left, right):
    return lax.dot_general(left, right, (((0,), (0,)), ((), ())), preferred_element_type=F32)


def lanes(start, count=QUARTER):
    return pl.ds(pl.multiple_of(start, QUARTER), count)


def rows_at(start, count, unit):
    return pl.ds(pl.multiple_of(start, unit), count)


def iota(shape, dim):
    return lax.broadcasted_iota(jnp.int32, shape, dim)


def standard(states):
    center = states - jnp.mean(states, -1, keepdims=True)
    inverse = lax.rsqrt(jnp.mean(center * center, -1, keepdims=True) + EPS)
    return center * inverse, inverse


def norm_back(delta, normed, inverse):
    return inverse * (
        delta
        - jnp.mean(delta, -1, keepdims=True)
        - normed * jnp.mean(delta * normed, -1, keepdims=True)
    )


def gelu_parts(x):
    z = x * 0.7071067811865476
    t = 1.0 / (1.0 + 0.3275911 * jnp.abs(z))
    e = jnp.exp(-z * z)
    poly = t * (
        0.127414796
        + t * (-0.142248368 + t * (0.7107068705 + t * (-0.7265760135 + t * 0.5307027145)))
    )
    tail = poly * e
    phi = jnp.where(z >= 0, 1.0 - tail, tail)
    return x * phi, phi + x * e * 0.3989422804014327


def chips(who):
    c, k = who[0], who[1]
    return c, c ^ (1 + k), c ^ (2 - k), c ^ 3


def reader(refs, places):
    def read(r, at, rows):
        return refs[r][places[r] + at : places[r] + at + rows, :]

    return read


def writer(keep, pass_on, send):
    def write(r, at, value):
        if r % 2 == 0:
            (keep, pass_on)[r // 2][at : at + value.shape[0], :] = value
        else:
            send[r // 2, at : at + value.shape[0], :] = value

    return write


def pair_rows(pair):
    is_value = pair >= 8
    first = jnp.where(is_value, 512 + 64 * (pair - 8), 256 * (pair >> 2) + 32 * (pair & 3))
    second = jnp.where(is_value, first + 32, first + 128)
    return first, second


def pack_attn(k, turned, merge, put, base):
    for p in range(3):
        chunk = turned[rows_at(128 * p + 64 * k, 64, 64), :]
        for j in range(4):
            put(base + j * 192 + p * 64, chunk[:, 128 * j : 128 * j + 128])
    for pair in range(4):
        put(base + 768 + pair * 64, merge[rows_at(128 * pair + 64 * k, 64, 64), :])


def unpack_attn(who, read, base, project, merge):
    for r, q in enumerate(chips(who)):
        for p in range(3):
            first, second = pair_rows(3 * q + p)
            for j in range(4):
                block = read(r, base + j * 192 + p * 64, 64)
                project[rows_at(first, 32, 32), 128 * j : 128 * j + 128] = block[:32]
                project[rows_at(second, 32, 32), 128 * j : 128 * j + 128] = block[32:]
        for pair in range(4):
            merge[64 * pair : 64 * pair + 64, lanes(128 * q)] = read(r, base + 768 + pair * 64, 64)


def regroup_attn(who, write, base, project, merge):
    for r, q in enumerate(chips(who)):
        for p in range(3):
            first, second = pair_rows(3 * q + p)
            for j in range(4):
                at = base + j * 192 + p * 64
                write(r, at, project[rows_at(first, 32, 32), 128 * j : 128 * j + 128])
                write(r, at + 32, project[rows_at(second, 32, 32), 128 * j : 128 * j + 128])
        for pair in range(4):
            write(r, base + 768 + pair * 64, merge[64 * pair : 64 * pair + 64, lanes(128 * q)])


def pack_ffn(k, widen, narrow, put):
    for lc in range(2):
        put(512 * lc, widen.at[:, lanes(256 * k + 128 * lc)])
    for qq in range(4):
        put(1024 + 256 * qq, narrow.at[rows_at(512 * qq + 256 * k, 256, 256), :])


def unpack_ffn(who, read, widen, narrow):
    for r, q in enumerate(chips(who)):
        for lc in range(2):
            widen[:, lanes(256 * q + 128 * lc)] = read(r, 512 * lc, 512)
        narrow[:, lanes(128 * q)] = read(r, 1024, 1024)


def regroup_ffn(who, write, base, widen, narrow):
    for r, q in enumerate(chips(who)):
        for lc in range(2):
            write(r, base + 512 * lc, widen[:, lanes(256 * q + 128 * lc)])
        write(r, base + 1024, narrow[:, lanes(128 * q)])


def pack_pool(k, pool, put, base):
    for i in range(6):
        put(base + i * 128, pool.at[rows_at(512 * (i // 2) + 256 * k + 128 * (i % 2), 128, 128), :])


def unpack_pool(who, read, base, pool):
    for r, q in enumerate(chips(who)):
        for i in range(6):
            pool[128 * i : 128 * i + 128, lanes(128 * q)] = read(r, base + i * 128, 128)


def regroup_pool(who, write, base, pool):
    for r, q in enumerate(chips(who)):
        for i in range(6):
            write(r, base + i * 128, pool[128 * i : 128 * i + 128, lanes(128 * q)])


def pack_expand(k, expand, put, base):
    for i in range(6):
        put(base + i * 128, expand.at[rows_at(256 * k + 128 * (i % 2), 128, 128), pl.ds(128 * (i // 2), 128)])


def unpack_expand(who, read, base, expand):
    for r, q in enumerate(chips(who)):
        for i in range(6):
            block = read(r, base + i * 128, 128)
            expand[128 * (i % 2) : 128 * (i % 2) + 128, lanes(384 * q + 128 * (i // 2))] = block


def regroup_expand(who, write, base, expand):
    for r, q in enumerate(chips(who)):
        for i in range(6):
            block = expand[128 * (i % 2) : 128 * (i % 2) + 128, lanes(384 * q + 128 * (i // 2))]
            write(r, base + i * 128, block)


def regroup_gain(who, write, gain):
    for r, q in enumerate(chips(who)):
        write(r, 0, gain[:, lanes(128 * q)].astype(BF))


class Copies:
    def __init__(self, sems):
        self.sems, self.all = sems, []

    def start(self, source, target):
        copy = pltpu.make_async_copy(source, target, self.sems.at[len(self.all)])
        copy.start()
        self.all.append(copy)

    def putter(self, ref):
        def put(at, source):
            self.start(source, ref.at[pl.ds(at, source.shape[0]), :])

        return put

    def wait(self):
        for copy in self.all:
            copy.wait()


def putter(ref):
    def put(at, value):
        ref[at : at + value.shape[0], :] = value

    return put


def core():
    return lax.rem(lax.axis_index("dp"), 2)


def pack_first_kernel(project, merge, g0, g1, g2, g3, out, project_in, merge_in, turned, i0, i1, i2, i3, sems):
    copies = Copies(sems)
    copies.start(project, project_in)
    copies.start(merge, merge_in)
    inside = (i0, i1, i2, i3)
    for gain, place in zip((g0, g1, g2, g3), inside):
        copies.start(gain, place)
    copies.wait()
    row = iota((PAD, QUARTER), 0)
    gains = jnp.zeros((PAD, QUARTER), F32)
    for i, place in enumerate(inside):
        gains = jnp.where(row == i, place[...].astype(F32), gains)
    out[0:PAD, :] = gains.astype(BF)
    turned[...] = jnp.swapaxes(project_in[...], 0, 1)
    pack_attn(core(), turned, merge_in, putter(out), PAD)


def pack_rest_kernel(
    widen, narrow, pool, project, merge, expand, s_widen, s_narrow, out2, out3, out4, project_in, merge_in, turned, sems
):
    k = core()
    copies, last = Copies(sems), Copies(sems.at[pl.ds(2, 24)])
    copies.start(project, project_in)
    copies.start(merge, merge_in)
    pack_ffn(k, widen, narrow, last.putter(out2))
    pack_pool(k, pool, last.putter(out3), 0)
    pack_expand(k, expand, last.putter(out3), THIRD + ATTN)
    pack_ffn(k, s_widen, s_narrow, last.putter(out4))
    copies.wait()
    turned[...] = jnp.swapaxes(project_in[...], 0, 1)
    pack_attn(k, turned, merge_in, putter(out3), THIRD)
    last.wait()


def ends_of(who):
    e0 = who[2]
    e1 = e0 + who[3]
    e2 = e1 + who[4]
    return e0, e1, e2, e2 + who[5]


def segment_of(who, index, unit):
    return sum((index >= unit * end).astype(jnp.int32) for end in ends_of(who))


def head_masks():
    lane = iota((1, HALF), 1)
    turned = [((lane & 127) >> 5 == h).astype(F32).astype(BF) for h in range(LOCAL)]
    plain = [((lane >> 6) == h).astype(F32).astype(BF) for h in range(LOCAL)]
    return turned, plain


def attention_forward(who, states, gain, cos, sin, project, merge, first, q, k, v, att, ctx, mix, unit, block):
    count = states.shape[0]
    normed, _ = standard(states)
    start = (normed * gain).astype(BF)
    first[...] = start
    packed = nt(start, project[...])
    cosine, sine = cos[...], sin[...]
    for ref, at in ((q, 0), (k, 256)):
        a, b = packed[:, at : at + 128], packed[:, at + 128 : at + 256]
        ref[:, 0:128] = (a * cosine - b * sine).astype(BF)
        ref[:, 128:256] = (b * cosine + a * sine).astype(BF)
    v[...] = packed[:, 512:768].astype(BF)
    turned, plain = head_masks()
    scale = jnp.asarray(SIZE**-0.5, BF)
    for b in range(count // block):
        low, stop = b * block, (b + 1) * block
        at_row = low + iota((block, 1), 0)
        at_col = iota((1, stop), 1)
        allowed = (segment_of(who, at_row, unit) == segment_of(who, at_col, unit)) & (at_row >= at_col)
        queries = q[low:stop, :] * scale
        keys, values = k[0:stop, :], v[0:stop, :]
        total_context = jnp.zeros((block, HALF), F32)
        for h in range(LOCAL):
            scores = jnp.where(allowed, nt(queries * turned[h], keys), NEG)
            powered = jnp.exp(scores - jnp.max(scores, -1, keepdims=True))
            attend = (powered * (1.0 / jnp.sum(powered, -1, keepdims=True))).astype(BF)
            att[b, h * block : (h + 1) * block, 0:stop] = attend
            total_context = total_context + nn(attend, values * plain[h])
        ctx[low:stop, :] = total_context.astype(BF)
    mix[...] = nn(ctx[...], merge[...]).astype(BF)


def full_attention_kernel(
    who, own, came, cos, sin, s, x, y, d, row, gains, project, merge, first, q, k, v, att, ctx, mix, sems
):
    c = who[0]
    here = who[1] == c >> 1
    for i, (source, taken) in enumerate(((own, here), (came, jnp.logical_not(here)))):

        @pl.when(taken)
        def _():
            copy = pltpu.make_async_copy(source.at[0], row, sems.at[i])
            copy.start()
            copy.wait()

    read = reader((s, x, y, d), (0,) * 4)
    for r, chip in enumerate(chips(who)):
        gains[:, lanes(128 * chip)] = read(r, 0, PAD).astype(F32)
    unpack_attn(who, read, PAD, project, merge)
    states = row[...].astype(F32)
    attention_forward(
        who, states, gains[0:1, :], cos, sin, project, merge, first, q, k, v, att, ctx, mix, 3, QUARTER
    )


def short_attention_kernel(
    places, who, own, came, cos, sin, gains, s, x, y, d, states, project, merge, first, q, k, v, att, ctx, mix
):
    unpack_attn(who, reader((s, x, y, d), places), THIRD, project, merge)
    states[...] = (own[...].astype(F32) + came[...].astype(F32)).astype(BF)
    attention_forward(
        who, states[...].astype(F32), gains[2:3, :], cos, sin, project, merge, first, q, k, v, att, ctx, mix,
        1, own.shape[0],
    )


def ffn_kernel(
    gain_row, places, who, states, own, came, gains, s, x, y, d, middle, second, widen, narrow, hidden, slope, out
):
    unpack_ffn(who, reader((s, x, y, d), places), widen, narrow)
    mid = states[...].astype(F32) + (own[...].astype(F32) + came[...].astype(F32))
    middle[...] = mid
    normed, _ = standard(mid)
    start = (normed * gains[gain_row : gain_row + 1, :]).astype(BF)
    second[...] = start

    @pl.loop(0, 4)
    def _(i):
        cols = lanes(HALF * i, HALF)
        value, back = gelu_parts(nn(second[...], widen[:, cols]))
        hidden[:, cols] = value.astype(BF)
        slope[:, cols] = back.astype(BF)

    out[...] = nn(hidden[...], narrow[...]).astype(BF)


def join_masks(who, groups, count, real):
    g = iota((groups, 1), 0)
    t = iota((1, count), 1)
    ends = ends_of(who)
    keep = (g != ends[0]) & (g != ends[1]) & (g != ends[2]) & (g < real)
    return [
        jnp.where((t == 3 * g - 2) & keep, 1.0, 0.0).astype(BF),
        jnp.where((t == 3 * g - 1) & keep, 1.0, 0.0).astype(BF),
        jnp.where((t == 3 * g) & (g < real), 1.0, 0.0).astype(BF),
    ]


def group_masks(groups, count, real):
    g = iota((groups, 1), 0)
    t = iota((1, count), 1)
    return [jnp.where((t == 3 * g + i) & (g < real), 1.0, 0.0).astype(BF) for i in range(3)]


def pool_kernel(real, places, who, middle, own, came, s, x, y, d, full, pool, joined, out):
    k = who[1]
    unpack_pool(who, reader((s, x, y, d), places), 0, pool)
    full[...] = (middle[...] + (own[...].astype(F32) + came[...].astype(F32))).astype(BF)
    part = full[:, lanes(HALF * k, HALF)]
    for j, mask in enumerate(join_masks(who, joined.shape[0], full.shape[0], real)):
        joined[:, HALF * j : HALF * j + HALF] = nn(mask, part).astype(BF)
    out[...] = nn(joined[...], pool[...]).astype(BF)


def expand_back_kernel(real, places, who, own, came, s, x, y, d, target, expand, grouped, out, sems):
    here = who[1] == who[0] >> 1
    for i, (source, taken) in enumerate(((own, here), (came, jnp.logical_not(here)))):

        @pl.when(taken)
        def _():
            copy = pltpu.make_async_copy(source.at[1], target, sems.at[i])
            copy.start()
            copy.wait()

    live = segment_of(who, iota((target.shape[0], 1), 0), 3) < 3
    target[...] = jnp.where(live, target[...].astype(F32), 0.0).astype(BF)
    unpack_expand(who, reader((s, x, y, d), places), THIRD + ATTN, expand)
    for i, mask in enumerate(group_masks(grouped.shape[0], target.shape[0], real)):
        grouped[:, WIDTH * i : WIDTH * i + WIDTH] = nn(mask, target[...]).astype(BF)
    out[...] = nt(grouped[...], expand[...]).astype(BF)


def expand_kernel(real, who, middle, own, came, expand, part, out, short):
    k = who[1]
    short[...] = (middle[...] + (own[...].astype(F32) + came[...].astype(F32))).astype(BF)
    part[...] = short[:, lanes(HALF * k, HALF)]
    grown = nn(part[...], expand[...]).astype(BF)
    total = jnp.zeros(out.shape, F32)
    for i, mask in enumerate(group_masks(part.shape[0], out.shape[0], real)):
        total = total + tn(mask, grown[:, WIDTH * i : WIDTH * i + WIDTH])
    out[...] = total.astype(BF)


def ffn_back(gain_row, delta, middle, gains, slope, widen, narrow, inner, out, gain):
    total = jnp.zeros(middle.shape, F32)
    for i in range(4):
        cols = slice(HALF * i, HALF * i + HALF)
        value = (nt(delta, narrow[cols, :]) * slope[:, cols].astype(F32)).astype(BF)
        inner[:, cols] = value
        total = total + nt(value, widen[:, cols])
    normed, _ = standard(middle[...])
    out[...] = total.astype(BF)
    gain[...] = jnp.broadcast_to(jnp.sum(total * normed, 0, keepdims=True), gain.shape)


def full_ffn_back_kernel(
    who, target, own, came, middle, gains, slope, widen, narrow, delta, low, inner, out, gain
):
    k = who[1]
    delta[:, lanes(HALF * k, HALF)] = own[...].astype(F32)
    delta[:, lanes(HALF * (1 - k), HALF)] = came[...].astype(F32)
    delta[...] = delta[...] + target[...].astype(F32)
    low[...] = delta[...].astype(BF)
    ffn_back(1, low[...], middle, gains, slope, widen, narrow, inner, out, gain)


def attention_back_kernel(
    first_row, second_row, block, who, delta, own, came, middle, gains, states, merge, project, q, k, v, att, cos, sin,
    mid, mix, packed, out, gain, dk, dv,
):
    count = middle.shape[0]
    normed, inverse = standard(middle[...])
    dsecond = own[...].astype(F32) + came[...].astype(F32)
    dmid = delta[...].astype(F32) + norm_back(dsecond * gains[second_row : second_row + 1, :], normed, inverse)
    mid[...] = dmid
    low = dmid.astype(BF)
    mix[...] = low
    dctx = nt(low, merge[...]).astype(BF)
    turned, plain = head_masks()
    scale = SIZE**-0.5
    cosine, sine = cos[...], sin[...]
    dk[...] = jnp.zeros(dk.shape, F32)
    dv[...] = jnp.zeros(dv.shape, F32)
    for b in range(count // block):
        start, stop = b * block, (b + 1) * block
        keys, values = k[0:stop, :], v[0:stop, :]
        queries = q[start:stop, :]
        dcontext = dctx[start:stop, :]
        dq = jnp.zeros((block, HALF), F32)
        for h in range(LOCAL):
            dhead = dcontext * plain[h]
            low_attend = att[b, h * block : (h + 1) * block, 0:stop]
            attend = low_attend.astype(F32)
            dattend = nt(dhead, values)
            dscores = attend * (dattend - jnp.sum(attend * dattend, -1, keepdims=True))
            dscores = (dscores * scale).astype(BF)
            dq = dq + nn(dscores, keys * turned[h])
            dk[0:stop, :] += tn(dscores, queries * turned[h])
            dv[0:stop, :] += tn(low_attend, dhead)
        a, c = dq[:, 0:128], dq[:, 128:256]
        packed[start:stop, 0:128] = (a * cosine[start:stop] + c * sine[start:stop]).astype(BF)
        packed[start:stop, 128:256] = (c * cosine[start:stop] - a * sine[start:stop]).astype(BF)
    a, c = dk[:, 0:128], dk[:, 128:256]
    packed[:, 256:384] = (a * cosine + c * sine).astype(BF)
    packed[:, 384:512] = (c * cosine - a * sine).astype(BF)
    packed[:, 512:768] = dv[...].astype(BF)
    dfirst = nn(packed[...], project[...])
    out[...] = dfirst.astype(BF)
    normed_one, _ = standard(states[...].astype(F32))
    gain[...] = jnp.broadcast_to(jnp.sum(dfirst * normed_one, 0, keepdims=True), gain.shape)


def input_gradient(gain_row, mid, own, came, gains, states):
    normed, inverse = standard(states[...].astype(F32))
    dfirst = own[...].astype(F32) + came[...].astype(F32)
    return mid[...] + norm_back(dfirst * gains[gain_row : gain_row + 1, :], normed, inverse)


def pool_back_kernel(real, who, mid, own, came, gains, states, pool, delta, out):
    delta[...] = input_gradient(2, mid, own, came, gains, states).astype(BF)
    djoined = nt(delta[...], pool[...]).astype(BF)
    total = jnp.zeros(out.shape, F32)
    for j, mask in enumerate(join_masks(who, delta.shape[0], out.shape[0], real)):
        total = total + tn(mask, djoined[:, HALF * j : HALF * j + HALF])
    out[...] = total.astype(BF)


def outputs_kernel(who, full, grown, grown_came, mid, own, came, gains, states, o0, o1, o2, o3, whole):
    @pl.when(who[1] == 0)
    def _():
        whole[...] = (full[...].astype(F32) + (grown[...].astype(F32) + grown_came[...].astype(F32))).astype(BF)

    @pl.when(who[1] != 0)
    def _():
        whole[...] = input_gradient(0, mid, own, came, gains, states).astype(BF)

    for q, out in zip(chips(who), (o0, o1, o2, o3)):
        out[...] = whole[0 : out.shape[0], lanes(128 * q)]


def ffn_weights(who, write, hidden, delta, second, inner, gain, dwiden, dnarrow):
    dnarrow[...] = tn(hidden[...], delta[...]).astype(BF)
    dwiden[...] = tn(second[...], inner[...]).astype(BF)
    regroup_gain(who, write, gain)
    regroup_ffn(who, write, PAD, dwiden, dnarrow)


def attn_weights(who, write, ctx, mix, packed, first, gain, dproject, dmerge):
    dproject[...] = tn(packed[...], first[...]).astype(BF)
    dmerge[...] = tn(ctx[...], mix[...]).astype(BF)
    regroup_gain(who, write, gain)
    regroup_attn(who, write, PAD, dproject, dmerge)


def group_b_kernel(
    who, ctx, mix, packed, first, gain, joined, delta, part, grouped, keep, pass_on, send, dproject, dmerge, dpool, dexpand
):
    write = writer(keep, pass_on, send)
    attn_weights(who, write, ctx, mix, packed, first, gain, dproject, dmerge)
    dpool[...] = tn(joined[...], delta[...]).astype(BF)
    regroup_pool(who, write, PAD + ATTN, dpool)
    dexpand[...] = tn(part[...], grouped[...]).astype(BF)
    regroup_expand(who, write, PAD + ATTN + THIRD, dexpand)


def short_ffn_kernel(
    places, who, states, own, came, gains, s, x, y, d, d_own, d_came, middle, out, delta, dsecond, keep, pass_on, send,
    second, widen, narrow, hidden, slope, inner, gain, dwiden, dnarrow,
):
    k = who[1]
    ffn_kernel(
        3, places, who, states, own, came, gains, s, x, y, d, middle, second, widen, narrow, hidden, slope, out
    )
    delta[:, lanes(HALF * k, HALF)] = d_own[...]
    delta[:, lanes(HALF * (1 - k), HALF)] = d_came[...]
    ffn_back(3, delta[...], middle, gains, slope, widen, narrow, inner, dsecond, gain)
    ffn_weights(who, writer(keep, pass_on, send), hidden, delta, second, inner, gain, dwiden, dnarrow)


def ffn_group_kernel(who, hidden, delta, second, inner, gain, keep, pass_on, send, dwiden, dnarrow):
    ffn_weights(who, writer(keep, pass_on, send), hidden, delta, second, inner, gain, dwiden, dnarrow)


def attn_group_kernel(who, ctx, mix, packed, first, gain, keep, pass_on, send, dproject, dmerge):
    attn_weights(who, writer(keep, pass_on, send), ctx, mix, packed, first, gain, dproject, dmerge)


class Halves:
    def __init__(self, first, second, start=0):
        self.first, self.second, self.half, self.start = first, second, first.shape[0], start

    def after(self, rows):
        return Halves(self.first, self.second, self.start + rows)

    def read(self, at, rows):
        at = at + self.start
        stop = at + rows
        if stop <= self.half:
            return self.first[at:stop, :].astype(F32)
        if at >= self.half:
            return self.second[at - self.half : stop - self.half, :].astype(F32)
        parts = (self.first[at : self.half, :], self.second[0 : stop - self.half, :])
        return jnp.concatenate([part.astype(F32) for part in parts], 0)


def both(who, own, came):
    return ((who[1], own.read), (1 - who[1], came.read))


def spread_gain(own, came, gain):
    gain[...] = own.read(0, 8)[0:1] + came.read(0, 8)[0:1]


def spread_ffn(who, own, came, widen, narrow):
    for k, read in both(who, own, came):
        for lc in range(2):
            widen[:, lanes(256 * k + 128 * lc)] = read(PAD + 512 * lc, 512)
        for qq in range(4):
            narrow[rows_at(512 * qq + 256 * k, 256, 256), :] = read(PAD + 1024 + 256 * qq, 256)


def spread_attn(who, own, came, project, merge, turned):
    for k, read in both(who, own, came):
        for j in range(4):
            for p in range(3):
                block = read(PAD + j * 192 + p * 64, 64)
                turned[rows_at(128 * p + 64 * k, 64, 64), 128 * j : 128 * j + 128] = block
        for pair in range(4):
            merge[rows_at(128 * pair + 64 * k, 64, 64), :] = read(PAD + 768 + pair * 64, 64)
    project[...] = jnp.swapaxes(turned[...], 0, 1)


def spread_whole(kernel, who, own, came, *outs):
    half = own.shape[0] // 2
    kernel(who, *[Halves(*[ref.at[pl.ds(half * i, half), :] for i in range(2)]) for ref in (own, came)], *outs)


def spread_either(kernel, who, keep, rest, keep_came, rest_came, *outs):
    @pl.when(who[6] == 0)
    def _():
        kernel(who, Halves(keep, rest), Halves(keep_came, rest_came), *outs)

    @pl.when(who[6] != 0)
    def _():
        kernel(who, Halves(rest, keep), Halves(rest_came, keep_came), *outs)


def spread_b_kernel(who, own, came, gain, project, merge, pool, expand, turned):
    spread_gain(own, came, gain)
    spread_attn(who, own, came, project, merge, turned)
    for k, read in both(who, own, came):
        for i in range(6):
            pool[rows_at(512 * (i // 2) + 256 * k + 128 * (i % 2), 128, 128), :] = read(PAD + ATTN + i * 128, 128)
            block = read(PAD + ATTN + THIRD + i * 128, 128)
            expand[rows_at(256 * k + 128 * (i % 2), 128, 128), 128 * (i // 2) : 128 * (i // 2) + 128] = block


def spread_ffn_kernel(who, own, came, gain, widen, narrow):
    spread_gain(own, came, gain)
    spread_ffn(who, own, came, widen, narrow)


def spread_attn_kernel(who, own, came, gain, project, merge, turned):
    spread_gain(own, came, gain)
    spread_attn(who, own, came, project, merge, turned)


class Far:
    def __init__(self, array):
        self.array = array


class Raw(Far):
    pass


class Far:
    def __init__(self, array):
        self.array = array


class Raw(Far):
    pass


def spread_both_kernel(who, own, came, gain_ffn, widen, narrow, gain_attn, project, merge, turned):
    spread_ffn_kernel(who, own, came, gain_ffn, widen, narrow)
    own, came = own.after(PAD + FFN), came.after(PAD + FFN)
    spread_attn_kernel(who, own, came, gain_attn, project, merge, turned)


def call(kernel, name, outs, who, *args, scratch=(), sems=0, space=pltpu.VMEM, limit=VMEM_LIMIT):
    whole = pl.BlockSpec(memory_space=pltpu.VMEM)
    whos = [] if who is None else [who]
    spaces = [pltpu.HBM if isinstance(a, Far) else space for a in args]
    kinds = [pltpu.HBM if isinstance(a, Raw) else space for a in args]
    args = [a.array if isinstance(a, Far) else a for a in args]
    return pl.pallas_call(
        kernel,
        name=name,
        out_shape=[(pltpu.HBM if far else pltpu.VMEM)(shape, dtype) for shape, dtype, *far in outs],
        in_specs=[pl.BlockSpec(memory_space=pltpu.SMEM)] * len(whos) + [pl.BlockSpec(memory_space=kind) for kind in kinds],
        out_specs=[whole] * len(outs),
        scratch_shapes=[pltpu.VMEM(shape, dtype) for shape, dtype in scratch]
        + ([pltpu.SemaphoreType.DMA((sems,))] if sems else []),
        compiler_params=pltpu.CompilerParams(vmem_limit_bytes=limit),
        cost_estimate=pl.CostEstimate(flops=1024, bytes_accessed=1024, transcendentals=0),
    )(*whos, *[pltpu.with_memory_space_constraint(a, place) for a, place in zip(args, spaces)])


def swap(value, role):
    count = lax.axis_size("dp")
    route = []
    for chip in range(lax.axis_size("section")):
        for d in range(count):
            distance = (0, 1 + d % 2, 2 - d % 2, 3)[role]
            route.append((chip * count + d, (chip ^ distance) * count + d))
    return lax.ppermute(value, ("section", "dp"), route)


def across(value):
    return lax.ppermute(value, "dp", [(i, i ^ 1) for i in range(lax.axis_size("dp"))])


class Order:
    def __init__(self):
        self.last = None

    def tie(self, value, *others):
        others = [o for o in (self.last, *others) if o is not None]
        return lax.optimization_barrier((value, others))[0] if others else value

    def wait(self, *values):
        self.last = lax.optimization_barrier((self.last, values))[0]

    def call(self, kernel, name, outs, who, *args, **options):
        results = call(kernel, name, outs, None if who is None else self.tie(who), *args, **options)
        self.last = results[-1]
        return results

    def add(self, first, *others):
        total = self.tie(first)
        for other in others:
            total = total + other
        self.last = total
        return total


class Stage:
    def __init__(self, pieces):
        self.pieces = [pieces]

    def start(self, order):
        own = order.tie(self.pieces[0])
        self.pieces += [swap(own, 1), swap(own, 2)]

    def relay(self, order):
        self.pieces.append(swap(order.tie(self.pieces[1]), 2))

    def all(self):
        return [Far(array) for array in self.pieces]

    def places(self):
        return (0,) * 4


class Sum:
    def __init__(self, order, group):
        self.order = order
        self.keep, self.pass_on, self.send = group

    def first(self):
        self.came = swap(self.order.tie(self.send), 1)

    def second(self):
        self.last = swap(self.order.add(self.came[1], self.pass_on), 2)

    def across_rows(self, value, distance):
        route = [(i, i ^ (2 * distance)) for i in range(lax.axis_size("dp"))]
        return lax.ppermute(value, "dp", route)

    def total(self):
        return self.order.add(self.last, self.came[0], self.keep)

    def third(self, apart=False):
        total = self.total()
        count = lax.axis_size("dp")
        self.short = count == 8 and not apart
        if self.short:
            half = total.shape[0] // 2
            odd = (lax.axis_index("dp") // 2) % 2 == 1
            self.keep = jnp.where(odd, total[half:], total[:half])
            self.came = self.across_rows(jnp.where(odd, total[:half], total[half:]), 1)
        else:
            groups = [[i for i in range(count) if i % 2 == core] for core in range(2)]
            self.keep = lax.psum(total, "dp", axis_index_groups=groups)

    def fourth(self):
        if self.short:
            self.keep = self.order.add(self.came, self.keep)
            self.came = self.across_rows(self.keep, 2)

    def fifth(self):
        if self.short:
            self.keep = self.order.add(self.came, self.keep)
            self.rest = self.across_rows(self.keep, 1)

    def sixth(self):
        if self.short:
            self.keep, self.rest = self.order.tie((self.keep, self.rest))
            self.keep_came, self.rest_came = across(self.keep), across(self.rest)
        else:
            self.keep = self.order.tie(self.keep)
            self.keep_came = across(self.keep)

    def all(self):
        if self.short:
            return self.keep, self.rest, self.keep_came, self.rest_came
        return self.keep, self.keep_came


class Delivery:
    def __init__(self, order, pieces, c, k):
        self.order, self.c, self.k = order, c, k
        pieces = order.tie(pieces)
        self.came = [pieces[0]] + [swap(pieces[r], r) for r in range(1, 4)]

    def row(self, chip):
        far, came = self.c ^ chip, self.came
        first = far == 1 + self.k
        return jnp.where(far == 0, came[0], jnp.where(first, came[1], jnp.where(far == 3, came[3], came[2])))

    def turn(self):
        k = self.k
        self.came = self.order.tie(self.came)
        self.own = jnp.concatenate([self.row(2 * k), self.row(2 * k + 1)], 0)
        other = jnp.concatenate([self.row(2 - 2 * k), self.row(3 - 2 * k)], 0)
        self.order.last = other
        self.other = across(other)

    def finish(self):
        own, other = self.own, self.order.tie(self.other)
        results = jnp.where(self.k == 0, own, other), jnp.where(self.k == 0, other, own)
        self.order.last = results[0]
        return results


def angles(places):
    freq = 10000.0 ** (-2.0 * jnp.arange(SIZE // 2, dtype=F32) / SIZE)
    phase = places.astype(F32)[:, None] * jnp.tile(freq, LOCAL)[None, :]
    return jnp.cos(phase), jnp.sin(phase)


def places_of(counts, count, unit):
    at = jnp.arange(count, dtype=jnp.int32)
    starts = unit * jnp.sum(jnp.where(jnp.arange(3)[:, None] >= jnp.arange(3)[None, :], counts[None, :3], 0), 1)
    begin = jnp.max(jnp.where(at[:, None] >= starts[None, :], starts[None, :], 0), 1)
    return at - begin


def body(
    tokens,
    lengths,
    cotangent,
    full_first_gain,
    full_project,
    full_merge,
    full_second_gain,
    full_widen,
    full_narrow,
    pool_weight,
    short_first_gain,
    short_project,
    short_merge,
    short_second_gain,
    short_widen,
    short_narrow,
    expand_weight,
):
    c = lax.axis_index("section")
    d = lax.axis_index("dp")
    k = d % 2
    rows = lengths.shape[0]
    length = tokens.shape[0] // rows
    groups = length // 3
    count = -(-length // QUARTER) * QUARTER
    short = -(-groups // 16) * 16

    here = k == c // 2
    who_k = jnp.stack([c, k]).astype(jnp.int32)
    order = Order()
    gain_rows = [
        g.reshape(1, QUARTER) for g in (full_first_gain, full_second_gain, short_first_gain, short_second_gain)
    ]
    attn_in = [((WIDTH, 3 * QUARTER), BF), ((WIDTH, QUARTER), BF), ((3 * QUARTER, WIDTH), BF)]
    pieces1, = order.call(
        pack_first_kernel, "pack_first", [((PAD + ATTN, QUARTER), BF)], None, full_project, full_merge, *gain_rows,
        scratch=attn_in + [((1, QUARTER), BF)] * 4, sems=6, space=pltpu.HBM, limit=PACK_LIMIT,
    )
    stage1 = [pieces1] + [swap(pieces1, r) for r in (1, 2, 3)]

    j = order.tie(c % 2)
    pairs = jnp.stack([lax.dynamic_index_in_dim(a.reshape(rows, length, WIDTH), j, 0, False) for a in (tokens, cotangent)])
    ends = lax.dynamic_index_in_dim(lengths, j, 0, False).astype(BF)
    ends = jnp.pad(ends, (0, WIDTH - ends.shape[0]))
    own_row = jnp.concatenate([pairs, jnp.broadcast_to(ends, (2, count - length, WIDTH))], 1)
    came_row = across(own_row)

    pieces2, pieces3, pieces4 = order.call(
        pack_rest_kernel, "pack_rest", [((n, QUARTER), BF) for n in (FFN, THIRD + ATTN + THIRD, FFN)],
        None, full_widen, full_narrow, pool_weight, short_project, short_merge, expand_weight, short_widen,
        short_narrow, scratch=attn_in, sems=26, space=pltpu.HBM, limit=PACK_LIMIT,
    )
    stage2, stage3, stage4 = (Stage(p) for p in (pieces2, pieces3, pieces4))
    stage2.start(order)
    stage3.start(order)

    counts = jnp.where(here, own_row[0, length, :SEGS], came_row[0, length, :SEGS]).astype(jnp.int32)
    odd = (d // 2) % 2 if lax.axis_size("dp") == 8 else jnp.zeros_like(d)
    who = jnp.concatenate([who_k, counts, jnp.stack([odd, odd]).astype(jnp.int32)])
    cos, sin = angles(places_of(counts, count, 3))
    short_cos, short_sin = angles(places_of(counts, short, 1))

    def block_outs(n):
        outs = [
            ((3 * HALF, WIDTH), BF, Far),
            ((HALF, WIDTH), BF, Far),
            ((n, WIDTH), BF, Far),
            ((n, HALF), BF, Far),
            ((n, HALF), BF, Far),
            ((n, HALF), BF, Far),
        ]
        return outs if n == count else [out[:2] for out in outs]

    def ffn_outs(n):
        outs = [
            ((n, WIDTH), F32, Far),
            ((n, WIDTH), BF, Far),
            ((WIDTH, HIDDEN), BF, Far),
            ((HIDDEN, WIDTH), BF, Far),
            ((n, HIDDEN), BF, Far),
            ((n, HIDDEN), BF, Far),
            ((n, WIDTH), BF),
        ]
        return outs if n == count else [out[:2] for out in outs]

    def back_outs(n):
        return [
            ((n, WIDTH), F32),
            ((n, WIDTH), BF),
            ((n, 3 * HALF), BF),
            ((n, WIDTH), BF),
            ((PAD, WIDTH), F32),
        ]

    def sent(part):
        return [((part, QUARTER), BF, Far)] * 2 + [((2, part, QUARTER), BF, Far)]

    row, gains, project, merge, first, q, key, v, att, ctx, mix = order.call(
        full_attention_kernel, "full_attention",
        [((count, WIDTH), BF), ((PAD, WIDTH), F32)] + block_outs(count)
        + [((count // QUARTER, LOCAL * QUARTER, count), BF, Far), ((count, HALF), BF, Far), ((count, WIDTH), BF)],
        who, Raw(own_row), Raw(came_row), cos, sin, *[Far(a) for a in stage1], sems=2,
    )
    mix_came = across(mix)
    stage2.relay(order)
    stage3.relay(order)
    stage4.start(order)
    middle, second, widen, narrow, hidden, slope, part = order.call(
        functools.partial(ffn_kernel, 1, stage2.places()), "full_ffn", ffn_outs(count),
        who, row, mix, mix_came, gains, *stage2.all(),
    )
    part_came = across(part)
    full, pool, joined, pooled = order.call(
        functools.partial(pool_kernel, groups, stage3.places()), "pool",
        [((count, WIDTH), BF, Far), ((3 * HALF, WIDTH), BF, Far), ((short, 3 * HALF), BF, Far), ((short, WIDTH), BF)],
        who, Far(middle), part, part_came, *stage3.all(),
    )
    s_in, s_project, s_merge, s_first, s_q, s_key, s_v, s_att, s_ctx, s_mix = order.call(
        functools.partial(short_attention_kernel, stage3.places()), "short_attention",
        [((short, WIDTH), BF)] + block_outs(short)
        + [((1, LOCAL * short, short), BF), ((short, HALF), BF), ((short, WIDTH), BF)],
        who, pooled, across(pooled), short_cos, short_sin, gains, *stage3.all(),
    )
    s_mix_came = across(s_mix)
    stage4.relay(order)
    target, expand, grouped, d_half = order.call(
        functools.partial(expand_back_kernel, groups, stage3.places()), "expand_back",
        [((count, WIDTH), BF, Far), ((HALF, 3 * WIDTH), BF), ((short, 3 * WIDTH), BF), ((short, HALF), BF)],
        who, Raw(own_row), Raw(came_row), *stage3.all(), sems=2,
    )
    d_came = across(d_half)
    s_middle, s_part, s_delta, s_dsecond, *group = order.call(
        functools.partial(short_ffn_kernel, stage4.places()), "short_ffn",
        [((short, WIDTH), F32)] + [((short, WIDTH), BF)] * 3 + sent(PAD + FFN),
        who, s_in, s_mix, s_mix_came, gains, *stage4.all(), d_half, d_came,
        scratch=[
            ((short, WIDTH), BF), ((WIDTH, HIDDEN), BF), ((HIDDEN, WIDTH), BF), ((short, HIDDEN), BF),
            ((short, HIDDEN), BF), ((short, HIDDEN), BF), ((PAD, WIDTH), F32), ((WIDTH, HIDDEN), BF),
            ((HIDDEN, WIDTH), BF),
        ],
    )
    s_dsecond_came = across(s_dsecond)
    sum_a = Sum(order, group)
    sum_a.first()
    s_part_came = across(s_part)
    s_mid, s_dmix, s_dpacked, s_dfirst, s_gain1 = order.call(
        functools.partial(attention_back_kernel, 2, 3, short), "short_attention_back", back_outs(short),
        who, s_delta, s_dsecond, s_dsecond_came, s_middle, gains, s_in, s_merge, s_project, s_q, s_key, s_v, s_att,
        short_cos, short_sin, scratch=[((short, HALF), F32)] * 2,
    )
    s_dfirst_came = across(s_dfirst)
    s_half, grown = order.call(
        functools.partial(expand_kernel, groups), "expand", [((short, HALF), BF), ((count, WIDTH), BF, Far)],
        who, s_middle, s_part, s_part_came, expand, scratch=[((short, WIDTH), BF)],
    )
    grown_came = across(grown)
    d_in, d_low = order.call(
        functools.partial(pool_back_kernel, groups), "pool_back", [((short, WIDTH), BF), ((count, HALF), BF)],
        who, s_mid, s_dfirst, s_dfirst_came, gains, s_in, Far(pool),
    )
    d_low_came = across(d_low)
    order.wait(grown_came)
    sum_b = Sum(order, order.call(
        group_b_kernel, "group_b", sent(PAD + ATTN + 2 * THIRD),
        who, s_ctx, s_dmix, s_dpacked, s_first, s_gain1, Far(joined), d_in, s_half, grouped,
        scratch=[((3 * HALF, WIDTH), BF), ((HALF, WIDTH), BF), ((3 * HALF, WIDTH), BF), ((HALF, 3 * WIDTH), BF)],
    ))
    sum_b.first()
    sum_a.second()
    delta, low, inner, dsecond, gain2 = order.call(
        full_ffn_back_kernel, "full_ffn_back",
        [((count, WIDTH), F32), ((count, WIDTH), BF), ((count, HIDDEN), BF), ((count, WIDTH), BF), ((PAD, WIDTH), F32)],
        who, Far(target), d_low, d_low_came, Far(middle), gains, Far(slope), Far(widen), Far(narrow),
    )
    dsecond_came = across(dsecond)
    sum_c = Sum(order, order.call(
        ffn_group_kernel, "group_c", sent(PAD + FFN), who, Far(hidden), low, Far(second), inner, gain2,
        scratch=[((WIDTH, HIDDEN), BF), ((HIDDEN, WIDTH), BF)],
    ))
    sum_a.third()
    sum_b.second()
    sum_a.fourth()
    sum_c.first()
    mid, dmix, dpacked, dfirst, gain1 = order.call(
        functools.partial(attention_back_kernel, 0, 1, QUARTER), "full_attention_back", back_outs(count),
        who, delta, dsecond, dsecond_came, Far(middle), gains, row, Far(merge), Far(project), Far(q), Far(key), Far(v),
        Far(att), cos, sin, scratch=[((count, HALF), F32)] * 2,
    )
    dfirst_came = across(dfirst)
    sum_b.third()
    sum_d = Sum(order, order.call(
        attn_group_kernel, "group_d", sent(PAD + ATTN), who, Far(ctx), dmix, dpacked, Far(first), gain1,
        scratch=[((3 * HALF, WIDTH), BF), ((HALF, WIDTH), BF)],
    ))
    sum_c.second()
    sum_d.first()
    sent_rows = order.call(
        outputs_kernel, "outputs", [((length, QUARTER), BF)] * 4,
        who, Far(full), Far(grown), grown_came, mid, dfirst, dfirst_came, gains, row, scratch=[((count, WIDTH), BF)],
    )


    gain_out = ((1, QUARTER), F32)
    ffn_out = [((WIDTH, WIDTH), F32), ((4 * WIDTH, QUARTER), F32)]
    attn_out = [((WIDTH, 3 * QUARTER), F32), ((WIDTH, QUARTER), F32)]
    turned = [((3 * QUARTER, WIDTH), F32)]

    def spread(kernel, name, outs, total, **options):
        outs = [(*out, Far) for out in outs]
        how = spread_either if total.short else spread_whole
        return order.call(functools.partial(how, kernel), name, outs, who, *total.all(), **options)

    sum_a.fifth()
    sum_b.fourth()
    sum_d.second()
    sum_c.third()
    sum_d.third()
    sum_a.sixth()
    sum_c.fourth()
    sum_b.fifth()
    sum_d.fourth()
    g_s2, g_s_widen, g_s_narrow = spread(spread_ffn_kernel, "spread_a", [gain_out] + ffn_out, sum_a)
    sum_c.fifth()
    sum_d.fifth()
    sum_c.sixth()
    sum_b.sixth()
    sum_d.sixth()
    g_s1, g_s_project, g_s_merge, g_pool, g_expand = spread(
        spread_b_kernel, "spread_b",
        [gain_out] + attn_out + [((3 * WIDTH, QUARTER), F32), ((WIDTH, 3 * QUARTER), F32)], sum_b, scratch=turned,
    )
    delivery = Delivery(order, sent_rows, c, k)
    delivery.turn()
    g_f2, g_widen, g_narrow = spread(spread_ffn_kernel, "spread_c", [gain_out] + ffn_out, sum_c)
    g_f1, g_project, g_merge = spread(spread_attn_kernel, "spread_d", [gain_out] + attn_out, sum_d, scratch=turned)
    mixed_out, token_gradient = delivery.finish()

    return (
        mixed_out,
        token_gradient,
        g_f1.reshape(-1),
        g_project,
        g_merge,
        g_f2.reshape(-1),
        g_widen,
        g_narrow,
        g_pool,
        g_s1.reshape(-1),
        g_s_project,
        g_s_merge,
        g_s2.reshape(-1),
        g_s_widen,
        g_s_narrow,
        g_expand,
    )


def solution(mesh):
    in_specs = (
        P("dp", None),
        P("dp", None),
        P("dp", None),
        P("section"),
        P(None, "section"),
        P(None, "section"),
        P("section"),
        P(None, "section"),
        P(None, "section"),
        P(None, "section"),
        P("section"),
        P(None, "section"),
        P(None, "section"),
        P("section"),
        P(None, "section"),
        P(None, "section"),
        P(None, "section"),
    )
    out_specs = (
        P("dp", "section"),
        P("dp", "section"),
        P("section"),
        P(None, "section"),
        P(None, "section"),
        P("section"),
        P(None, "section"),
        P(None, "section"),
        P(None, "section"),
        P("section"),
        P(None, "section"),
        P(None, "section"),
        P("section"),
        P(None, "section"),
        P(None, "section"),
        P(None, "section"),
    )
    return jax.shard_map(body, mesh=mesh, in_specs=in_specs, out_specs=out_specs, check_vma=False)
```

```python
import functools

import jax
import jax.numpy as jnp
from jax import lax
from jax.experimental import pallas as pl
from jax.experimental.pallas import tpu as pltpu
from jax.sharding import PartitionSpec as P


WIDTH = 512
QUARTER = 128
HALF = 256
HIDDEN = 1024
SEGS = 4
LOCAL = 4
SIZE = 64
EPS = 1e-05
NEG = -1e30

BF = jnp.bfloat16
F32 = jnp.float32

ATTN = 1024
FFN = 2048
THIRD = 768
PAD = 32
VMEM_LIMIT = 16 * 2**20
PACK_LIMIT = 60 * 2**20


def nn(left, right):
    return lax.dot_general(left, right, (((1,), (0,)), ((), ())), preferred_element_type=F32)


def nt(left, right):
    return lax.dot_general(left, right, (((1,), (1,)), ((), ())), preferred_element_type=F32)


def tn(left, right):
    return lax.dot_general(left, right, (((0,), (0,)), ((), ())), preferred_element_type=F32)


def lanes(start, count=QUARTER):
    return pl.ds(pl.multiple_of(start, QUARTER), count)


def rows_at(start, count, unit):
    return pl.ds(pl.multiple_of(start, unit), count)


def iota(shape, dim):
    return lax.broadcasted_iota(jnp.int32, shape, dim)


def standard(states):
    center = states - jnp.mean(states, -1, keepdims=True)
    inverse = lax.rsqrt(jnp.mean(center * center, -1, keepdims=True) + EPS)
    return center * inverse, inverse


def norm_back(delta, normed, inverse):
    return inverse * (
        delta
        - jnp.mean(delta, -1, keepdims=True)
        - normed * jnp.mean(delta * normed, -1, keepdims=True)
    )


def gelu_parts(x):
    z = x * 0.7071067811865476
    t = 1.0 / (1.0 + 0.3275911 * jnp.abs(z))
    e = jnp.exp(-z * z)
    poly = t * (
        0.127414796
        + t * (-0.142248368 + t * (0.7107068705 + t * (-0.7265760135 + t * 0.5307027145)))
    )
    tail = poly * e
    phi = jnp.where(z >= 0, 1.0 - tail, tail)
    return x * phi, phi + x * e * 0.3989422804014327


def chips(who):
    c, k = who[0], who[1]
    return c, c ^ (1 + k), c ^ (2 - k), c ^ 3


def reader(refs, places):
    def read(r, at, rows):
        return refs[r][places[r] + at : places[r] + at + rows, :]

    return read


def writer(keep, pass_on, send):
    def write(r, at, value):
        if r % 2 == 0:
            (keep, pass_on)[r // 2][at : at + value.shape[0], :] = value
        else:
            send[r // 2, at : at + value.shape[0], :] = value

    return write


def pair_rows(pair):
    is_value = pair >= 8
    first = jnp.where(is_value, 512 + 64 * (pair - 8), 256 * (pair >> 2) + 32 * (pair & 3))
    second = jnp.where(is_value, first + 32, first + 128)
    return first, second


def pack_attn(k, turned, merge, put, base):
    for p in range(3):
        chunk = turned[rows_at(128 * p + 64 * k, 64, 64), :]
        for j in range(4):
            put(base + j * 192 + p * 64, chunk[:, 128 * j : 128 * j + 128])
    for pair in range(4):
        put(base + 768 + pair * 64, merge[rows_at(128 * pair + 64 * k, 64, 64), :])


def unpack_attn(who, read, base, project, merge):
    for r, q in enumerate(chips(who)):
        for p in range(3):
            first, second = pair_rows(3 * q + p)
            for j in range(4):
                block = read(r, base + j * 192 + p * 64, 64)
                project[rows_at(first, 32, 32), 128 * j : 128 * j + 128] = block[:32]
                project[rows_at(second, 32, 32), 128 * j : 128 * j + 128] = block[32:]
        for pair in range(4):
            merge[64 * pair : 64 * pair + 64, lanes(128 * q)] = read(r, base + 768 + pair * 64, 64)


def regroup_attn(who, write, base, project, merge):
    for r, q in enumerate(chips(who)):
        for p in range(3):
            first, second = pair_rows(3 * q + p)
            for j in range(4):
                at = base + j * 192 + p * 64
                write(r, at, project[rows_at(first, 32, 32), 128 * j : 128 * j + 128])
                write(r, at + 32, project[rows_at(second, 32, 32), 128 * j : 128 * j + 128])
        for pair in range(4):
            write(r, base + 768 + pair * 64, merge[64 * pair : 64 * pair + 64, lanes(128 * q)])


def pack_ffn(k, widen, narrow, put):
    for lc in range(2):
        put(512 * lc, widen.at[:, lanes(256 * k + 128 * lc)])
    for qq in range(4):
        put(1024 + 256 * qq, narrow.at[rows_at(512 * qq + 256 * k, 256, 256), :])


def unpack_ffn(who, read, widen, narrow):
    for r, q in enumerate(chips(who)):
        for lc in range(2):
            widen[:, lanes(256 * q + 128 * lc)] = read(r, 512 * lc, 512)
        narrow[:, lanes(128 * q)] = read(r, 1024, 1024)


def regroup_ffn(who, write, base, widen, narrow):
    for r, q in enumerate(chips(who)):
        for lc in range(2):
            write(r, base + 512 * lc, widen[:, lanes(256 * q + 128 * lc)])
        write(r, base + 1024, narrow[:, lanes(128 * q)])


def pack_pool(k, pool, put, base):
    for i in range(6):
        put(base + i * 128, pool.at[rows_at(512 * (i // 2) + 256 * k + 128 * (i % 2), 128, 128), :])


def unpack_pool(who, read, base, pool):
    for r, q in enumerate(chips(who)):
        for i in range(6):
            pool[128 * i : 128 * i + 128, lanes(128 * q)] = read(r, base + i * 128, 128)


def regroup_pool(who, write, base, pool):
    for r, q in enumerate(chips(who)):
        for i in range(6):
            write(r, base + i * 128, pool[128 * i : 128 * i + 128, lanes(128 * q)])


def pack_expand(k, expand, put, base):
    for i in range(6):
        put(base + i * 128, expand.at[rows_at(256 * k + 128 * (i % 2), 128, 128), pl.ds(128 * (i // 2), 128)])


def unpack_expand(who, read, base, expand):
    for r, q in enumerate(chips(who)):
        for i in range(6):
            block = read(r, base + i * 128, 128)
            expand[128 * (i % 2) : 128 * (i % 2) + 128, lanes(384 * q + 128 * (i // 2))] = block


def regroup_expand(who, write, base, expand):
    for r, q in enumerate(chips(who)):
        for i in range(6):
            block = expand[128 * (i % 2) : 128 * (i % 2) + 128, lanes(384 * q + 128 * (i // 2))]
            write(r, base + i * 128, block)


def regroup_gain(who, write, gain):
    for r, q in enumerate(chips(who)):
        write(r, 0, gain[:, lanes(128 * q)].astype(BF))


class Copies:
    def __init__(self, sems):
        self.sems, self.all = sems, []

    def start(self, source, target):
        copy = pltpu.make_async_copy(source, target, self.sems.at[len(self.all)])
        copy.start()
        self.all.append(copy)

    def putter(self, ref):
        def put(at, source):
            self.start(source, ref.at[pl.ds(at, source.shape[0]), :])

        return put

    def wait(self):
        for copy in self.all:
            copy.wait()


def putter(ref):
    def put(at, value):
        ref[at : at + value.shape[0], :] = value

    return put


def core():
    return lax.rem(lax.axis_index("dp"), 2)


def pack_first_kernel(project, merge, g0, g1, g2, g3, out, project_in, merge_in, turned, i0, i1, i2, i3, sems):
    copies = Copies(sems)
    copies.start(project, project_in)
    copies.start(merge, merge_in)
    inside = (i0, i1, i2, i3)
    for gain, place in zip((g0, g1, g2, g3), inside):
        copies.start(gain, place)
    copies.wait()
    row = iota((PAD, QUARTER), 0)
    gains = jnp.zeros((PAD, QUARTER), F32)
    for i, place in enumerate(inside):
        gains = jnp.where(row == i, place[...].astype(F32), gains)
    out[0:PAD, :] = gains.astype(BF)
    turned[...] = jnp.swapaxes(project_in[...], 0, 1)
    pack_attn(core(), turned, merge_in, putter(out), PAD)


def pack_rest_kernel(
    widen, narrow, pool, project, merge, expand, s_widen, s_narrow, out2, out3, out4, project_in, merge_in, turned, sems
):
    k = core()
    copies, last = Copies(sems), Copies(sems.at[pl.ds(2, 24)])
    copies.start(project, project_in)
    copies.start(merge, merge_in)
    pack_ffn(k, widen, narrow, last.putter(out2))
    pack_pool(k, pool, last.putter(out3), 0)
    pack_expand(k, expand, last.putter(out3), THIRD + ATTN)
    pack_ffn(k, s_widen, s_narrow, last.putter(out4))
    copies.wait()
    turned[...] = jnp.swapaxes(project_in[...], 0, 1)
    pack_attn(k, turned, merge_in, putter(out3), THIRD)
    last.wait()


def ends_of(who):
    e0 = who[2]
    e1 = e0 + who[3]
    e2 = e1 + who[4]
    return e0, e1, e2, e2 + who[5]


def segment_of(who, index, unit):
    return sum((index >= unit * end).astype(jnp.int32) for end in ends_of(who))


def head_masks():
    lane = iota((1, HALF), 1)
    turned = [((lane & 127) >> 5 == h).astype(F32).astype(BF) for h in range(LOCAL)]
    plain = [((lane >> 6) == h).astype(F32).astype(BF) for h in range(LOCAL)]
    return turned, plain


def attention_forward(who, states, gain, cos, sin, project, merge, first, q, k, v, att, ctx, mix, unit, block):
    count = states.shape[0]
    normed, _ = standard(states)
    start = (normed * gain).astype(BF)
    first[...] = start
    packed = nt(start, project[...])
    cosine, sine = cos[...], sin[...]
    for ref, at in ((q, 0), (k, 256)):
        a, b = packed[:, at : at + 128], packed[:, at + 128 : at + 256]
        ref[:, 0:128] = (a * cosine - b * sine).astype(BF)
        ref[:, 128:256] = (b * cosine + a * sine).astype(BF)
    v[...] = packed[:, 512:768].astype(BF)
    turned, plain = head_masks()
    scale = jnp.asarray(SIZE**-0.5, BF)
    for b in range(count // block):
        low, stop = b * block, (b + 1) * block
        at_row = low + iota((block, 1), 0)
        at_col = iota((1, stop), 1)
        allowed = (segment_of(who, at_row, unit) == segment_of(who, at_col, unit)) & (at_row >= at_col)
        queries = q[low:stop, :] * scale
        keys, values = k[0:stop, :], v[0:stop, :]
        total_context = jnp.zeros((block, HALF), F32)
        for h in range(LOCAL):
            scores = jnp.where(allowed, nt(queries * turned[h], keys), NEG)
            powered = jnp.exp(scores - jnp.max(scores, -1, keepdims=True))
            attend = (powered * (1.0 / jnp.sum(powered, -1, keepdims=True))).astype(BF)
            att[b, h * block : (h + 1) * block, 0:stop] = attend
            total_context = total_context + nn(attend, values * plain[h])
        ctx[low:stop, :] = total_context.astype(BF)
    mix[...] = nn(ctx[...], merge[...]).astype(BF)


def full_attention_kernel(
    who, own, came, cos, sin, s, x, y, d, row, gains, project, merge, first, q, k, v, att, ctx, mix, sems
):
    c = who[0]
    here = who[1] == c >> 1
    for i, (source, taken) in enumerate(((own, here), (came, jnp.logical_not(here)))):

        @pl.when(taken)
        def _():
            copy = pltpu.make_async_copy(source.at[0], row, sems.at[i])
            copy.start()
            copy.wait()

    read = reader((s, x, y, d), (0,) * 4)
    for r, chip in enumerate(chips(who)):
        gains[:, lanes(128 * chip)] = read(r, 0, PAD).astype(F32)
    unpack_attn(who, read, PAD, project, merge)
    states = row[...].astype(F32)
    attention_forward(
        who, states, gains[0:1, :], cos, sin, project, merge, first, q, k, v, att, ctx, mix, 3, QUARTER
    )


def short_attention_kernel(
    who, own, came, cos, sin, gains, s, x, y, d, states, project, merge, first, q, k, v, att, ctx, mix, box, sems
):
    unpack_attn(who, boxed((s, x, y, d), THIRD, box, sems), 0, project, merge)
    states[...] = (own[...].astype(F32) + came[...].astype(F32)).astype(BF)
    attention_forward(
        who, states[...].astype(F32), gains[2:3, :], cos, sin, project, merge, first, q, k, v, att, ctx, mix,
        1, own.shape[0],
    )


def ffn_kernel(
    gain_row, places, who, states, own, came, gains, s, x, y, d, middle, second, widen, narrow, hidden, slope, out
):
    unpack_ffn(who, reader((s, x, y, d), places), widen, narrow)
    mid = states[...].astype(F32) + (own[...].astype(F32) + came[...].astype(F32))
    middle[...] = mid
    normed, _ = standard(mid)
    start = (normed * gains[gain_row : gain_row + 1, :]).astype(BF)
    second[...] = start

    @pl.loop(0, 4)
    def _(i):
        cols = lanes(HALF * i, HALF)
        value, back = gelu_parts(nn(second[...], widen[:, cols]))
        hidden[:, cols] = value.astype(BF)
        slope[:, cols] = back.astype(BF)

    out[...] = nn(hidden[...], narrow[...]).astype(BF)


def join_masks(who, groups, count, real):
    g = iota((groups, 1), 0)
    t = iota((1, count), 1)
    ends = ends_of(who)
    keep = (g != ends[0]) & (g != ends[1]) & (g != ends[2]) & (g < real)
    return [
        jnp.where((t == 3 * g - 2) & keep, 1.0, 0.0).astype(BF),
        jnp.where((t == 3 * g - 1) & keep, 1.0, 0.0).astype(BF),
        jnp.where((t == 3 * g) & (g < real), 1.0, 0.0).astype(BF),
    ]


def group_masks(groups, count, real):
    g = iota((groups, 1), 0)
    t = iota((1, count), 1)
    return [jnp.where((t == 3 * g + i) & (g < real), 1.0, 0.0).astype(BF) for i in range(3)]


def boxed(refs, at, box, sems):
    copies = Copies(sems)
    for r, ref in enumerate(refs):
        copies.start(ref.at[pl.ds(at, box.shape[1]), :], box.at[r])
    copies.wait()

    def read(r, at, rows):
        return box[r, at : at + rows, :]

    return read


def pool_kernel(real, who, middle, own, came, s, x, y, d, full, pool, joined, out, box, sems):
    unpack_pool(who, boxed((s, x, y, d), 0, box, sems), 0, pool)
    full[...] = (middle[...] + (own[...].astype(F32) + came[...].astype(F32))).astype(BF)
    part = full[:, lanes(HALF * who[1], HALF)]
    for j, mask in enumerate(join_masks(who, joined.shape[0], full.shape[0], real)):
        joined[:, HALF * j : HALF * j + HALF] = nn(mask, part).astype(BF)
    out[...] = nn(joined[...], pool[...]).astype(BF)


def target_kernel(real, who, own, came, target, grouped, sems):
    here = who[1] == who[0] >> 1
    for i, (source, taken) in enumerate(((own, here), (came, jnp.logical_not(here)))):

        @pl.when(taken)
        def _():
            copy = pltpu.make_async_copy(source.at[1], target, sems.at[i])
            copy.start()
            copy.wait()

    live = segment_of(who, iota((target.shape[0], 1), 0), 3) < 3
    target[...] = jnp.where(live, target[...].astype(F32), 0.0).astype(BF)
    for i, mask in enumerate(group_masks(grouped.shape[0], target.shape[0], real)):
        grouped[:, WIDTH * i : WIDTH * i + WIDTH] = nn(mask, target[...]).astype(BF)


def expand_back_kernel(who, grouped, s, x, y, d, expand, out, box, sems):
    unpack_expand(who, boxed((s, x, y, d), THIRD + ATTN, box, sems), 0, expand)
    out[...] = nt(grouped[...], expand[...]).astype(BF)


def expand_kernel(real, who, middle, own, came, expand, part, out, short):
    k = who[1]
    short[...] = (middle[...] + (own[...].astype(F32) + came[...].astype(F32))).astype(BF)
    part[...] = short[:, lanes(HALF * k, HALF)]
    grown = nn(part[...], expand[...]).astype(BF)
    total = jnp.zeros(out.shape, F32)
    for i, mask in enumerate(group_masks(part.shape[0], out.shape[0], real)):
        total = total + tn(mask, grown[:, WIDTH * i : WIDTH * i + WIDTH])
    out[...] = total.astype(BF)


def ffn_back(gain_row, delta, middle, gains, slope, widen, narrow, inner, out, gain):
    total = jnp.zeros(middle.shape, F32)
    for i in range(4):
        cols = slice(HALF * i, HALF * i + HALF)
        value = (nt(delta, narrow[cols, :]) * slope[:, cols].astype(F32)).astype(BF)
        inner[:, cols] = value
        total = total + nt(value, widen[:, cols])
    normed, _ = standard(middle[...])
    out[...] = total.astype(BF)
    gain[...] = jnp.broadcast_to(jnp.sum(total * normed, 0, keepdims=True), gain.shape)


def full_ffn_back_kernel(
    who, target, own, came, middle, gains, slope, widen, narrow, delta, low, inner, out, gain
):
    k = who[1]
    delta[:, lanes(HALF * k, HALF)] = own[...].astype(F32)
    delta[:, lanes(HALF * (1 - k), HALF)] = came[...].astype(F32)
    delta[...] = delta[...] + target[...].astype(F32)
    low[...] = delta[...].astype(BF)
    ffn_back(1, low[...], middle, gains, slope, widen, narrow, inner, out, gain)


def attention_back_kernel(
    first_row, second_row, block, who, delta, own, came, middle, gains, states, merge, project, q, k, v, att, cos, sin,
    mid, mix, packed, out, gain, dk, dv,
):
    count = middle.shape[0]
    normed, inverse = standard(middle[...])
    dsecond = own[...].astype(F32) + came[...].astype(F32)
    dmid = delta[...].astype(F32) + norm_back(dsecond * gains[second_row : second_row + 1, :], normed, inverse)
    mid[...] = dmid
    low = dmid.astype(BF)
    mix[...] = low
    dctx = nt(low, merge[...]).astype(BF)
    turned, plain = head_masks()
    scale = SIZE**-0.5
    cosine, sine = cos[...], sin[...]
    dk[...] = jnp.zeros(dk.shape, F32)
    dv[...] = jnp.zeros(dv.shape, F32)
    for b in range(count // block):
        start, stop = b * block, (b + 1) * block
        keys, values = k[0:stop, :], v[0:stop, :]
        queries = q[start:stop, :]
        dcontext = dctx[start:stop, :]
        dq = jnp.zeros((block, HALF), F32)
        for h in range(LOCAL):
            dhead = dcontext * plain[h]
            low_attend = att[b, h * block : (h + 1) * block, 0:stop]
            attend = low_attend.astype(F32)
            dattend = nt(dhead, values)
            dscores = attend * (dattend - jnp.sum(attend * dattend, -1, keepdims=True))
            dscores = (dscores * scale).astype(BF)
            dq = dq + nn(dscores, keys * turned[h])
            dk[0:stop, :] += tn(dscores, queries * turned[h])
            dv[0:stop, :] += tn(low_attend, dhead)
        a, c = dq[:, 0:128], dq[:, 128:256]
        packed[start:stop, 0:128] = (a * cosine[start:stop] + c * sine[start:stop]).astype(BF)
        packed[start:stop, 128:256] = (c * cosine[start:stop] - a * sine[start:stop]).astype(BF)
    a, c = dk[:, 0:128], dk[:, 128:256]
    packed[:, 256:384] = (a * cosine + c * sine).astype(BF)
    packed[:, 384:512] = (c * cosine - a * sine).astype(BF)
    packed[:, 512:768] = dv[...].astype(BF)
    dfirst = nn(packed[...], project[...])
    out[...] = dfirst.astype(BF)
    normed_one, _ = standard(states[...].astype(F32))
    gain[...] = jnp.broadcast_to(jnp.sum(dfirst * normed_one, 0, keepdims=True), gain.shape)


def input_gradient(gain_row, mid, own, came, gains, states):
    normed, inverse = standard(states[...].astype(F32))
    dfirst = own[...].astype(F32) + came[...].astype(F32)
    return mid[...] + norm_back(dfirst * gains[gain_row : gain_row + 1, :], normed, inverse)


def pool_back_kernel(real, who, mid, own, came, gains, states, pool, delta, out):
    delta[...] = input_gradient(2, mid, own, came, gains, states).astype(BF)
    djoined = nt(delta[...], pool[...]).astype(BF)
    total = jnp.zeros(out.shape, F32)
    for j, mask in enumerate(join_masks(who, delta.shape[0], out.shape[0], real)):
        total = total + tn(mask, djoined[:, HALF * j : HALF * j + HALF])
    out[...] = total.astype(BF)


def outputs_kernel(who, full, grown, grown_came, mid, own, came, gains, states, o0, o1, o2, o3, whole):
    @pl.when(who[1] == 0)
    def _():
        whole[...] = (full[...].astype(F32) + (grown[...].astype(F32) + grown_came[...].astype(F32))).astype(BF)

    @pl.when(who[1] != 0)
    def _():
        whole[...] = input_gradient(0, mid, own, came, gains, states).astype(BF)

    for q, out in zip(chips(who), (o0, o1, o2, o3)):
        out[...] = whole[0 : out.shape[0], lanes(128 * q)]


def ffn_weights(who, write, hidden, delta, second, inner, gain, dwiden, dnarrow):
    dnarrow[...] = tn(hidden[...], delta[...]).astype(BF)
    dwiden[...] = tn(second[...], inner[...]).astype(BF)
    regroup_gain(who, write, gain)
    regroup_ffn(who, write, PAD, dwiden, dnarrow)


def attn_weights(who, write, ctx, mix, packed, first, gain, dproject, dmerge):
    dproject[...] = tn(packed[...], first[...]).astype(BF)
    dmerge[...] = tn(ctx[...], mix[...]).astype(BF)
    regroup_gain(who, write, gain)
    regroup_attn(who, write, PAD, dproject, dmerge)


def group_b_kernel(
    who, ctx, mix, packed, first, gain, joined, delta, part, grouped, keep, pass_on, send, dproject, dmerge, dpool, dexpand
):
    write = writer(keep, pass_on, send)
    attn_weights(who, write, ctx, mix, packed, first, gain, dproject, dmerge)
    dpool[...] = tn(joined[...], delta[...]).astype(BF)
    regroup_pool(who, write, PAD + ATTN, dpool)
    dexpand[...] = tn(part[...], grouped[...]).astype(BF)
    regroup_expand(who, write, PAD + ATTN + THIRD, dexpand)


def short_ffn_kernel(
    who, states, own, came, gains, s, x, y, d, d_own, d_came, middle, hidden, delta, narrow, dsecond,
    keep, pass_on, send, second, widen, inner, gain, dwiden, dnarrow,
):
    k = who[1]
    unpack_ffn(who, reader((s, x, y, d), (0,) * 4), widen, narrow)
    mid = states[...].astype(F32) + (own[...].astype(F32) + came[...].astype(F32))
    middle[...] = mid
    normed, _ = standard(mid)
    second[...] = (normed * gains[3:4, :]).astype(BF)
    delta[:, lanes(HALF * k, HALF)] = d_own[...]
    delta[:, lanes(HALF * (1 - k), HALF)] = d_came[...]
    for i in range(4):
        cols = slice(HALF * i, HALF * i + HALF)
        value, back = gelu_parts(nn(second[...], widen[:, cols]))
        hidden[:, cols] = value.astype(BF)
        inner[:, cols] = (nt(delta[...], narrow[cols, :]) * back).astype(BF)
    total = nt(inner[...], widen[...])
    dsecond[...] = total.astype(BF)
    gain[...] = jnp.broadcast_to(jnp.sum(total * normed, 0, keepdims=True), gain.shape)
    ffn_weights(who, writer(keep, pass_on, send), hidden, delta, second, inner, gain, dwiden, dnarrow)


def short_ffn_rest_kernel(who, hidden, narrow, out):
    out[...] = nn(hidden[...], narrow[...]).astype(BF)


def ffn_group_kernel(who, hidden, delta, second, inner, gain, keep, pass_on, send, dwiden, dnarrow):
    ffn_weights(who, writer(keep, pass_on, send), hidden, delta, second, inner, gain, dwiden, dnarrow)


def attn_group_kernel(who, ctx, mix, packed, first, gain, keep, pass_on, send, dproject, dmerge):
    attn_weights(who, writer(keep, pass_on, send), ctx, mix, packed, first, gain, dproject, dmerge)


class Halves:
    def __init__(self, first, second, start=0):
        self.first, self.second, self.half, self.start = first, second, first.shape[0], start

    def after(self, rows):
        return Halves(self.first, self.second, self.start + rows)

    def read(self, at, rows):
        at = at + self.start
        stop = at + rows
        if stop <= self.half:
            return self.first[at:stop, :].astype(F32)
        if at >= self.half:
            return self.second[at - self.half : stop - self.half, :].astype(F32)
        parts = (self.first[at : self.half, :], self.second[0 : stop - self.half, :])
        return jnp.concatenate([part.astype(F32) for part in parts], 0)


def both(who, own, came):
    return ((who[1], own.read), (1 - who[1], came.read))


def spread_gain(own, came, gain):
    gain[...] = own.read(0, 8)[0:1] + came.read(0, 8)[0:1]


def spread_ffn(who, own, came, widen, narrow):
    for k, read in both(who, own, came):
        for lc in range(2):
            widen[:, lanes(256 * k + 128 * lc)] = read(PAD + 512 * lc, 512)
        for qq in range(4):
            narrow[rows_at(512 * qq + 256 * k, 256, 256), :] = read(PAD + 1024 + 256 * qq, 256)


def spread_attn(who, own, came, project, merge, turned):
    for k, read in both(who, own, came):
        for j in range(4):
            for p in range(3):
                block = read(PAD + j * 192 + p * 64, 64)
                turned[rows_at(128 * p + 64 * k, 64, 64), 128 * j : 128 * j + 128] = block
        for pair in range(4):
            merge[rows_at(128 * pair + 64 * k, 64, 64), :] = read(PAD + 768 + pair * 64, 64)
    project[...] = jnp.swapaxes(turned[...], 0, 1)


def spread_whole(kernel, who, own, came, *outs):
    half = own.shape[0] // 2
    kernel(who, *[Halves(*[ref.at[pl.ds(half * i, half), :] for i in range(2)]) for ref in (own, came)], *outs)


def spread_either(kernel, who, keep, rest, keep_came, rest_came, *outs):
    @pl.when(who[6] == 0)
    def _():
        kernel(who, Halves(keep, rest), Halves(keep_came, rest_came), *outs)

    @pl.when(who[6] != 0)
    def _():
        kernel(who, Halves(rest, keep), Halves(rest_came, keep_came), *outs)


def spread_b_kernel(who, own, came, gain, project, merge, pool, expand, turned):
    spread_gain(own, came, gain)
    spread_attn(who, own, came, project, merge, turned)
    for k, read in both(who, own, came):
        for i in range(6):
            pool[rows_at(512 * (i // 2) + 256 * k + 128 * (i % 2), 128, 128), :] = read(PAD + ATTN + i * 128, 128)
            block = read(PAD + ATTN + THIRD + i * 128, 128)
            expand[rows_at(256 * k + 128 * (i % 2), 128, 128), 128 * (i // 2) : 128 * (i // 2) + 128] = block


def spread_ffn_kernel(who, own, came, gain, widen, narrow):
    spread_gain(own, came, gain)
    spread_ffn(who, own, came, widen, narrow)


def spread_attn_kernel(who, own, came, gain, project, merge, turned):
    spread_gain(own, came, gain)
    spread_attn(who, own, came, project, merge, turned)


class Far:
    def __init__(self, array):
        self.array = array


class Free(Far):
    pass


class Raw(Far):
    pass


def call(kernel, name, outs, who, *args, scratch=(), sems=0, space=pltpu.VMEM, limit=VMEM_LIMIT):
    whole = pl.BlockSpec(memory_space=pltpu.VMEM)
    whos = [] if who is None else [who]
    spaces = [
        None if isinstance(a, (Raw, Free)) else pltpu.HBM if isinstance(a, Far) or space == pltpu.HBM else None
        for a in args
    ]
    kinds = [pl.ANY if isinstance(a, Raw) else space for a in args]
    args = [a.array if isinstance(a, Far) else a for a in args]
    return pl.pallas_call(
        kernel,
        name=name,
        out_shape=[(pltpu.HBM if far else pltpu.VMEM)(shape, dtype) for shape, dtype, *far in outs],
        in_specs=[pl.BlockSpec(memory_space=pltpu.SMEM)] * len(whos) + [pl.BlockSpec(memory_space=kind) for kind in kinds],
        out_specs=[whole] * len(outs),
        scratch_shapes=[pltpu.VMEM(shape, dtype) for shape, dtype in scratch]
        + ([pltpu.SemaphoreType.DMA((sems,))] if sems else []),
        compiler_params=pltpu.CompilerParams(vmem_limit_bytes=limit),
        cost_estimate=pl.CostEstimate(flops=1024, bytes_accessed=1024, transcendentals=0),
    )(*whos, *[a if place is None else pltpu.with_memory_space_constraint(a, place) for a, place in zip(args, spaces)])


def swap(value, role):
    count = lax.axis_size("dp")
    route = []
    for chip in range(lax.axis_size("section")):
        for d in range(count):
            distance = (0, 1 + d % 2, 2 - d % 2, 3)[role]
            route.append((chip * count + d, (chip ^ distance) * count + d))
    return lax.ppermute(value, ("section", "dp"), route)


def across(value):
    return lax.ppermute(value, "dp", [(i, i ^ 1) for i in range(lax.axis_size("dp"))])


class Order:
    def __init__(self):
        self.last = None

    def tie(self, value, *others):
        others = [o for o in (self.last, *others) if o is not None]
        return lax.optimization_barrier((value, others))[0] if others else value

    def wait(self, *values):
        self.last = lax.optimization_barrier((self.last, values))[0]

    def call(self, kernel, name, outs, who, *args, **options):
        results = call(kernel, name, outs, None if who is None else self.tie(who), *args, **options)
        self.last = results[-1]
        return results

    def add(self, first, *others):
        total = self.tie(first)
        for other in others:
            total = total + other
        self.last = total
        return total


class Stage:
    def __init__(self, pieces):
        self.pieces = [pieces]

    def start(self, order):
        own = order.tie(self.pieces[0])
        self.pieces += [swap(own, 1), swap(own, 2)]

    def relay(self, order):
        self.pieces.append(swap(order.tie(self.pieces[1]), 2))

    def all(self):
        return [Free(array) for array in self.pieces]

    def places(self):
        return (0,) * 4


class Sum:
    def __init__(self, order, group):
        self.order = order
        self.keep, self.pass_on, self.send = group

    def first(self):
        self.came = swap(self.order.tie(self.send), 1)

    def second(self):
        self.last = swap(self.order.add(self.came[1], self.pass_on), 2)

    def across_rows(self, value, distance):
        route = [(i, i ^ (2 * distance)) for i in range(lax.axis_size("dp"))]
        return lax.ppermute(value, "dp", route)

    def total(self):
        return self.order.add(self.last, self.came[0], self.keep)

    def third(self, apart=False):
        total = self.total()
        count = lax.axis_size("dp")
        self.short = count == 8 and not apart
        if self.short:
            half = total.shape[0] // 2
            odd = (lax.axis_index("dp") // 2) % 2 == 1
            self.keep = jnp.where(odd, total[half:], total[:half])
            self.came = self.across_rows(jnp.where(odd, total[:half], total[half:]), 1)
        else:
            groups = [[i for i in range(count) if i % 2 == core] for core in range(2)]
            self.keep = lax.psum(total, "dp", axis_index_groups=groups)

    def fourth(self):
        if self.short:
            self.keep = self.order.add(self.came, self.keep)
            self.came = self.across_rows(self.keep, 2)

    def fifth(self):
        if self.short:
            self.keep = self.order.add(self.came, self.keep)
            self.rest = self.across_rows(self.keep, 1)

    def sixth(self):
        if self.short:
            self.keep, self.rest = self.order.tie((self.keep, self.rest))
            self.keep_came, self.rest_came = across(self.keep), across(self.rest)
        else:
            self.keep = self.order.tie(self.keep)
            self.keep_came = across(self.keep)

    def all(self):
        if self.short:
            return self.keep, self.rest, self.keep_came, self.rest_came
        return self.keep, self.keep_came


class Delivery:
    def __init__(self, order, pieces, c, k):
        self.order, self.c, self.k = order, c, k
        pieces = order.tie(pieces)
        self.came = [pieces[0]] + [swap(pieces[r], r) for r in range(1, 4)]

    def row(self, chip):
        far, came = self.c ^ chip, self.came
        first = far == 1 + self.k
        return jnp.where(far == 0, came[0], jnp.where(first, came[1], jnp.where(far == 3, came[3], came[2])))

    def turn(self):
        k = self.k
        self.came = self.order.tie(self.came)
        self.own = jnp.concatenate([self.row(2 * k), self.row(2 * k + 1)], 0)
        other = jnp.concatenate([self.row(2 - 2 * k), self.row(3 - 2 * k)], 0)
        self.order.last = other
        self.other = across(other)

    def finish(self):
        own, other = self.own, self.order.tie(self.other)
        results = jnp.where(self.k == 0, own, other), jnp.where(self.k == 0, other, own)
        self.order.last = results[0]
        return results


def angles(places):
    freq = 10000.0 ** (-2.0 * jnp.arange(SIZE // 2, dtype=F32) / SIZE)
    phase = places.astype(F32)[:, None] * jnp.tile(freq, LOCAL)[None, :]
    return jnp.cos(phase), jnp.sin(phase)


def places_of(counts, count, unit):
    at = jnp.arange(count, dtype=jnp.int32)
    starts = unit * jnp.sum(jnp.where(jnp.arange(3)[:, None] >= jnp.arange(3)[None, :], counts[None, :3], 0), 1)
    begin = jnp.max(jnp.where(at[:, None] >= starts[None, :], starts[None, :], 0), 1)
    return at - begin


def body(
    tokens,
    lengths,
    cotangent,
    full_first_gain,
    full_project,
    full_merge,
    full_second_gain,
    full_widen,
    full_narrow,
    pool_weight,
    short_first_gain,
    short_project,
    short_merge,
    short_second_gain,
    short_widen,
    short_narrow,
    expand_weight,
):
    c = lax.axis_index("section")
    d = lax.axis_index("dp")
    k = d % 2
    rows = lengths.shape[0]
    length = tokens.shape[0] // rows
    groups = length // 3
    count = -(-length // QUARTER) * QUARTER
    short = -(-groups // 16) * 16

    here = k == c // 2
    who_k = jnp.stack([c, k]).astype(jnp.int32)
    order = Order()
    gain_rows = [
        g.reshape(1, QUARTER) for g in (full_first_gain, full_second_gain, short_first_gain, short_second_gain)
    ]
    attn_in = [((WIDTH, 3 * QUARTER), BF), ((WIDTH, QUARTER), BF), ((3 * QUARTER, WIDTH), BF)]
    pieces1, = order.call(
        pack_first_kernel, "pack_first", [((PAD + ATTN, QUARTER), BF)], None, full_project, full_merge, *gain_rows,
        scratch=attn_in + [((1, QUARTER), BF)] * 4, sems=6, space=pltpu.HBM, limit=PACK_LIMIT,
    )
    stage1 = [pieces1] + [swap(pieces1, r) for r in (1, 2, 3)]

    j = order.tie(c % 2)
    pairs = jnp.stack([lax.dynamic_index_in_dim(a.reshape(rows, length, WIDTH), j, 0, False) for a in (tokens, cotangent)])
    ends = lax.dynamic_index_in_dim(lengths, j, 0, False).astype(BF)
    ends = jnp.pad(ends, (0, WIDTH - ends.shape[0]))
    own_row = jnp.concatenate([pairs, jnp.broadcast_to(ends, (2, count - length, WIDTH))], 1)
    came_row = across(own_row)

    pieces2, pieces3, pieces4 = order.call(
        pack_rest_kernel, "pack_rest", [((n, QUARTER), BF) for n in (FFN, THIRD + ATTN + THIRD, FFN)],
        None, full_widen, full_narrow, pool_weight, short_project, short_merge, expand_weight, short_widen,
        short_narrow, scratch=attn_in, sems=26, space=pltpu.HBM, limit=PACK_LIMIT,
    )
    stage2, stage3, stage4 = (Stage(p) for p in (pieces2, pieces3, pieces4))
    stage2.start(order)
    stage3.start(order)

    counts = jnp.where(here, own_row[0, length, :SEGS], came_row[0, length, :SEGS]).astype(jnp.int32)
    odd = (d // 2) % 2 if lax.axis_size("dp") == 8 else jnp.zeros_like(d)
    who = jnp.concatenate([who_k, counts, jnp.stack([odd, odd]).astype(jnp.int32)])
    cos, sin = angles(places_of(counts, count, 3))
    short_cos, short_sin = angles(places_of(counts, short, 1))

    def block_outs(n):
        outs = [
            ((3 * HALF, WIDTH), BF, Far),
            ((HALF, WIDTH), BF, Far),
            ((n, WIDTH), BF, Far),
            ((n, HALF), BF, Far),
            ((n, HALF), BF, Far),
            ((n, HALF), BF, Far),
        ]
        return outs if n == count else [out[:2] for out in outs]

    def ffn_outs(n):
        outs = [
            ((n, WIDTH), F32, Far),
            ((n, WIDTH), BF, Far),
            ((WIDTH, HIDDEN), BF, Far),
            ((HIDDEN, WIDTH), BF, Far),
            ((n, HIDDEN), BF, Far),
            ((n, HIDDEN), BF, Far),
            ((n, WIDTH), BF),
        ]
        return outs if n == count else [out[:2] for out in outs]

    def back_outs(n):
        return [
            ((n, WIDTH), F32),
            ((n, WIDTH), BF),
            ((n, 3 * HALF), BF),
            ((n, WIDTH), BF),
            ((PAD, WIDTH), F32),
        ]

    def sent(part):
        return [((part, QUARTER), BF, Far)] * 2 + [((2, part, QUARTER), BF, Far)]

    row, gains, project, merge, first, q, key, v, att, ctx, mix = order.call(
        full_attention_kernel, "full_attention",
        [((count, WIDTH), BF), ((PAD, WIDTH), F32)] + block_outs(count)
        + [((count // QUARTER, LOCAL * QUARTER, count), BF, Far), ((count, HALF), BF, Far), ((count, WIDTH), BF)],
        who, Raw(own_row), Raw(came_row), cos, sin, *[Far(a) for a in stage1], sems=2,
    )
    mix_came = across(mix)
    stage2.relay(order)
    order.wait(stage2.pieces[2])
    stage4.start(order)
    target, grouped = order.call(
        functools.partial(target_kernel, groups), "target",
        [((count, WIDTH), BF, Far), ((short, 3 * WIDTH), BF)], who, Raw(own_row), Raw(came_row), sems=2,
    )
    stage3.relay(order)
    middle, second, widen, narrow, hidden, slope, part = order.call(
        functools.partial(ffn_kernel, 1, stage2.places()), "full_ffn", ffn_outs(count),
        who, row, mix, mix_came, gains, *stage2.all(),
    )
    part_came = across(part)
    stage4.relay(order)
    raw3 = [Raw(a) for a in stage3.pieces]
    full, pool, joined, pooled = order.call(
        functools.partial(pool_kernel, groups), "pool",
        [((count, WIDTH), BF, Far), ((3 * HALF, WIDTH), BF, Far), ((short, 3 * HALF), BF), ((short, WIDTH), BF)],
        who, Far(middle), part, part_came, *raw3, scratch=[((4, THIRD, QUARTER), BF)], sems=4,
    )
    pooled_came = across(pooled)
    expand, d_half = order.call(
        expand_back_kernel, "expand_back", [((HALF, 3 * WIDTH), BF), ((short, HALF), BF)], who, grouped, *raw3,
        scratch=[((4, THIRD, QUARTER), BF)], sems=4,
    )
    d_came = across(d_half)
    s_in, s_project, s_merge, s_first, s_q, s_key, s_v, s_att, s_ctx, s_mix = order.call(
        short_attention_kernel, "short_attention",
        [((short, WIDTH), BF)] + block_outs(short)
        + [((1, LOCAL * short, short), BF), ((short, HALF), BF), ((short, WIDTH), BF)],
        who, pooled, pooled_came, short_cos, short_sin, gains, *raw3,
        scratch=[((4, ATTN, QUARTER), BF)], sems=4,
    )
    s_mix_came = across(s_mix)
    s_middle, s_hidden, s_delta, s_narrow, s_dsecond, *group = order.call(
        short_ffn_kernel, "short_ffn",
        [((short, WIDTH), F32), ((short, HIDDEN), BF), ((short, WIDTH), BF), ((HIDDEN, WIDTH), BF), ((short, WIDTH), BF)]
        + sent(PAD + FFN),
        who, s_in, s_mix, s_mix_came, gains, *stage4.all(), d_half, d_came,
        scratch=[
            ((short, WIDTH), BF), ((WIDTH, HIDDEN), BF), ((short, HIDDEN), BF), ((PAD, WIDTH), F32),
            ((WIDTH, HIDDEN), BF), ((HIDDEN, WIDTH), BF),
        ],
    )
    sum_a = Sum(order, group)
    sum_a.first()
    s_dsecond_came = across(s_dsecond)
    s_part, = order.call(short_ffn_rest_kernel, "short_ffn_rest", [((short, WIDTH), BF)], who, s_hidden, s_narrow)
    s_part_came = across(s_part)
    s_mid, s_dmix, s_dpacked, s_dfirst, s_gain1 = order.call(
        functools.partial(attention_back_kernel, 2, 3, short), "short_attention_back", back_outs(short),
        who, s_delta, s_dsecond, s_dsecond_came, s_middle, gains, s_in, s_merge, s_project, s_q, s_key, s_v, s_att,
        short_cos, short_sin, scratch=[((short, HALF), F32)] * 2,
    )
    s_dfirst_came = across(s_dfirst)
    s_half, grown = order.call(
        functools.partial(expand_kernel, groups), "expand", [((short, HALF), BF), ((count, WIDTH), BF, Far)],
        who, s_middle, s_part, s_part_came, expand, scratch=[((short, WIDTH), BF)],
    )
    grown_came = across(grown)
    d_in, d_low = order.call(
        functools.partial(pool_back_kernel, groups), "pool_back", [((short, WIDTH), BF), ((count, HALF), BF)],
        who, s_mid, s_dfirst, s_dfirst_came, gains, s_in, Far(pool),
    )
    d_low_came = across(d_low)
    order.wait(grown_came)
    sum_b = Sum(order, order.call(
        group_b_kernel, "group_b", sent(PAD + ATTN + 2 * THIRD),
        who, s_ctx, s_dmix, s_dpacked, s_first, s_gain1, joined, d_in, s_half, grouped,
        scratch=[((3 * HALF, WIDTH), BF), ((HALF, WIDTH), BF), ((3 * HALF, WIDTH), BF), ((HALF, 3 * WIDTH), BF)],
    ))
    sum_b.first()
    sum_a.second()
    delta, low, inner, dsecond, gain2 = order.call(
        full_ffn_back_kernel, "full_ffn_back",
        [((count, WIDTH), F32), ((count, WIDTH), BF), ((count, HIDDEN), BF), ((count, WIDTH), BF), ((PAD, WIDTH), F32)],
        who, Far(target), d_low, d_low_came, Far(middle), gains, Far(slope), Far(widen), Far(narrow),
    )
    dsecond_came = across(dsecond)
    sum_c = Sum(order, order.call(
        ffn_group_kernel, "group_c", sent(PAD + FFN), who, Far(hidden), low, Far(second), inner, gain2,
        scratch=[((WIDTH, HIDDEN), BF), ((HIDDEN, WIDTH), BF)],
    ))
    sum_a.third()
    sum_b.second()
    sum_a.fourth()
    sum_c.first()
    mid, dmix, dpacked, dfirst, gain1 = order.call(
        functools.partial(attention_back_kernel, 0, 1, QUARTER), "full_attention_back", back_outs(count),
        who, delta, dsecond, dsecond_came, Far(middle), gains, row, Far(merge), Far(project), Far(q), Far(key), Far(v),
        Far(att), cos, sin, scratch=[((count, HALF), F32)] * 2,
    )
    dfirst_came = across(dfirst)
    sum_b.third()
    sum_d = Sum(order, order.call(
        attn_group_kernel, "group_d", sent(PAD + ATTN), who, Far(ctx), dmix, dpacked, Far(first), gain1,
        scratch=[((3 * HALF, WIDTH), BF), ((HALF, WIDTH), BF)],
    ))
    sum_c.second()
    sum_d.first()
    sent_rows = order.call(
        outputs_kernel, "outputs", [((length, QUARTER), BF)] * 4,
        who, Far(full), Far(grown), grown_came, mid, dfirst, dfirst_came, gains, row, scratch=[((count, WIDTH), BF)],
    )


    gain_out = ((1, QUARTER), F32)
    ffn_out = [((WIDTH, WIDTH), F32), ((4 * WIDTH, QUARTER), F32)]
    attn_out = [((WIDTH, 3 * QUARTER), F32), ((WIDTH, QUARTER), F32)]
    turned = [((3 * QUARTER, WIDTH), F32)]

    def spread(kernel, name, outs, total, **options):
        outs = [(*out, Far) for out in outs]
        how = spread_either if total.short else spread_whole
        return order.call(functools.partial(how, kernel), name, outs, who, *total.all(), **options)

    sum_a.fifth()
    sum_b.fourth()
    sum_d.second()
    sum_c.third()
    sum_d.third()
    sum_a.sixth()
    sum_c.fourth()
    sum_b.fifth()
    sum_d.fourth()
    g_s2, g_s_widen, g_s_narrow = spread(spread_ffn_kernel, "spread_a", [gain_out] + ffn_out, sum_a)
    sum_c.fifth()
    sum_d.fifth()
    delivery = Delivery(order, sent_rows, c, k)
    sum_c.sixth()
    sum_d.sixth()
    sum_b.sixth()
    g_s1, g_s_project, g_s_merge, g_pool, g_expand = spread(
        spread_b_kernel, "spread_b",
        [gain_out] + attn_out + [((3 * WIDTH, QUARTER), F32), ((WIDTH, 3 * QUARTER), F32)], sum_b, scratch=turned,
    )
    delivery.turn()
    g_f2, g_widen, g_narrow = spread(spread_ffn_kernel, "spread_c", [gain_out] + ffn_out, sum_c)
    g_f1, g_project, g_merge = spread(spread_attn_kernel, "spread_d", [gain_out] + attn_out, sum_d, scratch=turned)
    mixed_out, token_gradient = delivery.finish()

    return (
        mixed_out,
        token_gradient,
        g_f1.reshape(-1),
        g_project,
        g_merge,
        g_f2.reshape(-1),
        g_widen,
        g_narrow,
        g_pool,
        g_s1.reshape(-1),
        g_s_project,
        g_s_merge,
        g_s2.reshape(-1),
        g_s_widen,
        g_s_narrow,
        g_expand,
    )


def solution(mesh):
    in_specs = (
        P("dp", None),
        P("dp", None),
        P("dp", None),
        P("section"),
        P(None, "section"),
        P(None, "section"),
        P("section"),
        P(None, "section"),
        P(None, "section"),
        P(None, "section"),
        P("section"),
        P(None, "section"),
        P(None, "section"),
        P("section"),
        P(None, "section"),
        P(None, "section"),
        P(None, "section"),
    )
    out_specs = (
        P("dp", "section"),
        P("dp", "section"),
        P("section"),
        P(None, "section"),
        P(None, "section"),
        P("section"),
        P(None, "section"),
        P(None, "section"),
        P(None, "section"),
        P("section"),
        P(None, "section"),
        P(None, "section"),
        P("section"),
        P(None, "section"),
        P(None, "section"),
        P(None, "section"),
    )
    return jax.shard_map(body, mesh=mesh, in_specs=in_specs, out_specs=out_specs, check_vma=False)
```

```python
import functools

import jax
import jax.numpy as jnp
from jax import lax
from jax.experimental import pallas as pl
from jax.experimental.pallas import tpu as pltpu
from jax.sharding import PartitionSpec as P


WIDTH = 512
QUARTER = 128
HALF = 256
HIDDEN = 1024
SEGS = 4
LOCAL = 4
SIZE = 64
EPS = 1e-05
NEG = -1e30

BF = jnp.bfloat16
F32 = jnp.float32

ATTN = 1024
FFN = 2048
THIRD = 768
PAD = 32
VMEM_LIMIT = 16 * 2**20
PACK_LIMIT = 60 * 2**20


def nn(left, right):
    return lax.dot_general(left, right, (((1,), (0,)), ((), ())), preferred_element_type=F32)


def nt(left, right):
    return lax.dot_general(left, right, (((1,), (1,)), ((), ())), preferred_element_type=F32)


def tn(left, right):
    return lax.dot_general(left, right, (((0,), (0,)), ((), ())), preferred_element_type=F32)


def lanes(start, count=QUARTER):
    return pl.ds(pl.multiple_of(start, QUARTER), count)


def rows_at(start, count, unit):
    return pl.ds(pl.multiple_of(start, unit), count)


def iota(shape, dim):
    return lax.broadcasted_iota(jnp.int32, shape, dim)


def standard(states):
    center = states - jnp.mean(states, -1, keepdims=True)
    inverse = lax.rsqrt(jnp.mean(center * center, -1, keepdims=True) + EPS)
    return center * inverse, inverse


def norm_back(delta, normed, inverse):
    return inverse * (
        delta
        - jnp.mean(delta, -1, keepdims=True)
        - normed * jnp.mean(delta * normed, -1, keepdims=True)
    )


def gelu_parts(x):
    z = x * 0.7071067811865476
    t = 1.0 / (1.0 + 0.3275911 * jnp.abs(z))
    e = jnp.exp(-z * z)
    poly = t * (
        0.127414796
        + t * (-0.142248368 + t * (0.7107068705 + t * (-0.7265760135 + t * 0.5307027145)))
    )
    tail = poly * e
    phi = jnp.where(z >= 0, 1.0 - tail, tail)
    return x * phi, phi + x * e * 0.3989422804014327


def chips(who):
    c, k = who[0], who[1]
    return c, c ^ (1 + k), c ^ (2 - k), c ^ 3


def reader(refs, places):
    def read(r, at, rows):
        return refs[r][places[r] + at : places[r] + at + rows, :]

    return read


def writer(*refs):
    def write(r, at, value):
        refs[r][at : at + value.shape[0], :] = value

    return write


def pair_rows(pair):
    is_value = pair >= 8
    first = jnp.where(is_value, 512 + 64 * (pair - 8), 256 * (pair >> 2) + 32 * (pair & 3))
    second = jnp.where(is_value, first + 32, first + 128)
    return first, second


def pack_attn(k, turned, merge, put, base):
    for p in range(3):
        chunk = turned[rows_at(128 * p + 64 * k, 64, 64), :]
        for j in range(4):
            put(base + j * 192 + p * 64, chunk[:, 128 * j : 128 * j + 128])
    for pair in range(4):
        put(base + 768 + pair * 64, merge[rows_at(128 * pair + 64 * k, 64, 64), :])


def unpack_attn(who, read, base, project, merge):
    for r, q in enumerate(chips(who)):
        for p in range(3):
            first, second = pair_rows(3 * q + p)
            for j in range(4):
                block = read(r, base + j * 192 + p * 64, 64)
                project[rows_at(first, 32, 32), 128 * j : 128 * j + 128] = block[:32]
                project[rows_at(second, 32, 32), 128 * j : 128 * j + 128] = block[32:]
        for pair in range(4):
            merge[64 * pair : 64 * pair + 64, lanes(128 * q)] = read(r, base + 768 + pair * 64, 64)


def regroup_attn(who, write, base, project, merge):
    for r, q in enumerate(chips(who)):
        for p in range(3):
            first, second = pair_rows(3 * q + p)
            for j in range(4):
                at = base + j * 192 + p * 64
                write(r, at, project[rows_at(first, 32, 32), 128 * j : 128 * j + 128])
                write(r, at + 32, project[rows_at(second, 32, 32), 128 * j : 128 * j + 128])
        for pair in range(4):
            write(r, base + 768 + pair * 64, merge[64 * pair : 64 * pair + 64, lanes(128 * q)])


def pack_ffn(k, widen, narrow, put):
    for lc in range(2):
        put(512 * lc, widen.at[:, lanes(256 * k + 128 * lc)])
    for qq in range(4):
        put(1024 + 256 * qq, narrow.at[rows_at(512 * qq + 256 * k, 256, 256), :])


def unpack_ffn(who, read, widen, narrow):
    for r, q in enumerate(chips(who)):
        for lc in range(2):
            widen[:, lanes(256 * q + 128 * lc)] = read(r, 512 * lc, 512)
        narrow[:, lanes(128 * q)] = read(r, 1024, 1024)


def regroup_ffn(who, write, base, widen, narrow):
    for r, q in enumerate(chips(who)):
        for lc in range(2):
            write(r, base + 512 * lc, widen[:, lanes(256 * q + 128 * lc)])
        write(r, base + 1024, narrow[:, lanes(128 * q)])


def pack_pool(k, pool, put, base):
    for i in range(6):
        put(base + i * 128, pool.at[rows_at(512 * (i // 2) + 256 * k + 128 * (i % 2), 128, 128), :])


def unpack_pool(who, read, base, pool):
    for r, q in enumerate(chips(who)):
        for i in range(6):
            pool[128 * i : 128 * i + 128, lanes(128 * q)] = read(r, base + i * 128, 128)


def regroup_pool(who, write, base, pool):
    for r, q in enumerate(chips(who)):
        for i in range(6):
            write(r, base + i * 128, pool[128 * i : 128 * i + 128, lanes(128 * q)])


def pack_expand(k, expand, put, base):
    for i in range(6):
        put(base + i * 128, expand.at[rows_at(256 * k + 128 * (i % 2), 128, 128), pl.ds(128 * (i // 2), 128)])


def unpack_expand(who, read, base, expand):
    for r, q in enumerate(chips(who)):
        for i in range(6):
            block = read(r, base + i * 128, 128)
            expand[128 * (i % 2) : 128 * (i % 2) + 128, lanes(384 * q + 128 * (i // 2))] = block


def regroup_expand(who, write, base, expand):
    for r, q in enumerate(chips(who)):
        for i in range(6):
            block = expand[128 * (i % 2) : 128 * (i % 2) + 128, lanes(384 * q + 128 * (i // 2))]
            write(r, base + i * 128, block)


def regroup_gain(who, write, gain):
    for r, q in enumerate(chips(who)):
        write(r, 0, gain[:, lanes(128 * q)].astype(BF))


class Copies:
    def __init__(self, sems):
        self.sems, self.all = sems, []

    def start(self, source, target):
        copy = pltpu.make_async_copy(source, target, self.sems.at[len(self.all)])
        copy.start()
        self.all.append(copy)

    def putter(self, ref):
        def put(at, source):
            self.start(source, ref.at[pl.ds(at, source.shape[0]), :])

        return put

    def wait(self):
        for copy in self.all:
            copy.wait()


def putter(ref):
    def put(at, value):
        ref[at : at + value.shape[0], :] = value

    return put


def core():
    return lax.rem(lax.axis_index("dp"), 2)


def pack_first_kernel(project, merge, g0, g1, g2, g3, out, project_in, merge_in, turned, i0, i1, i2, i3, sems):
    copies = Copies(sems)
    copies.start(project, project_in)
    copies.start(merge, merge_in)
    inside = (i0, i1, i2, i3)
    for gain, place in zip((g0, g1, g2, g3), inside):
        copies.start(gain, place)
    copies.wait()
    row = iota((PAD, QUARTER), 0)
    gains = jnp.zeros((PAD, QUARTER), F32)
    for i, place in enumerate(inside):
        gains = jnp.where(row == i, place[...].astype(F32), gains)
    out[0:PAD, :] = gains.astype(BF)
    turned[...] = jnp.swapaxes(project_in[...], 0, 1)
    pack_attn(core(), turned, merge_in, putter(out), PAD)


def pack_rest_kernel(
    widen, narrow, pool, project, merge, expand, s_widen, s_narrow, out2, out3, out4, project_in, merge_in, turned, sems
):
    k = core()
    copies, last = Copies(sems), Copies(sems.at[pl.ds(2, 24)])
    copies.start(project, project_in)
    copies.start(merge, merge_in)
    pack_ffn(k, widen, narrow, last.putter(out2))
    pack_pool(k, pool, last.putter(out3), 0)
    pack_expand(k, expand, last.putter(out3), THIRD + ATTN)
    pack_ffn(k, s_widen, s_narrow, last.putter(out4))
    copies.wait()
    turned[...] = jnp.swapaxes(project_in[...], 0, 1)
    pack_attn(k, turned, merge_in, putter(out3), THIRD)
    last.wait()


def ends_of(who):
    e0 = who[2]
    e1 = e0 + who[3]
    e2 = e1 + who[4]
    return e0, e1, e2, e2 + who[5]


def segment_of(who, index, unit):
    return sum((index >= unit * end).astype(jnp.int32) for end in ends_of(who))


def head_masks():
    lane = iota((1, HALF), 1)
    turned = [((lane & 127) >> 5 == h).astype(F32).astype(BF) for h in range(LOCAL)]
    plain = [((lane >> 6) == h).astype(F32).astype(BF) for h in range(LOCAL)]
    return turned, plain


def attention_forward(who, states, gain, cos, sin, project, merge, first, q, k, v, att, ctx, mix, unit, block):
    count = states.shape[0]
    normed, _ = standard(states)
    start = (normed * gain).astype(BF)
    first[...] = start
    packed = nt(start, project[...])
    cosine, sine = cos[...], sin[...]
    for ref, at in ((q, 0), (k, 256)):
        a, b = packed[:, at : at + 128], packed[:, at + 128 : at + 256]
        ref[:, 0:128] = (a * cosine - b * sine).astype(BF)
        ref[:, 128:256] = (b * cosine + a * sine).astype(BF)
    v[...] = packed[:, 512:768].astype(BF)
    turned, plain = head_masks()
    scale = jnp.asarray(SIZE**-0.5, BF)
    for b in range(count // block):
        low, stop = b * block, (b + 1) * block
        at_row = low + iota((block, 1), 0)
        at_col = iota((1, stop), 1)
        allowed = (segment_of(who, at_row, unit) == segment_of(who, at_col, unit)) & (at_row >= at_col)
        queries = q[low:stop, :] * scale
        keys, values = k[0:stop, :], v[0:stop, :]
        total_context = jnp.zeros((block, HALF), F32)
        for h in range(LOCAL):
            scores = jnp.where(allowed, nt(queries * turned[h], keys), NEG)
            powered = jnp.exp(scores - jnp.max(scores, -1, keepdims=True))
            attend = (powered * (1.0 / jnp.sum(powered, -1, keepdims=True))).astype(BF)
            att[b, h * block : (h + 1) * block, 0:stop] = attend
            total_context = total_context + nn(attend, values * plain[h])
        ctx[low:stop, :] = total_context.astype(BF)
    mix[...] = nn(ctx[...], merge[...]).astype(BF)


def full_attention_kernel(
    who, own, came, cos, sin, s, x, y, d, row, gains, project, merge, first, q, k, v, att, ctx, mix, sems
):
    c = who[0]
    here = who[1] == c >> 1
    for i, (source, taken) in enumerate(((own, here), (came, jnp.logical_not(here)))):

        @pl.when(taken)
        def _():
            copy = pltpu.make_async_copy(source.at[0], row, sems.at[i])
            copy.start()
            copy.wait()

    read = reader((s, x, y, d), (0,) * 4)
    for r, chip in enumerate(chips(who)):
        gains[:, lanes(128 * chip)] = read(r, 0, PAD).astype(F32)
    unpack_attn(who, read, PAD, project, merge)
    states = row[...].astype(F32)
    attention_forward(
        who, states, gains[0:1, :], cos, sin, project, merge, first, q, k, v, att, ctx, mix, 3, QUARTER
    )


def short_attention_kernel(
    who, own, came, cos, sin, gains, s, x, y, d, states, project, merge, first, q, k, v, att, ctx, mix, box, sems
):
    unpack_attn(who, boxed((s, x, y, d), THIRD, box, sems), 0, project, merge)
    states[...] = (own[...].astype(F32) + came[...].astype(F32)).astype(BF)
    attention_forward(
        who, states[...].astype(F32), gains[2:3, :], cos, sin, project, merge, first, q, k, v, att, ctx, mix,
        1, own.shape[0],
    )


def ffn_kernel(
    gain_row, places, who, states, own, came, gains, s, x, y, d, middle, second, widen, narrow, hidden, slope, out
):
    unpack_ffn(who, reader((s, x, y, d), places), widen, narrow)
    mid = states[...].astype(F32) + (own[...].astype(F32) + came[...].astype(F32))
    middle[...] = mid
    normed, _ = standard(mid)
    start = (normed * gains[gain_row : gain_row + 1, :]).astype(BF)
    second[...] = start

    @pl.loop(0, 4)
    def _(i):
        cols = lanes(HALF * i, HALF)
        value, back = gelu_parts(nn(second[...], widen[:, cols]))
        hidden[:, cols] = value.astype(BF)
        slope[:, cols] = back.astype(BF)

    out[...] = nn(hidden[...], narrow[...]).astype(BF)


def join_masks(who, groups, count, real):
    g = iota((groups, 1), 0)
    t = iota((1, count), 1)
    ends = ends_of(who)
    keep = (g != ends[0]) & (g != ends[1]) & (g != ends[2]) & (g < real)
    return [
        jnp.where((t == 3 * g - 2) & keep, 1.0, 0.0).astype(BF),
        jnp.where((t == 3 * g - 1) & keep, 1.0, 0.0).astype(BF),
        jnp.where((t == 3 * g) & (g < real), 1.0, 0.0).astype(BF),
    ]


def group_masks(groups, count, real):
    g = iota((groups, 1), 0)
    t = iota((1, count), 1)
    return [jnp.where((t == 3 * g + i) & (g < real), 1.0, 0.0).astype(BF) for i in range(3)]


def boxed(refs, at, box, sems):
    copies = Copies(sems)
    for r, ref in enumerate(refs):
        copies.start(ref.at[pl.ds(at, box.shape[1]), :], box.at[r])
    copies.wait()

    def read(r, at, rows):
        return box[r, at : at + rows, :]

    return read


def pool_kernel(real, who, middle, own, came, s, x, y, d, full, pool, joined, out, box, sems):
    unpack_pool(who, boxed((s, x, y, d), 0, box, sems), 0, pool)
    full[...] = (middle[...] + (own[...].astype(F32) + came[...].astype(F32))).astype(BF)
    part = full[:, lanes(HALF * who[1], HALF)]
    for j, mask in enumerate(join_masks(who, joined.shape[0], full.shape[0], real)):
        joined[:, HALF * j : HALF * j + HALF] = nn(mask, part).astype(BF)
    out[...] = nn(joined[...], pool[...]).astype(BF)


def target_kernel(real, who, own, came, target, grouped, sems):
    here = who[1] == who[0] >> 1
    for i, (source, taken) in enumerate(((own, here), (came, jnp.logical_not(here)))):

        @pl.when(taken)
        def _():
            copy = pltpu.make_async_copy(source.at[1], target, sems.at[i])
            copy.start()
            copy.wait()

    live = segment_of(who, iota((target.shape[0], 1), 0), 3) < 3
    target[...] = jnp.where(live, target[...].astype(F32), 0.0).astype(BF)
    for i, mask in enumerate(group_masks(grouped.shape[0], target.shape[0], real)):
        grouped[:, WIDTH * i : WIDTH * i + WIDTH] = nn(mask, target[...]).astype(BF)


def expand_back_kernel(who, grouped, s, x, y, d, expand, out, box, sems):
    unpack_expand(who, boxed((s, x, y, d), THIRD + ATTN, box, sems), 0, expand)
    out[...] = nt(grouped[...], expand[...]).astype(BF)


def expand_kernel(real, who, middle, own, came, expand, part, out, short):
    k = who[1]
    short[...] = (middle[...] + (own[...].astype(F32) + came[...].astype(F32))).astype(BF)
    part[...] = short[:, lanes(HALF * k, HALF)]
    grown = nn(part[...], expand[...]).astype(BF)
    total = jnp.zeros(out.shape, F32)
    for i, mask in enumerate(group_masks(part.shape[0], out.shape[0], real)):
        total = total + tn(mask, grown[:, WIDTH * i : WIDTH * i + WIDTH])
    out[...] = total.astype(BF)


def ffn_back(gain_row, delta, middle, gains, slope, widen, narrow, inner, out, gain):
    total = jnp.zeros(middle.shape, F32)
    for i in range(4):
        cols = slice(HALF * i, HALF * i + HALF)
        value = (nt(delta, narrow[cols, :]) * slope[:, cols].astype(F32)).astype(BF)
        inner[:, cols] = value
        total = total + nt(value, widen[:, cols])
    normed, _ = standard(middle[...])
    out[...] = total.astype(BF)
    gain[...] = jnp.broadcast_to(jnp.sum(total * normed, 0, keepdims=True), gain.shape)


def full_ffn_back_kernel(
    who, target, own, came, middle, gains, slope, widen, narrow, delta, low, inner, out, gain
):
    k = who[1]
    delta[:, lanes(HALF * k, HALF)] = own[...].astype(F32)
    delta[:, lanes(HALF * (1 - k), HALF)] = came[...].astype(F32)
    delta[...] = delta[...] + target[...].astype(F32)
    low[...] = delta[...].astype(BF)
    ffn_back(1, low[...], middle, gains, slope, widen, narrow, inner, out, gain)


def attention_back_kernel(
    first_row, second_row, block, who, delta, own, came, middle, gains, states, merge, project, q, k, v, att, cos, sin,
    mid, mix, packed, out, gain, dk, dv,
):
    count = middle.shape[0]
    normed, inverse = standard(middle[...])
    dsecond = own[...].astype(F32) + came[...].astype(F32)
    dmid = delta[...].astype(F32) + norm_back(dsecond * gains[second_row : second_row + 1, :], normed, inverse)
    mid[...] = dmid
    low = dmid.astype(BF)
    mix[...] = low
    dctx = nt(low, merge[...]).astype(BF)
    turned, plain = head_masks()
    scale = SIZE**-0.5
    cosine, sine = cos[...], sin[...]
    dk[...] = jnp.zeros(dk.shape, F32)
    dv[...] = jnp.zeros(dv.shape, F32)
    for b in range(count // block):
        start, stop = b * block, (b + 1) * block
        keys, values = k[0:stop, :], v[0:stop, :]
        queries = q[start:stop, :]
        dcontext = dctx[start:stop, :]
        dq = jnp.zeros((block, HALF), F32)
        for h in range(LOCAL):
            dhead = dcontext * plain[h]
            low_attend = att[b, h * block : (h + 1) * block, 0:stop]
            attend = low_attend.astype(F32)
            dattend = nt(dhead, values)
            dscores = attend * (dattend - jnp.sum(attend * dattend, -1, keepdims=True))
            dscores = (dscores * scale).astype(BF)
            dq = dq + nn(dscores, keys * turned[h])
            dk[0:stop, :] += tn(dscores, queries * turned[h])
            dv[0:stop, :] += tn(low_attend, dhead)
        a, c = dq[:, 0:128], dq[:, 128:256]
        packed[start:stop, 0:128] = (a * cosine[start:stop] + c * sine[start:stop]).astype(BF)
        packed[start:stop, 128:256] = (c * cosine[start:stop] - a * sine[start:stop]).astype(BF)
    a, c = dk[:, 0:128], dk[:, 128:256]
    packed[:, 256:384] = (a * cosine + c * sine).astype(BF)
    packed[:, 384:512] = (c * cosine - a * sine).astype(BF)
    packed[:, 512:768] = dv[...].astype(BF)
    dfirst = nn(packed[...], project[...])
    out[...] = dfirst.astype(BF)
    normed_one, _ = standard(states[...].astype(F32))
    gain[...] = jnp.broadcast_to(jnp.sum(dfirst * normed_one, 0, keepdims=True), gain.shape)


def input_gradient(gain_row, mid, own, came, gains, states):
    normed, inverse = standard(states[...].astype(F32))
    dfirst = own[...].astype(F32) + came[...].astype(F32)
    return mid[...] + norm_back(dfirst * gains[gain_row : gain_row + 1, :], normed, inverse)


def pool_back_kernel(real, who, mid, own, came, gains, states, pool, delta, out):
    delta[...] = input_gradient(2, mid, own, came, gains, states).astype(BF)
    djoined = nt(delta[...], pool[...]).astype(BF)
    total = jnp.zeros(out.shape, F32)
    for j, mask in enumerate(join_masks(who, delta.shape[0], out.shape[0], real)):
        total = total + tn(mask, djoined[:, HALF * j : HALF * j + HALF])
    out[...] = total.astype(BF)


def outputs_kernel(who, full, grown, grown_came, mid, own, came, gains, states, o0, o1, o2, o3, whole):
    @pl.when(who[1] == 0)
    def _():
        whole[...] = (full[...].astype(F32) + (grown[...].astype(F32) + grown_came[...].astype(F32))).astype(BF)

    @pl.when(who[1] != 0)
    def _():
        whole[...] = input_gradient(0, mid, own, came, gains, states).astype(BF)

    for q, out in zip(chips(who), (o0, o1, o2, o3)):
        out[...] = whole[0 : out.shape[0], lanes(128 * q)]


def ffn_weights(who, write, hidden, delta, second, inner, gain, dwiden, dnarrow):
    dnarrow[...] = tn(hidden[...], delta[...]).astype(BF)
    dwiden[...] = tn(second[...], inner[...]).astype(BF)
    regroup_gain(who, write, gain)
    regroup_ffn(who, write, PAD, dwiden, dnarrow)


def attn_weights(who, write, ctx, mix, packed, first, gain, dproject, dmerge):
    dproject[...] = tn(packed[...], first[...]).astype(BF)
    dmerge[...] = tn(ctx[...], mix[...]).astype(BF)
    regroup_gain(who, write, gain)
    regroup_attn(who, write, PAD, dproject, dmerge)


def group_b_kernel(
    who, ctx, mix, packed, first, gain, joined, delta, part, grouped, keep, send, pass_on, relay, dproject, dmerge, dpool, dexpand
):
    write = writer(keep, send, pass_on, relay)
    attn_weights(who, write, ctx, mix, packed, first, gain, dproject, dmerge)
    dpool[...] = tn(joined[...], delta[...]).astype(BF)
    regroup_pool(who, write, PAD + ATTN, dpool)
    dexpand[...] = tn(part[...], grouped[...]).astype(BF)
    regroup_expand(who, write, PAD + ATTN + THIRD, dexpand)


def short_ffn_kernel(
    who, states, own, came, gains, s, x, y, d, d_own, d_came, middle, hidden, delta, narrow, dsecond,
    keep, send, pass_on, relay, second, widen, inner, gain, dwiden, dnarrow,
):
    k = who[1]
    unpack_ffn(who, reader((s, x, y, d), (0,) * 4), widen, narrow)
    mid = states[...].astype(F32) + (own[...].astype(F32) + came[...].astype(F32))
    middle[...] = mid
    normed, _ = standard(mid)
    second[...] = (normed * gains[3:4, :]).astype(BF)
    delta[:, lanes(HALF * k, HALF)] = d_own[...]
    delta[:, lanes(HALF * (1 - k), HALF)] = d_came[...]
    for i in range(4):
        cols = slice(HALF * i, HALF * i + HALF)
        value, back = gelu_parts(nn(second[...], widen[:, cols]))
        hidden[:, cols] = value.astype(BF)
        inner[:, cols] = (nt(delta[...], narrow[cols, :]) * back).astype(BF)
    total = nt(inner[...], widen[...])
    dsecond[...] = total.astype(BF)
    gain[...] = jnp.broadcast_to(jnp.sum(total * normed, 0, keepdims=True), gain.shape)
    ffn_weights(who, writer(keep, send, pass_on, relay), hidden, delta, second, inner, gain, dwiden, dnarrow)


def short_ffn_rest_kernel(who, hidden, narrow, out):
    out[...] = nn(hidden[...], narrow[...]).astype(BF)


def ffn_group_kernel(who, hidden, delta, second, inner, gain, keep, send, pass_on, relay, dwiden, dnarrow):
    ffn_weights(who, writer(keep, send, pass_on, relay), hidden, delta, second, inner, gain, dwiden, dnarrow)


def attn_group_kernel(who, ctx, mix, packed, first, gain, keep, send, pass_on, relay, dproject, dmerge):
    attn_weights(who, writer(keep, send, pass_on, relay), ctx, mix, packed, first, gain, dproject, dmerge)


class Halves:
    def __init__(self, first, second, start=0):
        self.first, self.second, self.half, self.start = first, second, first.shape[0], start

    def after(self, rows):
        return Halves(self.first, self.second, self.start + rows)

    def read(self, at, rows):
        at = at + self.start
        stop = at + rows
        if stop <= self.half:
            return self.first[at:stop, :].astype(F32)
        if at >= self.half:
            return self.second[at - self.half : stop - self.half, :].astype(F32)
        parts = (self.first[at : self.half, :], self.second[0 : stop - self.half, :])
        return jnp.concatenate([part.astype(F32) for part in parts], 0)


def both(who, own, came):
    return ((who[1], own.read), (1 - who[1], came.read))


def spread_gain(own, came, gain):
    gain[...] = own.read(0, 8)[0:1] + came.read(0, 8)[0:1]


def spread_ffn(who, own, came, widen, narrow):
    for k, read in both(who, own, came):
        for lc in range(2):
            widen[:, lanes(256 * k + 128 * lc)] = read(PAD + 512 * lc, 512)
        for qq in range(4):
            narrow[rows_at(512 * qq + 256 * k, 256, 256), :] = read(PAD + 1024 + 256 * qq, 256)


def spread_attn(who, own, came, project, merge, turned):
    for k, read in both(who, own, came):
        for j in range(4):
            for p in range(3):
                block = read(PAD + j * 192 + p * 64, 64)
                turned[rows_at(128 * p + 64 * k, 64, 64), 128 * j : 128 * j + 128] = block
        for pair in range(4):
            merge[rows_at(128 * pair + 64 * k, 64, 64), :] = read(PAD + 768 + pair * 64, 64)
    project[...] = jnp.swapaxes(turned[...], 0, 1)


def spread_whole(kernel, who, own, came, *outs):
    half = own.shape[0] // 2
    kernel(who, *[Halves(*[ref.at[pl.ds(half * i, half), :] for i in range(2)]) for ref in (own, came)], *outs)


def spread_either(kernel, who, keep, rest, keep_came, rest_came, *outs):
    @pl.when(who[6] == 0)
    def _():
        kernel(who, Halves(keep, rest), Halves(keep_came, rest_came), *outs)

    @pl.when(who[6] != 0)
    def _():
        kernel(who, Halves(rest, keep), Halves(rest_came, keep_came), *outs)


def spread_b_kernel(who, own, came, gain, project, merge, pool, expand, turned):
    spread_gain(own, came, gain)
    spread_attn(who, own, came, project, merge, turned)
    for k, read in both(who, own, came):
        for i in range(6):
            pool[rows_at(512 * (i // 2) + 256 * k + 128 * (i % 2), 128, 128), :] = read(PAD + ATTN + i * 128, 128)
            block = read(PAD + ATTN + THIRD + i * 128, 128)
            expand[rows_at(256 * k + 128 * (i % 2), 128, 128), 128 * (i // 2) : 128 * (i // 2) + 128] = block


def spread_ffn_kernel(who, own, came, gain, widen, narrow):
    spread_gain(own, came, gain)
    spread_ffn(who, own, came, widen, narrow)


def spread_attn_kernel(who, own, came, gain, project, merge, turned):
    spread_gain(own, came, gain)
    spread_attn(who, own, came, project, merge, turned)


class Far:
    def __init__(self, array):
        self.array = array


class Free(Far):
    pass


class Raw(Far):
    pass


def call(kernel, name, outs, who, *args, scratch=(), sems=0, space=pltpu.VMEM, limit=VMEM_LIMIT):
    whole = pl.BlockSpec(memory_space=pltpu.VMEM)
    whos = [] if who is None else [who]
    spaces = [
        None if isinstance(a, (Raw, Free)) else pltpu.HBM if isinstance(a, Far) or space == pltpu.HBM else None
        for a in args
    ]
    kinds = [pl.ANY if isinstance(a, Raw) else space for a in args]
    args = [a.array if isinstance(a, Far) else a for a in args]
    return pl.pallas_call(
        kernel,
        name=name,
        out_shape=[(pltpu.HBM if far else pltpu.VMEM)(shape, dtype) for shape, dtype, *far in outs],
        in_specs=[pl.BlockSpec(memory_space=pltpu.SMEM)] * len(whos) + [pl.BlockSpec(memory_space=kind) for kind in kinds],
        out_specs=[whole] * len(outs),
        scratch_shapes=[pltpu.VMEM(shape, dtype) for shape, dtype in scratch]
        + ([pltpu.SemaphoreType.DMA((sems,))] if sems else []),
        compiler_params=pltpu.CompilerParams(vmem_limit_bytes=limit),
        cost_estimate=pl.CostEstimate(flops=1024, bytes_accessed=1024, transcendentals=0),
    )(*whos, *[a if place is None else pltpu.with_memory_space_constraint(a, place) for a, place in zip(args, spaces)])


def swap(value, role):
    count = lax.axis_size("dp")
    route = []
    for chip in range(lax.axis_size("section")):
        for d in range(count):
            distance = (0, 1 + d % 2, 2 - d % 2, 3)[role]
            route.append((chip * count + d, (chip ^ distance) * count + d))
    return lax.ppermute(value, ("section", "dp"), route)


def across(value):
    return lax.ppermute(value, "dp", [(i, i ^ 1) for i in range(lax.axis_size("dp"))])


class Order:
    def __init__(self):
        self.last = None

    def tie(self, value, *others):
        others = [o for o in (self.last, *others) if o is not None]
        return lax.optimization_barrier((value, others))[0] if others else value

    def wait(self, *values):
        self.last = lax.optimization_barrier((self.last, values))[0]

    def call(self, kernel, name, outs, who, *args, **options):
        results = call(kernel, name, outs, None if who is None else self.tie(who), *args, **options)
        self.last = results[-1]
        return results

    def add(self, first, *others):
        total = self.tie(first)
        for other in others:
            total = total + other
        self.last = total
        return total


class Stage:
    def __init__(self, pieces):
        self.pieces = [pieces]

    def start(self, order):
        own = order.tie(self.pieces[0])
        self.pieces += [swap(own, 1), swap(own, 2)]

    def relay(self, order):
        self.pieces.append(swap(order.tie(self.pieces[1]), 2))

    def all(self):
        return [Free(array) for array in self.pieces]

    def places(self):
        return (0,) * 4


class Sum:
    def __init__(self, order, group):
        self.order = order
        self.keep, self.send, self.pass_on, self.relay = group

    def first(self):
        self.relayed = swap(self.order.tie(self.relay), 1)
        self.came = swap(self.order.tie(self.send), 1)

    def second(self):
        self.last = swap(self.order.add(self.relayed, self.pass_on), 2)

    def across_rows(self, value, distance):
        route = [(i, i ^ (2 * distance)) for i in range(lax.axis_size("dp"))]
        return lax.ppermute(value, "dp", route)

    def total(self):
        return self.order.add(self.last, self.came, self.keep)

    def third(self, apart=False):
        total = self.total()
        count = lax.axis_size("dp")
        self.short = count == 8 and not apart
        if self.short:
            half = total.shape[0] // 2
            odd = (lax.axis_index("dp") // 2) % 2 == 1
            self.keep = jnp.where(odd, total[half:], total[:half])
            self.came = self.across_rows(jnp.where(odd, total[:half], total[half:]), 1)
        else:
            groups = [[i for i in range(count) if i % 2 == core] for core in range(2)]
            self.keep = lax.psum(total, "dp", axis_index_groups=groups)

    def fourth(self):
        if self.short:
            self.keep = self.order.add(self.came, self.keep)
            self.came = self.across_rows(self.keep, 2)

    def fifth(self):
        if self.short:
            self.keep = self.order.add(self.came, self.keep)
            self.rest = self.across_rows(self.keep, 1)

    def sixth(self):
        if self.short:
            self.keep, self.rest = self.order.tie((self.keep, self.rest))
            self.keep_came, self.rest_came = across(self.keep), across(self.rest)
        else:
            self.keep = self.order.tie(self.keep)
            self.keep_came = across(self.keep)

    def all(self):
        if self.short:
            return self.keep, self.rest, self.keep_came, self.rest_came
        return self.keep, self.keep_came


class Delivery:
    def __init__(self, order, pieces, c, k):
        self.order, self.c, self.k = order, c, k
        pieces = order.tie(pieces)
        self.came = [pieces[0]] + [swap(pieces[r], r) for r in range(1, 4)]

    def row(self, chip):
        far, came = self.c ^ chip, self.came
        first = far == 1 + self.k
        return jnp.where(far == 0, came[0], jnp.where(first, came[1], jnp.where(far == 3, came[3], came[2])))

    def turn(self):
        k = self.k
        self.came = self.order.tie(self.came)
        self.own = jnp.concatenate([self.row(2 * k), self.row(2 * k + 1)], 0)
        other = jnp.concatenate([self.row(2 - 2 * k), self.row(3 - 2 * k)], 0)
        self.order.last = other
        self.other = across(other)

    def finish(self):
        own, other = self.own, self.order.tie(self.other)
        results = jnp.where(self.k == 0, own, other), jnp.where(self.k == 0, other, own)
        self.order.last = results[0]
        return results


def angles(places):
    freq = 10000.0 ** (-2.0 * jnp.arange(SIZE // 2, dtype=F32) / SIZE)
    phase = places.astype(F32)[:, None] * jnp.tile(freq, LOCAL)[None, :]
    return jnp.cos(phase), jnp.sin(phase)


def places_of(counts, count, unit):
    at = jnp.arange(count, dtype=jnp.int32)
    starts = unit * jnp.sum(jnp.where(jnp.arange(3)[:, None] >= jnp.arange(3)[None, :], counts[None, :3], 0), 1)
    begin = jnp.max(jnp.where(at[:, None] >= starts[None, :], starts[None, :], 0), 1)
    return at - begin


def body(
    tokens,
    lengths,
    cotangent,
    full_first_gain,
    full_project,
    full_merge,
    full_second_gain,
    full_widen,
    full_narrow,
    pool_weight,
    short_first_gain,
    short_project,
    short_merge,
    short_second_gain,
    short_widen,
    short_narrow,
    expand_weight,
):
    c = lax.axis_index("section")
    d = lax.axis_index("dp")
    k = d % 2
    rows = lengths.shape[0]
    length = tokens.shape[0] // rows
    groups = length // 3
    count = -(-length // QUARTER) * QUARTER
    short = -(-groups // 16) * 16

    here = k == c // 2
    who_k = jnp.stack([c, k]).astype(jnp.int32)
    order = Order()
    gain_rows = [
        g.reshape(1, QUARTER) for g in (full_first_gain, full_second_gain, short_first_gain, short_second_gain)
    ]
    attn_in = [((WIDTH, 3 * QUARTER), BF), ((WIDTH, QUARTER), BF), ((3 * QUARTER, WIDTH), BF)]
    pieces1, = order.call(
        pack_first_kernel, "pack_first", [((PAD + ATTN, QUARTER), BF)], None, full_project, full_merge, *gain_rows,
        scratch=attn_in + [((1, QUARTER), BF)] * 4, sems=6, space=pltpu.HBM, limit=PACK_LIMIT,
    )
    stage1 = [pieces1] + [swap(pieces1, r) for r in (1, 2, 3)]

    j = order.tie(c % 2)
    pairs = jnp.stack([lax.dynamic_index_in_dim(a.reshape(rows, length, WIDTH), j, 0, False) for a in (tokens, cotangent)])
    ends = lax.dynamic_index_in_dim(lengths, j, 0, False).astype(BF)
    ends = jnp.pad(ends, (0, WIDTH - ends.shape[0]))
    own_row = jnp.concatenate([pairs, jnp.broadcast_to(ends, (2, count - length, WIDTH))], 1)
    came_row = across(own_row)

    pieces2, pieces3, pieces4 = order.call(
        pack_rest_kernel, "pack_rest", [((n, QUARTER), BF) for n in (FFN, THIRD + ATTN + THIRD, FFN)],
        None, full_widen, full_narrow, pool_weight, short_project, short_merge, expand_weight, short_widen,
        short_narrow, scratch=attn_in, sems=26, space=pltpu.HBM, limit=PACK_LIMIT,
    )
    stage2, stage3, stage4 = (Stage(p) for p in (pieces2, pieces3, pieces4))
    stage2.start(order)
    stage3.start(order)

    counts = jnp.where(here, own_row[0, length, :SEGS], came_row[0, length, :SEGS]).astype(jnp.int32)
    odd = (d // 2) % 2 if lax.axis_size("dp") == 8 else jnp.zeros_like(d)
    who = jnp.concatenate([who_k, counts, jnp.stack([odd, odd]).astype(jnp.int32)])
    cos, sin = angles(places_of(counts, count, 3))
    short_cos, short_sin = angles(places_of(counts, short, 1))

    def block_outs(n):
        outs = [
            ((3 * HALF, WIDTH), BF, Far),
            ((HALF, WIDTH), BF, Far),
            ((n, WIDTH), BF, Far),
            ((n, HALF), BF, Far),
            ((n, HALF), BF, Far),
            ((n, HALF), BF, Far),
        ]
        return outs if n == count else [out[:2] for out in outs]

    def ffn_outs(n):
        outs = [
            ((n, WIDTH), F32, Far),
            ((n, WIDTH), BF, Far),
            ((WIDTH, HIDDEN), BF, Far),
            ((HIDDEN, WIDTH), BF, Far),
            ((n, HIDDEN), BF, Far),
            ((n, HIDDEN), BF, Far),
            ((n, WIDTH), BF),
        ]
        return outs if n == count else [out[:2] for out in outs]

    def back_outs(n):
        return [
            ((n, WIDTH), F32),
            ((n, WIDTH), BF),
            ((n, 3 * HALF), BF),
            ((n, WIDTH), BF),
            ((PAD, WIDTH), F32),
        ]

    def sent(part):
        return [((part, QUARTER), BF, Far)] * 4

    row, gains, project, merge, first, q, key, v, att, ctx, mix = order.call(
        full_attention_kernel, "full_attention",
        [((count, WIDTH), BF), ((PAD, WIDTH), F32)] + block_outs(count)
        + [((count // QUARTER, LOCAL * QUARTER, count), BF, Far), ((count, HALF), BF, Far), ((count, WIDTH), BF)],
        who, Raw(own_row), Raw(came_row), cos, sin, *[Far(a) for a in stage1], sems=2,
    )
    mix_came = across(mix)
    stage2.relay(order)
    order.wait(stage2.pieces[2])
    stage4.start(order)
    target, grouped = order.call(
        functools.partial(target_kernel, groups), "target",
        [((count, WIDTH), BF, Far), ((short, 3 * WIDTH), BF)], who, Raw(own_row), Raw(came_row), sems=2,
    )
    stage3.relay(order)
    middle, second, widen, narrow, hidden, slope, part = order.call(
        functools.partial(ffn_kernel, 1, stage2.places()), "full_ffn", ffn_outs(count),
        who, row, mix, mix_came, gains, *stage2.all(),
    )
    part_came = across(part)
    stage4.relay(order)
    raw3 = [Raw(a) for a in stage3.pieces]
    full, pool, joined, pooled = order.call(
        functools.partial(pool_kernel, groups), "pool",
        [((count, WIDTH), BF, Far), ((3 * HALF, WIDTH), BF, Far), ((short, 3 * HALF), BF), ((short, WIDTH), BF)],
        who, Far(middle), part, part_came, *raw3, scratch=[((4, THIRD, QUARTER), BF)], sems=4,
    )
    pooled_came = across(pooled)
    expand, d_half = order.call(
        expand_back_kernel, "expand_back", [((HALF, 3 * WIDTH), BF), ((short, HALF), BF)], who, grouped, *raw3,
        scratch=[((4, THIRD, QUARTER), BF)], sems=4,
    )
    d_came = across(d_half)
    s_in, s_project, s_merge, s_first, s_q, s_key, s_v, s_att, s_ctx, s_mix = order.call(
        short_attention_kernel, "short_attention",
        [((short, WIDTH), BF)] + block_outs(short)
        + [((1, LOCAL * short, short), BF), ((short, HALF), BF), ((short, WIDTH), BF)],
        who, pooled, pooled_came, short_cos, short_sin, gains, *raw3,
        scratch=[((4, ATTN, QUARTER), BF)], sems=4,
    )
    s_mix_came = across(s_mix)
    s_middle, s_hidden, s_delta, s_narrow, s_dsecond, *group = order.call(
        short_ffn_kernel, "short_ffn",
        [((short, WIDTH), F32), ((short, HIDDEN), BF), ((short, WIDTH), BF), ((HIDDEN, WIDTH), BF), ((short, WIDTH), BF)]
        + sent(PAD + FFN),
        who, s_in, s_mix, s_mix_came, gains, *stage4.all(), d_half, d_came,
        scratch=[
            ((short, WIDTH), BF), ((WIDTH, HIDDEN), BF), ((short, HIDDEN), BF), ((PAD, WIDTH), F32),
            ((WIDTH, HIDDEN), BF), ((HIDDEN, WIDTH), BF),
        ],
    )
    sum_a = Sum(order, group)
    sum_a.first()
    s_dsecond_came = across(s_dsecond)
    s_part, = order.call(short_ffn_rest_kernel, "short_ffn_rest", [((short, WIDTH), BF)], who, s_hidden, s_narrow)
    s_part_came = across(s_part)
    s_mid, s_dmix, s_dpacked, s_dfirst, s_gain1 = order.call(
        functools.partial(attention_back_kernel, 2, 3, short), "short_attention_back", back_outs(short),
        who, s_delta, s_dsecond, s_dsecond_came, s_middle, gains, s_in, s_merge, s_project, s_q, s_key, s_v, s_att,
        short_cos, short_sin, scratch=[((short, HALF), F32)] * 2,
    )
    s_dfirst_came = across(s_dfirst)
    s_half, grown = order.call(
        functools.partial(expand_kernel, groups), "expand", [((short, HALF), BF), ((count, WIDTH), BF, Far)],
        who, s_middle, s_part, s_part_came, expand, scratch=[((short, WIDTH), BF)],
    )
    grown_came = across(grown)
    d_in, d_low = order.call(
        functools.partial(pool_back_kernel, groups), "pool_back", [((short, WIDTH), BF), ((count, HALF), BF)],
        who, s_mid, s_dfirst, s_dfirst_came, gains, s_in, Far(pool),
    )
    d_low_came = across(d_low)
    order.wait(grown_came)
    sum_b = Sum(order, order.call(
        group_b_kernel, "group_b", sent(PAD + ATTN + 2 * THIRD),
        who, s_ctx, s_dmix, s_dpacked, s_first, s_gain1, joined, d_in, s_half, grouped,
        scratch=[((3 * HALF, WIDTH), BF), ((HALF, WIDTH), BF), ((3 * HALF, WIDTH), BF), ((HALF, 3 * WIDTH), BF)],
    ))
    sum_a.second()
    sum_b.first()
    delta, low, inner, dsecond, gain2 = order.call(
        full_ffn_back_kernel, "full_ffn_back",
        [((count, WIDTH), F32), ((count, WIDTH), BF), ((count, HIDDEN), BF), ((count, WIDTH), BF), ((PAD, WIDTH), F32)],
        who, Far(target), d_low, d_low_came, Far(middle), gains, Far(slope), Far(widen), Far(narrow),
    )
    dsecond_came = across(dsecond)
    sum_c = Sum(order, order.call(
        ffn_group_kernel, "group_c", sent(PAD + FFN), who, Far(hidden), low, Far(second), inner, gain2,
        scratch=[((WIDTH, HIDDEN), BF), ((HIDDEN, WIDTH), BF)],
    ))
    sum_a.third()
    sum_b.second()
    sum_a.fourth()
    sum_c.first()
    mid, dmix, dpacked, dfirst, gain1 = order.call(
        functools.partial(attention_back_kernel, 0, 1, QUARTER), "full_attention_back", back_outs(count),
        who, delta, dsecond, dsecond_came, Far(middle), gains, row, Far(merge), Far(project), Far(q), Far(key), Far(v),
        Far(att), cos, sin, scratch=[((count, HALF), F32)] * 2,
    )
    dfirst_came = across(dfirst)
    sum_a.fifth()
    sum_b.third()
    sum_c.second()
    sum_d = Sum(order, order.call(
        attn_group_kernel, "group_d", sent(PAD + ATTN), who, Far(ctx), dmix, dpacked, Far(first), gain1,
        scratch=[((3 * HALF, WIDTH), BF), ((HALF, WIDTH), BF)],
    ))
    sum_b.fourth()
    sum_d.first()
    sent_rows = order.call(
        outputs_kernel, "outputs", [((length, QUARTER), BF)] * 4,
        who, Far(full), Far(grown), grown_came, mid, dfirst, dfirst_came, gains, row, scratch=[((count, WIDTH), BF)],
    )


    gain_out = ((1, QUARTER), F32)
    ffn_out = [((WIDTH, WIDTH), F32), ((4 * WIDTH, QUARTER), F32)]
    attn_out = [((WIDTH, 3 * QUARTER), F32), ((WIDTH, QUARTER), F32)]
    turned = [((3 * QUARTER, WIDTH), F32)]

    def spread(kernel, name, outs, total, **options):
        outs = [(*out, Far) for out in outs]
        how = spread_either if total.short else spread_whole
        return order.call(functools.partial(how, kernel), name, outs, who, *total.all(), **options)

    sum_d.second()
    sum_c.third()
    sum_d.third()
    sum_a.sixth()
    sum_c.fourth()
    sum_b.fifth()
    g_s2, g_s_widen, g_s_narrow = spread(spread_ffn_kernel, "spread_a", [gain_out] + ffn_out, sum_a)
    sum_d.fourth()
    sum_c.fifth()
    delivery = Delivery(order, sent_rows, c, k)
    sum_d.fifth()
    sum_c.sixth()
    sum_d.sixth()
    sum_b.sixth()
    g_s1, g_s_project, g_s_merge, g_pool, g_expand = spread(
        spread_b_kernel, "spread_b",
        [gain_out] + attn_out + [((3 * WIDTH, QUARTER), F32), ((WIDTH, 3 * QUARTER), F32)], sum_b, scratch=turned,
    )
    delivery.turn()
    g_f2, g_widen, g_narrow = spread(spread_ffn_kernel, "spread_c", [gain_out] + ffn_out, sum_c)
    g_f1, g_project, g_merge = spread(spread_attn_kernel, "spread_d", [gain_out] + attn_out, sum_d, scratch=turned)
    mixed_out, token_gradient = delivery.finish()

    return (
        mixed_out,
        token_gradient,
        g_f1.reshape(-1),
        g_project,
        g_merge,
        g_f2.reshape(-1),
        g_widen,
        g_narrow,
        g_pool,
        g_s1.reshape(-1),
        g_s_project,
        g_s_merge,
        g_s2.reshape(-1),
        g_s_widen,
        g_s_narrow,
        g_expand,
    )


def solution(mesh):
    in_specs = (
        P("dp", None),
        P("dp", None),
        P("dp", None),
        P("section"),
        P(None, "section"),
        P(None, "section"),
        P("section"),
        P(None, "section"),
        P(None, "section"),
        P(None, "section"),
        P("section"),
        P(None, "section"),
        P(None, "section"),
        P("section"),
        P(None, "section"),
        P(None, "section"),
        P(None, "section"),
    )
    out_specs = (
        P("dp", "section"),
        P("dp", "section"),
        P("section"),
        P(None, "section"),
        P(None, "section"),
        P("section"),
        P(None, "section"),
        P(None, "section"),
        P(None, "section"),
        P("section"),
        P(None, "section"),
        P(None, "section"),
        P("section"),
        P(None, "section"),
        P(None, "section"),
        P(None, "section"),
    )
    return jax.shard_map(body, mesh=mesh, in_specs=in_specs, out_specs=out_specs, check_vma=False)
```

```python
import functools

import jax
import jax.numpy as jnp
from jax import lax
from jax.experimental import pallas as pl
from jax.experimental.pallas import tpu as pltpu
from jax.sharding import PartitionSpec as P


WIDTH = 512
QUARTER = 128
HALF = 256
HIDDEN = 1024
SEGS = 4
LOCAL = 4
SIZE = 64
EPS = 1e-05
NEG = -1e30

BF = jnp.bfloat16
F32 = jnp.float32

ATTN = 1024
FFN = 2048
THIRD = 768
PAD = 32
VMEM_LIMIT = 16 * 2**20
PACK_LIMIT = 60 * 2**20


def nn(left, right):
    return lax.dot_general(left, right, (((1,), (0,)), ((), ())), preferred_element_type=F32)


def nt(left, right):
    return lax.dot_general(left, right, (((1,), (1,)), ((), ())), preferred_element_type=F32)


def tn(left, right):
    return lax.dot_general(left, right, (((0,), (0,)), ((), ())), preferred_element_type=F32)


def lanes(start, count=QUARTER):
    return pl.ds(pl.multiple_of(start, QUARTER), count)


def rows_at(start, count, unit):
    return pl.ds(pl.multiple_of(start, unit), count)


def iota(shape, dim):
    return lax.broadcasted_iota(jnp.int32, shape, dim)


def standard(states):
    center = states - jnp.mean(states, -1, keepdims=True)
    inverse = lax.rsqrt(jnp.mean(center * center, -1, keepdims=True) + EPS)
    return center * inverse, inverse


def norm_back(delta, normed, inverse):
    return inverse * (
        delta
        - jnp.mean(delta, -1, keepdims=True)
        - normed * jnp.mean(delta * normed, -1, keepdims=True)
    )


def gelu_parts(x):
    z = x * 0.7071067811865476
    t = 1.0 / (1.0 + 0.3275911 * jnp.abs(z))
    e = jnp.exp(-z * z)
    poly = t * (
        0.127414796
        + t * (-0.142248368 + t * (0.7107068705 + t * (-0.7265760135 + t * 0.5307027145)))
    )
    tail = poly * e
    phi = jnp.where(z >= 0, 1.0 - tail, tail)
    return x * phi, phi + x * e * 0.3989422804014327


def chips(who):
    c, k = who[0], who[1]
    return c, c ^ (1 + k), c ^ (2 - k), c ^ 3


def reader(refs, places):
    def read(r, at, rows):
        return refs[r][places[r] + at : places[r] + at + rows, :]

    return read


def writer(*refs):
    def write(r, at, value):
        refs[r][at : at + value.shape[0], :] = value

    return write


def pair_rows(pair):
    is_value = pair >= 8
    first = jnp.where(is_value, 512 + 64 * (pair - 8), 256 * (pair >> 2) + 32 * (pair & 3))
    second = jnp.where(is_value, first + 32, first + 128)
    return first, second


def pack_attn(k, turned, merge, put, base):
    for p in range(3):
        chunk = turned[rows_at(128 * p + 64 * k, 64, 64), :]
        for j in range(4):
            put(base + j * 192 + p * 64, chunk[:, 128 * j : 128 * j + 128])
    for pair in range(4):
        put(base + 768 + pair * 64, merge[rows_at(128 * pair + 64 * k, 64, 64), :])


def unpack_attn(who, read, base, project, merge):
    for r, q in enumerate(chips(who)):
        for p in range(3):
            first, second = pair_rows(3 * q + p)
            for j in range(4):
                block = read(r, base + j * 192 + p * 64, 64)
                project[rows_at(first, 32, 32), 128 * j : 128 * j + 128] = block[:32]
                project[rows_at(second, 32, 32), 128 * j : 128 * j + 128] = block[32:]
        for pair in range(4):
            merge[64 * pair : 64 * pair + 64, lanes(128 * q)] = read(r, base + 768 + pair * 64, 64)


def regroup_attn(who, write, base, project, merge):
    for r, q in enumerate(chips(who)):
        for p in range(3):
            first, second = pair_rows(3 * q + p)
            for j in range(4):
                at = base + j * 192 + p * 64
                write(r, at, project[rows_at(first, 32, 32), 128 * j : 128 * j + 128])
                write(r, at + 32, project[rows_at(second, 32, 32), 128 * j : 128 * j + 128])
        for pair in range(4):
            write(r, base + 768 + pair * 64, merge[64 * pair : 64 * pair + 64, lanes(128 * q)])


def pack_ffn(k, widen, narrow, put):
    for lc in range(2):
        put(512 * lc, widen.at[:, lanes(256 * k + 128 * lc)])
    for qq in range(4):
        put(1024 + 256 * qq, narrow.at[rows_at(512 * qq + 256 * k, 256, 256), :])


def unpack_ffn(who, read, widen, narrow):
    for r, q in enumerate(chips(who)):
        for lc in range(2):
            widen[:, lanes(256 * q + 128 * lc)] = read(r, 512 * lc, 512)
        narrow[:, lanes(128 * q)] = read(r, 1024, 1024)


def regroup_ffn(who, write, base, widen, narrow):
    for r, q in enumerate(chips(who)):
        for lc in range(2):
            write(r, base + 512 * lc, widen[:, lanes(256 * q + 128 * lc)])
        write(r, base + 1024, narrow[:, lanes(128 * q)])


def pack_pool(k, pool, put, base):
    for i in range(6):
        put(base + i * 128, pool.at[rows_at(512 * (i // 2) + 256 * k + 128 * (i % 2), 128, 128), :])


def unpack_pool(who, read, base, pool):
    for r, q in enumerate(chips(who)):
        for i in range(6):
            pool[128 * i : 128 * i + 128, lanes(128 * q)] = read(r, base + i * 128, 128)


def regroup_pool(who, write, base, pool):
    for r, q in enumerate(chips(who)):
        for i in range(6):
            write(r, base + i * 128, pool[128 * i : 128 * i + 128, lanes(128 * q)])


def pack_expand(k, expand, put, base):
    for i in range(6):
        put(base + i * 128, expand.at[rows_at(256 * k + 128 * (i % 2), 128, 128), pl.ds(128 * (i // 2), 128)])


def unpack_expand(who, read, base, expand):
    for r, q in enumerate(chips(who)):
        for i in range(6):
            block = read(r, base + i * 128, 128)
            expand[128 * (i % 2) : 128 * (i % 2) + 128, lanes(384 * q + 128 * (i // 2))] = block


def regroup_expand(who, write, base, expand):
    for r, q in enumerate(chips(who)):
        for i in range(6):
            block = expand[128 * (i % 2) : 128 * (i % 2) + 128, lanes(384 * q + 128 * (i // 2))]
            write(r, base + i * 128, block)


def regroup_gain(who, write, gain):
    for r, q in enumerate(chips(who)):
        write(r, 0, gain[:, lanes(128 * q)].astype(BF))


class Copies:
    def __init__(self, sems):
        self.sems, self.all = sems, []

    def start(self, source, target):
        copy = pltpu.make_async_copy(source, target, self.sems.at[len(self.all)])
        copy.start()
        self.all.append(copy)

    def putter(self, ref):
        def put(at, source):
            self.start(source, ref.at[pl.ds(at, source.shape[0]), :])

        return put

    def wait(self):
        for copy in self.all:
            copy.wait()


def putter(ref):
    def put(at, value):
        ref[at : at + value.shape[0], :] = value

    return put


def core():
    return lax.rem(lax.axis_index("dp"), 2)


def pack_first_kernel(project, merge, g0, g1, g2, g3, out, project_in, merge_in, turned, i0, i1, i2, i3, sems):
    copies = Copies(sems)
    copies.start(project, project_in)
    copies.start(merge, merge_in)
    inside = (i0, i1, i2, i3)
    for gain, place in zip((g0, g1, g2, g3), inside):
        copies.start(gain, place)
    copies.wait()
    row = iota((PAD, QUARTER), 0)
    gains = jnp.zeros((PAD, QUARTER), F32)
    for i, place in enumerate(inside):
        gains = jnp.where(row == i, place[...].astype(F32), gains)
    out[0:PAD, :] = gains.astype(BF)
    turned[...] = jnp.swapaxes(project_in[...], 0, 1)
    pack_attn(core(), turned, merge_in, putter(out), PAD)


def pack_rest_kernel(
    widen, narrow, pool, project, merge, expand, s_widen, s_narrow, out2, out3, out4, project_in, merge_in, turned, sems
):
    k = core()
    copies, last = Copies(sems), Copies(sems.at[pl.ds(2, 24)])
    copies.start(project, project_in)
    copies.start(merge, merge_in)
    pack_ffn(k, widen, narrow, last.putter(out2))
    pack_pool(k, pool, last.putter(out3), 0)
    pack_expand(k, expand, last.putter(out3), THIRD + ATTN)
    pack_ffn(k, s_widen, s_narrow, last.putter(out4))
    copies.wait()
    turned[...] = jnp.swapaxes(project_in[...], 0, 1)
    pack_attn(k, turned, merge_in, putter(out3), THIRD)
    last.wait()


def ends_of(who):
    e0 = who[2]
    e1 = e0 + who[3]
    e2 = e1 + who[4]
    return e0, e1, e2, e2 + who[5]


def segment_of(who, index, unit):
    return sum((index >= unit * end).astype(jnp.int32) for end in ends_of(who))


def head_masks():
    lane = iota((1, HALF), 1)
    turned = [((lane & 127) >> 5 == h).astype(F32).astype(BF) for h in range(LOCAL)]
    plain = [((lane >> 6) == h).astype(F32).astype(BF) for h in range(LOCAL)]
    return turned, plain


def attention_forward(who, states, gain, cos, sin, project, merge, first, q, k, v, att, ctx, mix, unit, block):
    count = states.shape[0]
    normed, _ = standard(states)
    start = (normed * gain).astype(BF)
    first[...] = start
    packed = nt(start, project[...])
    cosine, sine = cos[...], sin[...]
    for ref, at in ((q, 0), (k, 256)):
        a, b = packed[:, at : at + 128], packed[:, at + 128 : at + 256]
        ref[:, 0:128] = (a * cosine - b * sine).astype(BF)
        ref[:, 128:256] = (b * cosine + a * sine).astype(BF)
    v[...] = packed[:, 512:768].astype(BF)
    turned, plain = head_masks()
    scale = jnp.asarray(SIZE**-0.5, BF)
    for b in range(count // block):
        low, stop = b * block, (b + 1) * block
        at_row = low + iota((block, 1), 0)
        at_col = iota((1, stop), 1)
        allowed = (segment_of(who, at_row, unit) == segment_of(who, at_col, unit)) & (at_row >= at_col)
        queries = q[low:stop, :] * scale
        keys, values = k[0:stop, :], v[0:stop, :]
        total_context = jnp.zeros((block, HALF), F32)
        for h in range(LOCAL):
            scores = jnp.where(allowed, nt(queries * turned[h], keys), NEG)
            powered = jnp.exp(scores - jnp.max(scores, -1, keepdims=True))
            attend = (powered * (1.0 / jnp.sum(powered, -1, keepdims=True))).astype(BF)
            att[b, h * block : (h + 1) * block, 0:stop] = attend
            total_context = total_context + nn(attend, values * plain[h])
        ctx[low:stop, :] = total_context.astype(BF)
    mix[...] = nn(ctx[...], merge[...]).astype(BF)


def full_attention_kernel(
    who, own, came, cos, sin, s, x, y, d, row, gains, project, merge, first, q, k, v, att, ctx, mix, sems
):
    c = who[0]
    here = who[1] == c >> 1
    for i, (source, taken) in enumerate(((own, here), (came, jnp.logical_not(here)))):

        @pl.when(taken)
        def _():
            copy = pltpu.make_async_copy(source.at[0], row, sems.at[i])
            copy.start()
            copy.wait()

    read = reader((s, x, y, d), (0,) * 4)
    for r, chip in enumerate(chips(who)):
        gains[:, lanes(128 * chip)] = read(r, 0, PAD).astype(F32)
    unpack_attn(who, read, PAD, project, merge)
    states = row[...].astype(F32)
    attention_forward(
        who, states, gains[0:1, :], cos, sin, project, merge, first, q, k, v, att, ctx, mix, 3, QUARTER
    )


def short_attention_kernel(
    who, own, came, cos, sin, gains, s, x, y, d, states, project, merge, first, q, k, v, att, ctx, mix, box, sems
):
    unpack_attn(who, boxed((s, x, y, d), THIRD, box, sems), 0, project, merge)
    states[...] = (own[...].astype(F32) + came[...].astype(F32)).astype(BF)
    attention_forward(
        who, states[...].astype(F32), gains[2:3, :], cos, sin, project, merge, first, q, k, v, att, ctx, mix,
        1, own.shape[0],
    )


def ffn_kernel(
    gain_row, places, who, states, own, came, gains, s, x, y, d, middle, second, widen, narrow, hidden, slope, out
):
    unpack_ffn(who, reader((s, x, y, d), places), widen, narrow)
    mid = states[...].astype(F32) + (own[...].astype(F32) + came[...].astype(F32))
    middle[...] = mid
    normed, _ = standard(mid)
    start = (normed * gains[gain_row : gain_row + 1, :]).astype(BF)
    second[...] = start

    @pl.loop(0, 4)
    def _(i):
        cols = lanes(HALF * i, HALF)
        value, back = gelu_parts(nn(second[...], widen[:, cols]))
        hidden[:, cols] = value.astype(BF)
        slope[:, cols] = back.astype(BF)

    out[...] = nn(hidden[...], narrow[...]).astype(BF)


def join_masks(who, groups, count, real):
    g = iota((groups, 1), 0)
    t = iota((1, count), 1)
    ends = ends_of(who)
    keep = (g != ends[0]) & (g != ends[1]) & (g != ends[2]) & (g < real)
    return [
        jnp.where((t == 3 * g - 2) & keep, 1.0, 0.0).astype(BF),
        jnp.where((t == 3 * g - 1) & keep, 1.0, 0.0).astype(BF),
        jnp.where((t == 3 * g) & (g < real), 1.0, 0.0).astype(BF),
    ]


def group_masks(groups, count, real):
    g = iota((groups, 1), 0)
    t = iota((1, count), 1)
    return [jnp.where((t == 3 * g + i) & (g < real), 1.0, 0.0).astype(BF) for i in range(3)]


def boxed(refs, at, box, sems):
    copies = Copies(sems)
    for r, ref in enumerate(refs):
        copies.start(ref.at[pl.ds(at, box.shape[1]), :], box.at[r])
    copies.wait()

    def read(r, at, rows):
        return box[r, at : at + rows, :]

    return read


def pool_kernel(real, who, middle, own, came, s, x, y, d, full, pool, joined, out, box, sems):
    unpack_pool(who, boxed((s, x, y, d), 0, box, sems), 0, pool)
    full[...] = (middle[...] + (own[...].astype(F32) + came[...].astype(F32))).astype(BF)
    part = full[:, lanes(HALF * who[1], HALF)]
    for j, mask in enumerate(join_masks(who, joined.shape[0], full.shape[0], real)):
        joined[:, HALF * j : HALF * j + HALF] = nn(mask, part).astype(BF)
    out[...] = nn(joined[...], pool[...]).astype(BF)


def target_kernel(real, who, own, came, target, grouped, sems):
    here = who[1] == who[0] >> 1
    for i, (source, taken) in enumerate(((own, here), (came, jnp.logical_not(here)))):

        @pl.when(taken)
        def _():
            copy = pltpu.make_async_copy(source.at[1], target, sems.at[i])
            copy.start()
            copy.wait()

    live = segment_of(who, iota((target.shape[0], 1), 0), 3) < 3
    target[...] = jnp.where(live, target[...].astype(F32), 0.0).astype(BF)
    for i, mask in enumerate(group_masks(grouped.shape[0], target.shape[0], real)):
        grouped[:, WIDTH * i : WIDTH * i + WIDTH] = nn(mask, target[...]).astype(BF)


def expand_back_kernel(who, grouped, s, x, y, d, expand, out, box, sems):
    unpack_expand(who, boxed((s, x, y, d), THIRD + ATTN, box, sems), 0, expand)
    out[...] = nt(grouped[...], expand[...]).astype(BF)


def expand_kernel(real, who, middle, own, came, expand, part, out, short):
    k = who[1]
    short[...] = (middle[...] + (own[...].astype(F32) + came[...].astype(F32))).astype(BF)
    part[...] = short[:, lanes(HALF * k, HALF)]
    grown = nn(part[...], expand[...]).astype(BF)
    total = jnp.zeros(out.shape, F32)
    for i, mask in enumerate(group_masks(part.shape[0], out.shape[0], real)):
        total = total + tn(mask, grown[:, WIDTH * i : WIDTH * i + WIDTH])
    out[...] = total.astype(BF)


def ffn_back(gain_row, delta, middle, gains, slope, widen, narrow, inner, out, gain):
    total = jnp.zeros(middle.shape, F32)
    for i in range(4):
        cols = slice(HALF * i, HALF * i + HALF)
        value = (nt(delta, narrow[cols, :]) * slope[:, cols].astype(F32)).astype(BF)
        inner[:, cols] = value
        total = total + nt(value, widen[:, cols])
    normed, _ = standard(middle[...])
    out[...] = total.astype(BF)
    gain[...] = jnp.broadcast_to(jnp.sum(total * normed, 0, keepdims=True), gain.shape)


def full_ffn_back_kernel(
    who, target, own, came, middle, gains, slope, widen, narrow, delta, low, inner, out, gain
):
    k = who[1]
    delta[:, lanes(HALF * k, HALF)] = own[...].astype(F32)
    delta[:, lanes(HALF * (1 - k), HALF)] = came[...].astype(F32)
    delta[...] = delta[...] + target[...].astype(F32)
    low[...] = delta[...].astype(BF)
    ffn_back(1, low[...], middle, gains, slope, widen, narrow, inner, out, gain)


def attention_back_kernel(
    first_row, second_row, block, who, delta, own, came, middle, gains, states, merge, project, q, k, v, att, cos, sin,
    mid, mix, packed, out, gain, dk, dv,
):
    count = middle.shape[0]
    normed, inverse = standard(middle[...])
    dsecond = own[...].astype(F32) + came[...].astype(F32)
    dmid = delta[...].astype(F32) + norm_back(dsecond * gains[second_row : second_row + 1, :], normed, inverse)
    mid[...] = dmid
    low = dmid.astype(BF)
    mix[...] = low
    dctx = nt(low, merge[...]).astype(BF)
    turned, plain = head_masks()
    scale = SIZE**-0.5
    cosine, sine = cos[...], sin[...]
    dk[...] = jnp.zeros(dk.shape, F32)
    dv[...] = jnp.zeros(dv.shape, F32)
    for b in range(count // block):
        start, stop = b * block, (b + 1) * block
        keys, values = k[0:stop, :], v[0:stop, :]
        queries = q[start:stop, :]
        dcontext = dctx[start:stop, :]
        dq = jnp.zeros((block, HALF), F32)
        for h in range(LOCAL):
            dhead = dcontext * plain[h]
            low_attend = att[b, h * block : (h + 1) * block, 0:stop]
            attend = low_attend.astype(F32)
            dattend = nt(dhead, values)
            dscores = attend * (dattend - jnp.sum(attend * dattend, -1, keepdims=True))
            dscores = (dscores * scale).astype(BF)
            dq = dq + nn(dscores, keys * turned[h])
            dk[0:stop, :] += tn(dscores, queries * turned[h])
            dv[0:stop, :] += tn(low_attend, dhead)
        a, c = dq[:, 0:128], dq[:, 128:256]
        packed[start:stop, 0:128] = (a * cosine[start:stop] + c * sine[start:stop]).astype(BF)
        packed[start:stop, 128:256] = (c * cosine[start:stop] - a * sine[start:stop]).astype(BF)
    a, c = dk[:, 0:128], dk[:, 128:256]
    packed[:, 256:384] = (a * cosine + c * sine).astype(BF)
    packed[:, 384:512] = (c * cosine - a * sine).astype(BF)
    packed[:, 512:768] = dv[...].astype(BF)
    dfirst = nn(packed[...], project[...])
    out[...] = dfirst.astype(BF)
    normed_one, _ = standard(states[...].astype(F32))
    gain[...] = jnp.broadcast_to(jnp.sum(dfirst * normed_one, 0, keepdims=True), gain.shape)


def input_gradient(gain_row, mid, own, came, gains, states):
    normed, inverse = standard(states[...].astype(F32))
    dfirst = own[...].astype(F32) + came[...].astype(F32)
    return mid[...] + norm_back(dfirst * gains[gain_row : gain_row + 1, :], normed, inverse)


def pool_back_kernel(real, who, mid, own, came, gains, states, pool, delta, out):
    delta[...] = input_gradient(2, mid, own, came, gains, states).astype(BF)
    djoined = nt(delta[...], pool[...]).astype(BF)
    total = jnp.zeros(out.shape, F32)
    for j, mask in enumerate(join_masks(who, delta.shape[0], out.shape[0], real)):
        total = total + tn(mask, djoined[:, HALF * j : HALF * j + HALF])
    out[...] = total.astype(BF)


def outputs_kernel(who, full, grown, grown_came, mid, own, came, gains, states, o0, o1, o2, o3, whole):
    @pl.when(who[1] == 0)
    def _():
        whole[...] = (full[...].astype(F32) + (grown[...].astype(F32) + grown_came[...].astype(F32))).astype(BF)

    @pl.when(who[1] != 0)
    def _():
        whole[...] = input_gradient(0, mid, own, came, gains, states).astype(BF)

    for q, out in zip(chips(who), (o0, o1, o2, o3)):
        out[...] = whole[0 : out.shape[0], lanes(128 * q)]


def ffn_weights(who, write, hidden, delta, second, inner, gain, dwiden, dnarrow):
    dnarrow[...] = tn(hidden[...], delta[...]).astype(BF)
    dwiden[...] = tn(second[...], inner[...]).astype(BF)
    regroup_gain(who, write, gain)
    regroup_ffn(who, write, PAD, dwiden, dnarrow)


def attn_weights(who, write, ctx, mix, packed, first, gain, dproject, dmerge):
    dproject[...] = tn(packed[...], first[...]).astype(BF)
    dmerge[...] = tn(ctx[...], mix[...]).astype(BF)
    regroup_gain(who, write, gain)
    regroup_attn(who, write, PAD, dproject, dmerge)


def group_b_kernel(
    who, ctx, mix, packed, first, gain, joined, delta, part, grouped, keep, send, pass_on, relay, dproject, dmerge, dpool, dexpand
):
    write = writer(keep, send, pass_on, relay)
    attn_weights(who, write, ctx, mix, packed, first, gain, dproject, dmerge)
    dpool[...] = tn(joined[...], delta[...]).astype(BF)
    regroup_pool(who, write, PAD + ATTN, dpool)
    dexpand[...] = tn(part[...], grouped[...]).astype(BF)
    regroup_expand(who, write, PAD + ATTN + THIRD, dexpand)


def short_ffn_kernel(
    who, states, own, came, gains, s, x, y, d, d_own, d_came, middle, hidden, delta, narrow, dsecond,
    keep, send, pass_on, relay, second, widen, inner, gain, dwiden, dnarrow,
):
    k = who[1]
    unpack_ffn(who, reader((s, x, y, d), (0,) * 4), widen, narrow)
    mid = states[...].astype(F32) + (own[...].astype(F32) + came[...].astype(F32))
    middle[...] = mid
    normed, _ = standard(mid)
    second[...] = (normed * gains[3:4, :]).astype(BF)
    delta[:, lanes(HALF * k, HALF)] = d_own[...]
    delta[:, lanes(HALF * (1 - k), HALF)] = d_came[...]
    for i in range(4):
        cols = slice(HALF * i, HALF * i + HALF)
        value, back = gelu_parts(nn(second[...], widen[:, cols]))
        hidden[:, cols] = value.astype(BF)
        inner[:, cols] = (nt(delta[...], narrow[cols, :]) * back).astype(BF)
    total = nt(inner[...], widen[...])
    dsecond[...] = total.astype(BF)
    gain[...] = jnp.broadcast_to(jnp.sum(total * normed, 0, keepdims=True), gain.shape)
    ffn_weights(who, writer(keep, send, pass_on, relay), hidden, delta, second, inner, gain, dwiden, dnarrow)


def short_ffn_rest_kernel(who, hidden, narrow, out):
    out[...] = nn(hidden[...], narrow[...]).astype(BF)


def ffn_group_kernel(who, hidden, delta, second, inner, gain, keep, send, pass_on, relay, dwiden, dnarrow):
    ffn_weights(who, writer(keep, send, pass_on, relay), hidden, delta, second, inner, gain, dwiden, dnarrow)


def attn_group_kernel(who, ctx, mix, packed, first, gain, keep, send, pass_on, relay, dproject, dmerge):
    attn_weights(who, writer(keep, send, pass_on, relay), ctx, mix, packed, first, gain, dproject, dmerge)


class Halves:
    def __init__(self, first, second, start=0):
        self.first, self.second, self.half, self.start = first, second, first.shape[0], start

    def after(self, rows):
        return Halves(self.first, self.second, self.start + rows)

    def read(self, at, rows):
        at = at + self.start
        stop = at + rows
        if stop <= self.half:
            return self.first[at:stop, :].astype(F32)
        if at >= self.half:
            return self.second[at - self.half : stop - self.half, :].astype(F32)
        parts = (self.first[at : self.half, :], self.second[0 : stop - self.half, :])
        return jnp.concatenate([part.astype(F32) for part in parts], 0)


def both(who, own, came):
    return ((who[1], own.read), (1 - who[1], came.read))


def spread_gain(own, came, gain):
    gain[...] = own.read(0, 8)[0:1] + came.read(0, 8)[0:1]


def spread_ffn(who, own, came, widen, narrow):
    for k, read in both(who, own, came):
        for lc in range(2):
            widen[:, lanes(256 * k + 128 * lc)] = read(PAD + 512 * lc, 512)
        for qq in range(4):
            narrow[rows_at(512 * qq + 256 * k, 256, 256), :] = read(PAD + 1024 + 256 * qq, 256)


def spread_attn(who, own, came, project, merge, turned):
    for k, read in both(who, own, came):
        for j in range(4):
            for p in range(3):
                block = read(PAD + j * 192 + p * 64, 64)
                turned[rows_at(128 * p + 64 * k, 64, 64), 128 * j : 128 * j + 128] = block
        for pair in range(4):
            merge[rows_at(128 * pair + 64 * k, 64, 64), :] = read(PAD + 768 + pair * 64, 64)
    project[...] = jnp.swapaxes(turned[...], 0, 1)


def spread_whole(kernel, who, own, came, *outs):
    half = own.shape[0] // 2
    kernel(who, *[Halves(*[ref.at[pl.ds(half * i, half), :] for i in range(2)]) for ref in (own, came)], *outs)


def spread_either(kernel, who, keep, rest, keep_came, rest_came, *outs):
    @pl.when(who[6] == 0)
    def _():
        kernel(who, Halves(keep, rest), Halves(keep_came, rest_came), *outs)

    @pl.when(who[6] != 0)
    def _():
        kernel(who, Halves(rest, keep), Halves(rest_came, keep_came), *outs)


def spread_b_kernel(who, own, came, gain, project, merge, pool, expand, turned):
    spread_gain(own, came, gain)
    spread_attn(who, own, came, project, merge, turned)
    for k, read in both(who, own, came):
        for i in range(6):
            pool[rows_at(512 * (i // 2) + 256 * k + 128 * (i % 2), 128, 128), :] = read(PAD + ATTN + i * 128, 128)
            block = read(PAD + ATTN + THIRD + i * 128, 128)
            expand[rows_at(256 * k + 128 * (i % 2), 128, 128), 128 * (i // 2) : 128 * (i // 2) + 128] = block


def spread_ffn_kernel(who, own, came, gain, widen, narrow):
    spread_gain(own, came, gain)
    spread_ffn(who, own, came, widen, narrow)


def spread_attn_kernel(who, own, came, gain, project, merge, turned):
    spread_gain(own, came, gain)
    spread_attn(who, own, came, project, merge, turned)


class Far:
    def __init__(self, array):
        self.array = array


class Free(Far):
    pass


class Raw(Far):
    pass


def call(kernel, name, outs, who, *args, scratch=(), sems=0, space=pltpu.VMEM, limit=VMEM_LIMIT):
    whole = pl.BlockSpec(memory_space=pltpu.VMEM)
    whos = [] if who is None else [who]
    spaces = [
        None if isinstance(a, (Raw, Free)) else pltpu.HBM if isinstance(a, Far) or space == pltpu.HBM else None
        for a in args
    ]
    kinds = [pl.ANY if isinstance(a, Raw) else space for a in args]
    args = [a.array if isinstance(a, Far) else a for a in args]
    return pl.pallas_call(
        kernel,
        name=name,
        out_shape=[(pltpu.HBM if far else pltpu.VMEM)(shape, dtype) for shape, dtype, *far in outs],
        in_specs=[pl.BlockSpec(memory_space=pltpu.SMEM)] * len(whos) + [pl.BlockSpec(memory_space=kind) for kind in kinds],
        out_specs=[whole] * len(outs),
        scratch_shapes=[pltpu.VMEM(shape, dtype) for shape, dtype in scratch]
        + ([pltpu.SemaphoreType.DMA((sems,))] if sems else []),
        compiler_params=pltpu.CompilerParams(vmem_limit_bytes=limit),
        cost_estimate=pl.CostEstimate(flops=1024, bytes_accessed=1024, transcendentals=0),
    )(*whos, *[a if place is None else pltpu.with_memory_space_constraint(a, place) for a, place in zip(args, spaces)])


def swap(value, role):
    count = lax.axis_size("dp")
    route = []
    for chip in range(lax.axis_size("section")):
        for d in range(count):
            distance = (0, 1 + d % 2, 2 - d % 2, 3)[role]
            route.append((chip * count + d, (chip ^ distance) * count + d))
    return lax.ppermute(value, ("section", "dp"), route)


def across(value):
    return lax.ppermute(value, "dp", [(i, i ^ 1) for i in range(lax.axis_size("dp"))])


class Order:
    def __init__(self):
        self.last = None

    def tie(self, value, *others):
        others = [o for o in (self.last, *others) if o is not None]
        return lax.optimization_barrier((value, others))[0] if others else value

    def wait(self, *values):
        self.last = lax.optimization_barrier((self.last, values))[0]

    def call(self, kernel, name, outs, who, *args, **options):
        results = call(kernel, name, outs, None if who is None else self.tie(who), *args, **options)
        self.last = results[-1]
        return results

    def add(self, first, *others):
        total = self.tie(first)
        for other in others:
            total = total + other
        self.last = total
        return total


class Stage:
    def __init__(self, pieces):
        self.pieces = [pieces]

    def start(self, order):
        own = order.tie(self.pieces[0])
        self.pieces += [swap(own, 1), swap(own, 2)]

    def relay(self, order):
        self.pieces.append(swap(order.tie(self.pieces[1]), 2))

    def all(self):
        return [Free(array) for array in self.pieces]

    def places(self):
        return (0,) * 4


class Sum:
    def __init__(self, order, group):
        self.order = order
        self.keep, self.send, self.pass_on, self.relay = group

    def first(self):
        self.relayed = swap(self.order.tie(self.relay), 1)
        self.came = swap(self.order.tie(self.send), 1)

    def second(self):
        self.last = swap(self.order.add(self.relayed, self.pass_on), 2)

    def across_rows(self, value, distance):
        route = [(i, i ^ (2 * distance)) for i in range(lax.axis_size("dp"))]
        return lax.ppermute(value, "dp", route)

    def total(self):
        return self.order.add(self.last, self.came, self.keep)

    def third(self, apart=False):
        total = self.total()
        count = lax.axis_size("dp")
        self.short = count == 8 and not apart
        if self.short:
            half = total.shape[0] // 2
            odd = (lax.axis_index("dp") // 2) % 2 == 1
            self.keep = jnp.where(odd, total[half:], total[:half])
            self.came = self.across_rows(jnp.where(odd, total[:half], total[half:]), 1)
        else:
            groups = [[i for i in range(count) if i % 2 == core] for core in range(2)]
            self.keep = lax.psum(total, "dp", axis_index_groups=groups)

    def fourth(self):
        if self.short:
            self.keep = self.order.add(self.came, self.keep)
            self.came = self.across_rows(self.keep, 2)

    def fifth(self):
        if self.short:
            self.keep = self.order.add(self.came, self.keep)
            self.rest = self.across_rows(self.keep, 1)

    def sixth(self):
        if self.short:
            self.keep, self.rest = self.order.tie((self.keep, self.rest))
            self.keep_came, self.rest_came = across(self.keep), across(self.rest)
        else:
            self.keep = self.order.tie(self.keep)
            self.keep_came = across(self.keep)

    def all(self):
        if self.short:
            return self.keep, self.rest, self.keep_came, self.rest_came
        return self.keep, self.keep_came


class Delivery:
    def __init__(self, order, pieces, c, k):
        self.order, self.c, self.k = order, c, k
        pieces = order.tie(pieces)
        self.came = [pieces[0]] + [swap(pieces[r], r) for r in range(1, 4)]

    def row(self, chip):
        far, came = self.c ^ chip, self.came
        first = far == 1 + self.k
        return jnp.where(far == 0, came[0], jnp.where(first, came[1], jnp.where(far == 3, came[3], came[2])))

    def turn(self):
        k = self.k
        self.came = self.order.tie(self.came)
        self.own = jnp.concatenate([self.row(2 * k), self.row(2 * k + 1)], 0)
        other = jnp.concatenate([self.row(2 - 2 * k), self.row(3 - 2 * k)], 0)
        self.order.last = other
        self.other = across(other)

    def finish(self):
        own, other = self.own, self.order.tie(self.other)
        results = jnp.where(self.k == 0, own, other), jnp.where(self.k == 0, other, own)
        self.order.last = results[0]
        return results


def angles(places):
    freq = 10000.0 ** (-2.0 * jnp.arange(SIZE // 2, dtype=F32) / SIZE)
    phase = places.astype(F32)[:, None] * jnp.tile(freq, LOCAL)[None, :]
    return jnp.cos(phase), jnp.sin(phase)


def places_of(counts, count, unit):
    at = jnp.arange(count, dtype=jnp.int32)
    starts = unit * jnp.sum(jnp.where(jnp.arange(3)[:, None] >= jnp.arange(3)[None, :], counts[None, :3], 0), 1)
    begin = jnp.max(jnp.where(at[:, None] >= starts[None, :], starts[None, :], 0), 1)
    return at - begin


def body(
    tokens,
    lengths,
    cotangent,
    full_first_gain,
    full_project,
    full_merge,
    full_second_gain,
    full_widen,
    full_narrow,
    pool_weight,
    short_first_gain,
    short_project,
    short_merge,
    short_second_gain,
    short_widen,
    short_narrow,
    expand_weight,
):
    c = lax.axis_index("section")
    d = lax.axis_index("dp")
    k = d % 2
    rows = lengths.shape[0]
    length = tokens.shape[0] // rows
    groups = length // 3
    count = -(-length // QUARTER) * QUARTER
    short = -(-groups // 16) * 16

    here = k == c // 2
    who_k = jnp.stack([c, k]).astype(jnp.int32)
    order = Order()
    gain_rows = [
        g.reshape(1, QUARTER) for g in (full_first_gain, full_second_gain, short_first_gain, short_second_gain)
    ]
    attn_in = [((WIDTH, 3 * QUARTER), BF), ((WIDTH, QUARTER), BF), ((3 * QUARTER, WIDTH), BF)]
    pieces1, = order.call(
        pack_first_kernel, "pack_first", [((PAD + ATTN, QUARTER), BF)], None, full_project, full_merge, *gain_rows,
        scratch=attn_in + [((1, QUARTER), BF)] * 4, sems=6, space=pltpu.HBM, limit=PACK_LIMIT,
    )
    stage1 = [pieces1] + [swap(pieces1, r) for r in (1, 2, 3)]

    j = order.tie(c % 2)
    pairs = jnp.stack([lax.dynamic_index_in_dim(a.reshape(rows, length, WIDTH), j, 0, False) for a in (tokens, cotangent)])
    ends = lax.dynamic_index_in_dim(lengths, j, 0, False).astype(BF)
    ends = jnp.pad(ends, (0, WIDTH - ends.shape[0]))
    own_row = jnp.concatenate([pairs, jnp.broadcast_to(ends, (2, count - length, WIDTH))], 1)
    came_row = across(own_row)

    pieces2, pieces3, pieces4 = order.call(
        pack_rest_kernel, "pack_rest", [((n, QUARTER), BF) for n in (FFN, THIRD + ATTN + THIRD, FFN)],
        None, full_widen, full_narrow, pool_weight, short_project, short_merge, expand_weight, short_widen,
        short_narrow, scratch=attn_in, sems=26, space=pltpu.HBM, limit=PACK_LIMIT,
    )
    stage2, stage3, stage4 = (Stage(p) for p in (pieces2, pieces3, pieces4))
    stage2.start(order)
    stage3.start(order)

    counts = jnp.where(here, own_row[0, length, :SEGS], came_row[0, length, :SEGS]).astype(jnp.int32)
    odd = (d // 2) % 2 if lax.axis_size("dp") == 8 else jnp.zeros_like(d)
    who = jnp.concatenate([who_k, counts, jnp.stack([odd, odd]).astype(jnp.int32)])
    cos, sin = angles(places_of(counts, count, 3))
    short_cos, short_sin = angles(places_of(counts, short, 1))

    def block_outs(n):
        outs = [
            ((3 * HALF, WIDTH), BF, Far),
            ((HALF, WIDTH), BF, Far),
            ((n, WIDTH), BF, Far),
            ((n, HALF), BF, Far),
            ((n, HALF), BF, Far),
            ((n, HALF), BF, Far),
        ]
        return outs if n == count else [out[:2] for out in outs]

    def ffn_outs(n):
        outs = [
            ((n, WIDTH), F32, Far),
            ((n, WIDTH), BF, Far),
            ((WIDTH, HIDDEN), BF, Far),
            ((HIDDEN, WIDTH), BF, Far),
            ((n, HIDDEN), BF, Far),
            ((n, HIDDEN), BF, Far),
            ((n, WIDTH), BF),
        ]
        return outs if n == count else [out[:2] for out in outs]

    def back_outs(n):
        return [
            ((n, WIDTH), F32),
            ((n, WIDTH), BF),
            ((n, 3 * HALF), BF),
            ((n, WIDTH), BF),
            ((PAD, WIDTH), F32),
        ]

    def sent(part):
        return [((part, QUARTER), BF, Far)] * 4

    row, gains, project, merge, first, q, key, v, att, ctx, mix = order.call(
        full_attention_kernel, "full_attention",
        [((count, WIDTH), BF), ((PAD, WIDTH), F32)] + block_outs(count)
        + [((count // QUARTER, LOCAL * QUARTER, count), BF, Far), ((count, HALF), BF, Far), ((count, WIDTH), BF)],
        who, Raw(own_row), Raw(came_row), cos, sin, *[Free(a) for a in stage1], sems=2,
    )
    mix_came = across(mix)
    stage2.relay(order)
    order.wait(stage2.pieces[2])
    stage4.start(order)
    target, grouped = order.call(
        functools.partial(target_kernel, groups), "target",
        [((count, WIDTH), BF, Far), ((short, 3 * WIDTH), BF)], who, Raw(own_row), Raw(came_row), sems=2,
    )
    stage3.relay(order)
    middle, second, widen, narrow, hidden, slope, part = order.call(
        functools.partial(ffn_kernel, 1, stage2.places()), "full_ffn", ffn_outs(count),
        who, row, mix, mix_came, gains, *stage2.all(),
    )
    part_came = across(part)
    stage4.relay(order)
    raw3 = [Raw(a) for a in stage3.pieces]
    full, pool, joined, pooled = order.call(
        functools.partial(pool_kernel, groups), "pool",
        [((count, WIDTH), BF, Far), ((3 * HALF, WIDTH), BF, Far), ((short, 3 * HALF), BF), ((short, WIDTH), BF)],
        who, Far(middle), part, part_came, *raw3, scratch=[((4, THIRD, QUARTER), BF)], sems=4,
    )
    pooled_came = across(pooled)
    expand, d_half = order.call(
        expand_back_kernel, "expand_back", [((HALF, 3 * WIDTH), BF), ((short, HALF), BF)], who, grouped, *raw3,
        scratch=[((4, THIRD, QUARTER), BF)], sems=4,
    )
    d_came = across(d_half)
    s_in, s_project, s_merge, s_first, s_q, s_key, s_v, s_att, s_ctx, s_mix = order.call(
        short_attention_kernel, "short_attention",
        [((short, WIDTH), BF)] + block_outs(short)
        + [((1, LOCAL * short, short), BF), ((short, HALF), BF), ((short, WIDTH), BF)],
        who, pooled, pooled_came, short_cos, short_sin, gains, *raw3,
        scratch=[((4, ATTN, QUARTER), BF)], sems=4,
    )
    s_mix_came = across(s_mix)
    s_middle, s_hidden, s_delta, s_narrow, s_dsecond, *group = order.call(
        short_ffn_kernel, "short_ffn",
        [((short, WIDTH), F32), ((short, HIDDEN), BF), ((short, WIDTH), BF), ((HIDDEN, WIDTH), BF), ((short, WIDTH), BF)]
        + sent(PAD + FFN),
        who, s_in, s_mix, s_mix_came, gains, *stage4.all(), d_half, d_came,
        scratch=[
            ((short, WIDTH), BF), ((WIDTH, HIDDEN), BF), ((short, HIDDEN), BF), ((PAD, WIDTH), F32),
            ((WIDTH, HIDDEN), BF), ((HIDDEN, WIDTH), BF),
        ],
    )
    sum_a = Sum(order, group)
    sum_a.first()
    s_dsecond_came = across(s_dsecond)
    s_part, = order.call(short_ffn_rest_kernel, "short_ffn_rest", [((short, WIDTH), BF)], who, s_hidden, s_narrow)
    s_part_came = across(s_part)
    s_mid, s_dmix, s_dpacked, s_dfirst, s_gain1 = order.call(
        functools.partial(attention_back_kernel, 2, 3, short), "short_attention_back", back_outs(short),
        who, s_delta, s_dsecond, s_dsecond_came, s_middle, gains, s_in, s_merge, s_project, s_q, s_key, s_v, s_att,
        short_cos, short_sin, scratch=[((short, HALF), F32)] * 2,
    )
    s_dfirst_came = across(s_dfirst)
    s_half, grown = order.call(
        functools.partial(expand_kernel, groups), "expand", [((short, HALF), BF), ((count, WIDTH), BF, Far)],
        who, s_middle, s_part, s_part_came, expand, scratch=[((short, WIDTH), BF)],
    )
    grown_came = across(grown)
    d_in, d_low = order.call(
        functools.partial(pool_back_kernel, groups), "pool_back", [((short, WIDTH), BF), ((count, HALF), BF)],
        who, s_mid, s_dfirst, s_dfirst_came, gains, s_in, Far(pool),
    )
    d_low_came = across(d_low)
    order.wait(grown_came)
    sum_b = Sum(order, order.call(
        group_b_kernel, "group_b", sent(PAD + ATTN + 2 * THIRD),
        who, s_ctx, s_dmix, s_dpacked, s_first, s_gain1, joined, d_in, s_half, grouped,
        scratch=[((3 * HALF, WIDTH), BF), ((HALF, WIDTH), BF), ((3 * HALF, WIDTH), BF), ((HALF, 3 * WIDTH), BF)],
    ))
    sum_a.second()
    sum_b.first()
    delta, low, inner, dsecond, gain2 = order.call(
        full_ffn_back_kernel, "full_ffn_back",
        [((count, WIDTH), F32), ((count, WIDTH), BF), ((count, HIDDEN), BF), ((count, WIDTH), BF), ((PAD, WIDTH), F32)],
        who, Far(target), d_low, d_low_came, Far(middle), gains, Far(slope), Far(widen), Far(narrow),
    )
    dsecond_came = across(dsecond)
    sum_c = Sum(order, order.call(
        ffn_group_kernel, "group_c", sent(PAD + FFN), who, Far(hidden), low, Far(second), inner, gain2,
        scratch=[((WIDTH, HIDDEN), BF), ((HIDDEN, WIDTH), BF)],
    ))
    sum_a.third()
    sum_b.second()
    sum_a.fourth()
    sum_c.first()
    mid, dmix, dpacked, dfirst, gain1 = order.call(
        functools.partial(attention_back_kernel, 0, 1, QUARTER), "full_attention_back", back_outs(count),
        who, delta, dsecond, dsecond_came, Far(middle), gains, row, Far(merge), Far(project), Far(q), Far(key), Far(v),
        Far(att), cos, sin, scratch=[((count, HALF), F32)] * 2,
    )
    dfirst_came = across(dfirst)
    sum_a.fifth()
    sum_b.third()
    sum_c.second()
    sum_d = Sum(order, order.call(
        attn_group_kernel, "group_d", sent(PAD + ATTN), who, Far(ctx), dmix, dpacked, Far(first), gain1,
        scratch=[((3 * HALF, WIDTH), BF), ((HALF, WIDTH), BF)],
    ))
    sum_b.fourth()
    sum_d.first()
    sent_rows = order.call(
        outputs_kernel, "outputs", [((length, QUARTER), BF)] * 4,
        who, Far(full), Far(grown), grown_came, mid, dfirst, dfirst_came, gains, row, scratch=[((count, WIDTH), BF)],
    )


    gain_out = ((1, QUARTER), F32)
    ffn_out = [((WIDTH, WIDTH), F32), ((4 * WIDTH, QUARTER), F32)]
    attn_out = [((WIDTH, 3 * QUARTER), F32), ((WIDTH, QUARTER), F32)]
    turned = [((3 * QUARTER, WIDTH), F32)]

    def spread(kernel, name, outs, total, **options):
        outs = [(*out, Far) for out in outs]
        how = spread_either if total.short else spread_whole
        return order.call(functools.partial(how, kernel), name, outs, who, *total.all(), **options)

    sum_d.second()
    sum_c.third()
    sum_d.third()
    sum_a.sixth()
    sum_c.fourth()
    sum_b.fifth()
    g_s2, g_s_widen, g_s_narrow = spread(spread_ffn_kernel, "spread_a", [gain_out] + ffn_out, sum_a)
    sum_d.fourth()
    sum_c.fifth()
    delivery = Delivery(order, sent_rows, c, k)
    sum_d.fifth()
    sum_c.sixth()
    sum_d.sixth()
    sum_b.sixth()
    g_s1, g_s_project, g_s_merge, g_pool, g_expand = spread(
        spread_b_kernel, "spread_b",
        [gain_out] + attn_out + [((3 * WIDTH, QUARTER), F32), ((WIDTH, 3 * QUARTER), F32)], sum_b, scratch=turned,
    )
    delivery.turn()
    g_f2, g_widen, g_narrow = spread(spread_ffn_kernel, "spread_c", [gain_out] + ffn_out, sum_c)
    g_f1, g_project, g_merge = spread(spread_attn_kernel, "spread_d", [gain_out] + attn_out, sum_d, scratch=turned)
    mixed_out, token_gradient = delivery.finish()

    return (
        mixed_out,
        token_gradient,
        g_f1.reshape(-1),
        g_project,
        g_merge,
        g_f2.reshape(-1),
        g_widen,
        g_narrow,
        g_pool,
        g_s1.reshape(-1),
        g_s_project,
        g_s_merge,
        g_s2.reshape(-1),
        g_s_widen,
        g_s_narrow,
        g_expand,
    )


def solution(mesh):
    in_specs = (
        P("dp", None),
        P("dp", None),
        P("dp", None),
        P("section"),
        P(None, "section"),
        P(None, "section"),
        P("section"),
        P(None, "section"),
        P(None, "section"),
        P(None, "section"),
        P("section"),
        P(None, "section"),
        P(None, "section"),
        P("section"),
        P(None, "section"),
        P(None, "section"),
        P(None, "section"),
    )
    out_specs = (
        P("dp", "section"),
        P("dp", "section"),
        P("section"),
        P(None, "section"),
        P(None, "section"),
        P("section"),
        P(None, "section"),
        P(None, "section"),
        P(None, "section"),
        P("section"),
        P(None, "section"),
        P(None, "section"),
        P("section"),
        P(None, "section"),
        P(None, "section"),
        P(None, "section"),
    )
    return jax.shard_map(body, mesh=mesh, in_specs=in_specs, out_specs=out_specs, check_vma=False)
```
